32 devices in a mesh: dp: 16 (over z, y, x), fsdp: 2 (over core).
Axes of the slice: x: 2, y: 2, z: 4, core: 2. Of those that a mesh axis runs over, the one named last changes fastest.
Arguments:
- clean_images: float32 [128, 3, 1024], P(('dp', 'fsdp')), may hold values from -1 to 1
- noise_field: float32 [128, 3, 1024], P(('dp', 'fsdp')), may hold values from -6 to 6
- step_counts: int32 [128], P(('dp', 'fsdp')), may hold values from 2 to 4, as said below
- time_index: int32 [128], P(('dp', 'fsdp')), may hold values from 0 to 3
- teacher_size: int32 [128], P(('dp', 'fsdp')), may hold values from 1 to 2
- image_counts: int32 [32], P(('dp', 'fsdp')), may hold values from 2 to 4, as said below
- adam_step: int32 [1], replicated, may hold values from 2 to 20
- stem_master: float32 [327680], P(('dp', 'fsdp'))
- stem_first: float32 [327680], P(('dp', 'fsdp'))
- stem_second: float32 [327680], P(('dp', 'fsdp'))
- res_master: float32 [1409024], P(('dp', 'fsdp'))
- res_first: float32 [1409024], P(('dp', 'fsdp'))
- res_second: float32 [1409024], P(('dp', 'fsdp'))
- attn_master: float32 [294912], P(('dp', 'fsdp'))
- attn_first: float32 [294912], P(('dp', 'fsdp'))
- attn_second: float32 [294912], P(('dp', 'fsdp'))
- head_master: float32 [327680], P(('dp', 'fsdp'))
- head_first: float32 [327680], P(('dp', 'fsdp'))
- head_second: float32 [327680], P(('dp', 'fsdp'))
Outputs:
- loss_value: float32 [], replicated
- grad_norm: float32 [], replicated
- stem_master_out: float32 [327680], P(('dp', 'fsdp'))
- stem_first_out: float32 [327680], P(('dp', 'fsdp'))
- stem_second_out: float32 [327680], P(('dp', 'fsdp'))
- stem_copy_out: bfloat16 [327680], P(('dp', 'fsdp'))
- res_master_out: float32 [1409024], P(('dp', 'fsdp'))
- res_first_out: float32 [1409024], P(('dp', 'fsdp'))
- res_second_out: float32 [1409024], P(('dp', 'fsdp'))
- res_copy_out: bfloat16 [1409024], P(('dp', 'fsdp'))
- attn_master_out: float32 [294912], P(('dp', 'fsdp'))
- attn_first_out: float32 [294912], P(('dp', 'fsdp'))
- attn_second_out: float32 [294912], P(('dp', 'fsdp'))
- attn_copy_out: bfloat16 [294912], P(('dp', 'fsdp'))
- head_master_out: float32 [327680], P(('dp', 'fsdp'))
- head_first_out: float32 [327680], P(('dp', 'fsdp'))
- head_second_out: float32 [327680], P(('dp', 'fsdp'))
- head_copy_out: bfloat16 [327680], P(('dp', 'fsdp'))
The draws below stay inside these ranges and needn't reach their ends.
Inputs may be any that keep to these rules, and one draw needn't show every extreme that they name: `step_counts`: each step count is 2 or 4. Device d's live images are its first image_counts[d] slots; some device has 4 live images and some has 2.
All inputs are finite; a program needn't handle non-finite values.
Results may differ from the reference program's by a relative error of at most 0.0091.
Values may be sent and summed in bfloat16 or wider, within the bound.
No kernel may reach another device: no remote copies, remote signals or barrier semaphores. Data moves between devices by JAX's collectives and lax.ppermute only.
A program may use at most 128 MiB of HBM per device.

```python
import math
import jax
import jax.numpy as jnp
from jax import lax

C1 = 128
CHANNELS_LOWER = 256
GROUPS = 32
TDIM = 128
TEMB = 512
CIN = 3
SIDE = 32
IMG_DEV = 4
HW = 1024
IMAGES = 128


clip_limit = 0.05


beta_one = 0.9


beta_two = 0.999


def block_layouts_drawn():
    return ((('kern_in', (9, CIN, C1)), ('bias_in', (C1,)), ('kern_down', (9, C1, CHANNELS_LOWER)), ('bias_down', (CHANNELS_LOWER,))), (('dense_one', (TDIM, TEMB)), ('bias_one', (TEMB,)), ('dense_two', (TEMB, CHANNELS_LOWER)), ('bias_two', (CHANNELS_LOWER,)), ('gain_first', (CHANNELS_LOWER,)), ('shift_first', (CHANNELS_LOWER,)), ('kern_first', (9, CHANNELS_LOWER, CHANNELS_LOWER)), ('bias_first', (CHANNELS_LOWER,)), ('gain_second', (CHANNELS_LOWER,)), ('shift_second', (CHANNELS_LOWER,)), ('kern_second', (9, CHANNELS_LOWER, CHANNELS_LOWER)), ('bias_second', (CHANNELS_LOWER,))), (('gain_attn', (CHANNELS_LOWER,)), ('shift_attn', (CHANNELS_LOWER,)), ('kern_qkv', (CHANNELS_LOWER, 3 * CHANNELS_LOWER)), ('kern_proj', (CHANNELS_LOWER, CHANNELS_LOWER)), ('bias_proj', (CHANNELS_LOWER,))), (('kern_up', (9, CHANNELS_LOWER, C1)), ('bias_up', (C1,)), ('gain_out', (C1,)), ('shift_out', (C1,)), ('kern_out', (9, C1, CIN)), ('bias_out', (CIN,))))


def padded_length(layout):
    raw_length = sum((math.prod(item_pair[1]) for item_pair in layout))
    return (raw_length + 32767) // 32768 * 32768


def grad_scale():
    whole = sum((padded_length(layout) for layout in block_layouts_drawn()))
    return clip_limit / math.sqrt(whole)


def block_key(key, block_idx):
    return jax.random.fold_in(key, 101 + 17 * block_idx)


def draw_master(key, block_idx):
    key = block_key(key, block_idx)
    layout = block_layouts_drawn()[block_idx]
    pieces = []
    for number, (label_name, dim_shape) in enumerate(layout):
        sub_key = jax.random.fold_in(key, number)
        extent = math.prod(dim_shape)
        if label_name[:4] == 'gain':
            piece = 1.0 + 0.3 * jax.random.uniform(sub_key, (extent,), jnp.float32, -1.0, 1.0)
        elif label_name[:5] == 'shift' or label_name[:4] == 'bias':
            piece = 0.3 * jax.random.normal(sub_key, (extent,), jnp.float32)
        else:
            fan_in = extent // dim_shape[-1]
            if label_name == 'kern_proj':
                fan_in = fan_in // 4
            piece = jax.random.normal(sub_key, (extent,), jnp.float32) * fan_in ** (-0.5)
        pieces.append(piece)
    column = jnp.concatenate(pieces)
    length = padded_length(layout)
    filler = 0.01 * jax.random.normal(jax.random.fold_in(key, 999), (length - column.shape[0],), jnp.float32)
    return jnp.concatenate([column, filler])


def draw_first(key, block_idx):
    key = block_key(key, block_idx)
    length = padded_length(block_layouts_drawn()[block_idx])
    signs = jnp.where(jax.random.bernoulli(jax.random.fold_in(key, 1), 0.5, (length,)), 1.0, -1.0)
    magnitude = jnp.exp(jax.random.uniform(jax.random.fold_in(key, 2), (length,), jnp.float32, math.log(0.5), math.log(2.0)))
    return signs * magnitude * ((1.0 - beta_one) / beta_one) * grad_scale()


def draw_second(key, block_idx):
    key = block_key(key, block_idx)
    length = padded_length(block_layouts_drawn()[block_idx])
    spread = jax.random.uniform(jax.random.fold_in(key, 3), (length,), jnp.float32, 1.0, 4.0)
    return spread * ((1.0 - beta_two) / beta_two) * grad_scale() ** 2


def draw_stem_master(key, part):
    return draw_master(key, 0)


def draw_res_master(key, part):
    return draw_master(key, 1)


def draw_attn_master(key, part):
    return draw_master(key, 2)


def draw_head_master(key, part):
    return draw_master(key, 3)


def draw_stem_first(key, part):
    return draw_first(key, 0)


def draw_res_first(key, part):
    return draw_first(key, 1)


def draw_attn_first(key, part):
    return draw_first(key, 2)


def draw_head_first(key, part):
    return draw_first(key, 3)


def draw_stem_second(key, part):
    return draw_second(key, 0)


def draw_res_second(key, part):
    return draw_second(key, 1)


def draw_attn_second(key, part):
    return draw_second(key, 2)


def draw_head_second(key, part):
    return draw_second(key, 3)


def draw_step_counts(key, part):
    return 2 * jax.random.randint(jax.random.fold_in(key, 5), (IMAGES,), 1, 3)


def draw_image_counts(key, part):
    devices = IMAGES // IMG_DEV
    counts = jax.random.randint(jax.random.fold_in(key, 6), (devices,), IMG_DEV // 2, IMG_DEV + 1)
    low_at = jax.random.randint(jax.random.fold_in(key, 7), (), 0, devices)
    high_at = (low_at + 1 + jax.random.randint(jax.random.fold_in(key, 8), (), 0, devices - 1)) % devices
    return counts.at[low_at].set(IMG_DEV // 2).at[high_at].set(IMG_DEV)


def touch_ends(entries, key, low, high):
    longest = entries.shape.index(max(entries.shape))
    spots = []
    for shift in (0, 1):
        where = [jax.random.randint(jax.random.fold_in(key, axis), (), 0, length) for axis, length in enumerate(entries.shape)]
        where[longest] = (where[longest] + shift) % entries.shape[longest]
        spots.append(tuple(where))
    return entries.at[spots[0]].set(low).at[spots[1]].set(high)


def block_levels(key, shape, cuts, low, top_value):
    loudness, own = 1.0, jax.random.fold_in(key, 6)
    for axis_at, blocks in cuts:
        heights = jnp.exp(jax.random.uniform(jax.random.fold_in(own, axis_at), (blocks,), jnp.float32, low / len(cuts), top_value / len(cuts)))
        loudness = loudness * jnp.repeat(heights, shape[axis_at] // blocks).reshape([-1 if axis == axis_at else 1 for axis in range(len(shape))])
    return loudness


def centred(own_key, shape, width, reach, cuts=(), kind=jnp.bfloat16):
    array = jax.random.normal(own_key, shape, jnp.float32) * width
    if len(cuts) > 0:
        array = block_levels(own_key, shape, cuts, -0.22, 0.18) * array
    return jnp.clip(array, min=-reach, max=reach).astype(kind)


def setup_inputs(seed: int = 0) -> dict:
    keys = jax.random.split(jax.random.key(seed), 20)
    return {
        "clean_images": jnp.clip(jax.random.uniform(keys[0], (IMAGES, CIN, HW), jnp.float32, -1.0, 1.0) * block_levels(keys[0], (IMAGES, CIN, HW), ((0, 32),), -0.4, 0.0), -1.0, 1.0),
        "noise_field": centred(keys[1], (IMAGES, CIN, HW), 1.0, 6.0, ((0, 32),), jnp.float32),
        "step_counts": draw_step_counts(jax.random.fold_in(keys[19], 71), 0),
        "time_index": touch_ends(jax.random.randint(keys[3], (IMAGES,), 0, 4), jax.random.fold_in(keys[3], 1), 0, 3).astype(jnp.int32),
        "teacher_size": touch_ends(jax.random.randint(keys[4], (IMAGES,), 1, 3), jax.random.fold_in(keys[4], 1), 1, 2).astype(jnp.int32),
        "image_counts": draw_image_counts(jax.random.fold_in(keys[19], 71), 0),
        "adam_step": jax.random.randint(keys[6], (1,), 2, 21).astype(jnp.int32),
        "stem_master": draw_stem_master(jax.random.fold_in(keys[19], 71), 0),
        "stem_first": draw_stem_first(jax.random.fold_in(keys[19], 71), 0),
        "stem_second": draw_stem_second(jax.random.fold_in(keys[19], 71), 0),
        "res_master": draw_res_master(jax.random.fold_in(keys[19], 71), 0),
        "res_first": draw_res_first(jax.random.fold_in(keys[19], 71), 0),
        "res_second": draw_res_second(jax.random.fold_in(keys[19], 71), 0),
        "attn_master": draw_attn_master(jax.random.fold_in(keys[19], 71), 0),
        "attn_first": draw_attn_first(jax.random.fold_in(keys[19], 71), 0),
        "attn_second": draw_attn_second(jax.random.fold_in(keys[19], 71), 0),
        "head_master": draw_head_master(jax.random.fold_in(keys[19], 71), 0),
        "head_first": draw_head_first(jax.random.fold_in(keys[19], 71), 0),
        "head_second": draw_head_second(jax.random.fold_in(keys[19], 71), 0),
    }


clip_limit = 0.05
learn_rate = 0.05
beta_one = 0.9
beta_two = 0.999
adam_eps = 1e-08
decay_rate = 0.01
norm_eps = 1e-05
highest_precision = lax.Precision.HIGHEST

@jax.custom_vjp
def lowered_input(v):
    return lax.optimization_barrier(v.astype(jnp.bfloat16)).astype(jnp.float32)

@jax.custom_vjp
def lowered_backward(v):
    return v

def low_keep(v):
    return (lowered_input(v), None)

def low_pass(kept, grad):
    return (grad,)

def back_keep(v):
    return (v, None)

def back_low(kept, grad):
    return (lowered_input(grad),)
lowered_input.defvjp(low_keep, low_pass)
lowered_backward.defvjp(back_keep, back_low)

def block_layouts():
    return ((('kern_in', (9, CIN, C1)), ('bias_in', (C1,)), ('kern_down', (9, C1, CHANNELS_LOWER)), ('bias_down', (CHANNELS_LOWER,))), (('dense_one', (TDIM, TEMB)), ('bias_one', (TEMB,)), ('dense_two', (TEMB, CHANNELS_LOWER)), ('bias_two', (CHANNELS_LOWER,)), ('gain_first', (CHANNELS_LOWER,)), ('shift_first', (CHANNELS_LOWER,)), ('kern_first', (9, CHANNELS_LOWER, CHANNELS_LOWER)), ('bias_first', (CHANNELS_LOWER,)), ('gain_second', (CHANNELS_LOWER,)), ('shift_second', (CHANNELS_LOWER,)), ('kern_second', (9, CHANNELS_LOWER, CHANNELS_LOWER)), ('bias_second', (CHANNELS_LOWER,))), (('gain_attn', (CHANNELS_LOWER,)), ('shift_attn', (CHANNELS_LOWER,)), ('kern_qkv', (CHANNELS_LOWER, 3 * CHANNELS_LOWER)), ('kern_proj', (CHANNELS_LOWER, CHANNELS_LOWER)), ('bias_proj', (CHANNELS_LOWER,))), (('kern_up', (9, CHANNELS_LOWER, C1)), ('bias_up', (C1,)), ('gain_out', (C1,)), ('shift_out', (C1,)), ('kern_out', (9, C1, CIN)), ('bias_out', (CIN,))))

def unpack(vector, layout):
    pieces = {}
    offset = 0
    for label_name, dim_shape in layout:
        extent = math.prod(dim_shape)
        pieces[label_name] = vector[offset:offset + extent].reshape(dim_shape)
        offset += extent
    return pieces

def conv_same(source, kernel, stride):
    tap_table = kernel.reshape(3, 3, kernel.shape[1], kernel.shape[2])
    return lax.conv_general_dilated(source, tap_table, (stride, stride), ((1, 1), (1, 1)), dimension_numbers=('NHWC', 'HWIO', 'NHWC'), precision=highest_precision)

def group_norm(values, gain_vec, shift_vec, active):
    img_count, height, width_px, channels = values.shape
    grouped = values.reshape(img_count, height, width_px, GROUPS, channels // GROUPS)
    center = lax.optimization_barrier(jnp.mean(grouped, axis=(1, 2, 4), keepdims=True))
    spread = lax.optimization_barrier(jnp.mean(jnp.square(grouped - center), axis=(1, 2, 4), keepdims=True))
    normalized_input = ((grouped - center) * lax.rsqrt(spread + norm_eps)).reshape(values.shape) * gain_vec + shift_vec
    if active:
        return jax.nn.silu(normalized_input)
    return normalized_input

def sinusoid(time_values):
    half_dim = TDIM // 2
    frequency = jnp.exp(-math.log(10000.0) * jnp.arange(half_dim, dtype=jnp.float32) / half_dim)
    angles = 1000.0 * time_values[:, None] * frequency[None, :]
    return jnp.concatenate([jnp.sin(angles), jnp.cos(angles)], axis=1)

def plan(step_counts, time_index, teacher_size):
    position = time_index % step_counts
    time_values = (2 * position + teacher_size).astype(jnp.float32) / (2 * step_counts).astype(jnp.float32)
    alpha_t = jnp.cos(0.5 * math.pi * time_values)
    sigma_t = jnp.sin(0.5 * math.pi * time_values)
    weight = jnp.maximum(alpha_t * alpha_t / (sigma_t * sigma_t), 1.0)
    return (time_values, alpha_t, sigma_t, weight)

def network(masters, noisy_in, embedded):
    stem_par, res_par, attention_params, head_par = [unpack(lowered_input(flat_block), layout) for flat_block, layout in zip(masters, block_layouts())]
    img_count = noisy_in.shape[0]
    top_feat = lowered_backward(conv_same(lowered_input(noisy_in), stem_par['kern_in'], 1) + stem_par['bias_in'])
    down_feat = lowered_backward(conv_same(lowered_input(top_feat), stem_par['kern_down'], 2) + stem_par['bias_down'])
    hidden_t = jax.nn.silu(jnp.dot(embedded, res_par['dense_one'], precision=highest_precision) + res_par['bias_one'])
    time_proj = jnp.dot(hidden_t, res_par['dense_two'], precision=highest_precision) + res_par['bias_two']
    act_one = lowered_input(group_norm(down_feat, res_par['gain_first'], res_par['shift_first'], True))
    inner = lowered_backward(conv_same(act_one, res_par['kern_first'], 1) + res_par['bias_first'] + time_proj[:, None, None, :])
    act_two = lowered_input(group_norm(inner, res_par['gain_second'], res_par['shift_second'], True))
    res_feat = down_feat + lowered_backward(conv_same(act_two, res_par['kern_second'], 1) + res_par['bias_second'])
    normalized_input = lowered_input(group_norm(res_feat, attention_params['gain_attn'], attention_params['shift_attn'], False)).reshape(img_count, -1, CHANNELS_LOWER)
    query_key_value = lowered_input(lowered_backward(jnp.einsum('hop,pk->hok', normalized_input, attention_params['kern_qkv'], precision=highest_precision)))
    query_matrix, key_matrix, value_matrix = (query_key_value[..., :CHANNELS_LOWER], query_key_value[..., CHANNELS_LOWER:2 * CHANNELS_LOWER], query_key_value[..., 2 * CHANNELS_LOWER:])
    attention_logits = lowered_backward(jnp.einsum('mnw,miw->mni', query_matrix, key_matrix, precision=highest_precision) * CHANNELS_LOWER ** (-0.5))
    probability_rows = jax.nn.softmax(attention_logits, axis=-1)
    blended_values = lowered_input(lowered_backward(jnp.einsum('ahs,ase->ahe', lowered_input(probability_rows), value_matrix, precision=highest_precision)))
    attention_output = lowered_backward(jnp.einsum('hop,pk->hok', blended_values, attention_params['kern_proj'], precision=highest_precision)) + attention_params['bias_proj']
    attn_feat = res_feat + attention_output.reshape(res_feat.shape)
    upsampled = jnp.repeat(jnp.repeat(lowered_input(attn_feat), 2, axis=1), 2, axis=2)
    merged = lowered_backward(conv_same(upsampled, head_par['kern_up'], 1) + head_par['bias_up']) + top_feat
    act_out = lowered_input(group_norm(merged, head_par['gain_out'], head_par['shift_out'], True))
    return lowered_backward(conv_same(act_out, head_par['kern_out'], 1) + head_par['bias_out'])

def adam_update(master, first, second, gradient, step_value):
    first_new = beta_one * first + (1.0 - beta_one) * gradient
    second_new = beta_two * second + (1.0 - beta_two) * gradient * gradient
    fix_one = 1.0 - jnp.power(jnp.float32(beta_one), step_value)
    fix_two = 1.0 - jnp.power(jnp.float32(beta_two), step_value)
    master_new = master - learn_rate * (first_new / fix_one / (jnp.sqrt(second_new / fix_two) + adam_eps) + decay_rate * master)
    return (master_new, first_new, second_new, master_new.astype(jnp.bfloat16))

def reference(clean_images, noise_field, step_counts, time_index, teacher_size, image_counts, adam_step, stem_master, stem_first, stem_second, res_master, res_first, res_second, attn_master, attn_first, attn_second, head_master, head_first, head_second):
    time_values, alpha_t, sigma_t, weight = plan(step_counts, time_index, teacher_size)
    slot_index = jnp.arange(IMAGES, dtype=jnp.int32) % IMG_DEV
    owner_count = jnp.repeat(image_counts, IMG_DEV)
    live_mask = (slot_index < owner_count).astype(jnp.float32)
    total_live = jnp.sum(image_counts).astype(jnp.float32)
    images = clean_images.transpose(0, 2, 1).reshape(IMAGES, SIDE, SIDE, CIN)
    noises = noise_field.transpose(0, 2, 1).reshape(IMAGES, SIDE, SIDE, CIN)
    noisy_in = alpha_t[:, None, None, None] * images + sigma_t[:, None, None, None] * noises
    factor = live_mask * weight / total_live
    embedded = sinusoid(time_values)
    groups = IMAGES // IMG_DEV
    masters = (stem_master, res_master, attn_master, head_master)

    def group_step(carried, inputs):
        noisy_g, images_g, factor_g, embed_g = inputs

        def loss_fn(parameter_tree):
            predict = network(parameter_tree, noisy_g, embed_g)
            return jnp.sum(factor_g * lax.optimization_barrier(jnp.mean(jnp.square(predict - images_g), axis=(1, 2, 3))))
        loss_part, pullback = jax.vjp(loss_fn, masters)
        gradients, = pullback(jnp.ones((), jnp.float32))
        summed = tuple((older + fresh for older, fresh in zip(carried[1], gradients)))
        return ((carried[0] + loss_part, summed), None)
    inputs = (noisy_in.reshape(groups, IMG_DEV, SIDE, SIDE, CIN), images.reshape(groups, IMG_DEV, SIDE, SIDE, CIN), factor.reshape(groups, IMG_DEV), embedded.reshape(groups, IMG_DEV, TDIM))
    start = (jnp.zeros((), jnp.float32), tuple((jnp.zeros_like(master) for master in masters)))
    (loss_value, gradients), unused = lax.scan(group_step, start, inputs)
    grad_norm = jnp.sqrt(sum((jnp.sum(jnp.square(gradient)) for gradient in gradients)))
    clip_scale = clip_limit / jnp.maximum(grad_norm, clip_limit)
    step_value = adam_step[0].astype(jnp.float32)
    firsts = (stem_first, res_first, attn_first, head_first)
    seconds = (stem_second, res_second, attn_second, head_second)
    results = [loss_value, grad_norm]
    for block_idx in range(4):
        results.extend(adam_update(masters[block_idx], firsts[block_idx], seconds[block_idx], gradients[block_idx] * clip_scale, step_value))
    return tuple(results)
```

```python
from functools import partial
import math

import jax
import jax.numpy as jnp
from jax import lax
from jax.experimental import pallas as pl
from jax.experimental.pallas import tpu as pltpu
from jax.sharding import PartitionSpec as P

C1 = 128
C2 = 256
GROUPS = 32
TDIM = 128
TEMB = 512
CIN = 3
SIDE = 32
LANES = 128
IMGS = 4
LOW = 256
ROWS = IMGS * LOW
PAD = 16
PADDED = LOW + 2 * PAD

clip_limit = 0.05
learn_rate = 0.05
beta_one = 0.9
beta_two = 0.999
adam_eps = 1e-08
decay_rate = 0.01
norm_eps = 1e-05

f32 = jnp.float32
bf16 = jnp.bfloat16
highest = lax.Precision.HIGHEST

STEM_ROWS, RES_ROWS, ATTN_ROWS, HEAD_ROWS = 2560, 11008, 2304, 2560

STEM_AT = dict(kern_in=0, bias_in=27, kern_down=28, bias_down=2332, end=2334)
RES_AT = dict(
    dense_one=0, bias_one=512, dense_two=516, bias_two=1540, gain_first=1542, shift_first=1544,
    kern_first=1546, bias_first=6154, gain_second=6156, shift_second=6158, kern_second=6160,
    bias_second=10768, end=10770,
)
ATTN_AT = dict(gain_attn=0, shift_attn=2, kern_qkv=4, kern_proj=1540, bias_proj=2052, end=2054)
HEAD_AT = dict(kern_up=0, bias_up=2304, gain_out=2305, shift_out=2306, kern_out=2307, bias_out=2334, end=2335)


def mm(a, b):
    return jnp.dot(a, b, preferred_element_type=f32)


def mm_nt(a, b):
    return lax.dot_general(a, b, (((1,), (1,)), ((), ())), preferred_element_type=f32)


def mm_tn(a, b):
    return lax.dot_general(a, b, (((0,), (0,)), ((), ())), preferred_element_type=f32)


def parts_of(values):
    high = values.astype(bf16)
    rest = values - high.astype(f32)
    middle = rest.astype(bf16)
    return high, middle, (rest - middle.astype(f32)).astype(bf16)


def mm_exact(values, matrix):
    return sum(mm(piece, matrix) for piece in parts_of(values))


def same_group(channels):
    size = channels // GROUPS
    down_at = lax.broadcasted_iota(jnp.int32, (channels, channels), 0) // size
    across = lax.broadcasted_iota(jnp.int32, (channels, channels), 1) // size
    return (down_at == across).astype(f32).astype(bf16)


def row_shift(values, step):
    count = values.shape[0]
    moved = pltpu.roll(values, (-step) % count, 0)
    column = lax.broadcasted_iota(jnp.int32, values.shape, 0) & 15
    return jnp.where(column == (0 if step < 0 else 15), 0.0, moved)


def chunks(total, size, body):
    def step(number, carry):
        body(pl.multiple_of(number * size, size))
        return carry

    lax.fori_loop(0, total // size, step, 0)


def widen(pieces, places, me, stage):
    for ref, (masks, lo, hi, per_shard, begin) in zip(pieces, places):
        for number, mask in enumerate(masks):
            owner = me ^ mask
            at = pl.multiple_of(owner * per_shard + begin, 8)
            stage[pl.ds(at, hi - lo), :] = ref[number, lo:hi, :].astype(f32)


def narrow_out(stage, me, outs, places):
    for ref, (masks, lo, hi, per_shard, begin) in zip(outs, places):
        for number, mask in enumerate(masks):
            owner = me ^ mask
            at = pl.multiple_of(owner * per_shard + begin, 8)
            ref[number, lo:hi, :] = stage[pl.ds(at, hi - lo), :].astype(ref.dtype)


def matrix_from(stage, base, out, depth, width):
    lanes = width // LANES

    def copy(at):
        for lane in range(lanes):
            out[pl.ds(at, 128), lane * LANES : (lane + 1) * LANES] = stage[
                pl.ds(base + lanes * at + lane, 128, lanes), :
            ].astype(bf16)

    chunks(depth, 128, copy)


def matrix_to(out, base, value):
    depth, width = value.shape
    lanes = width // LANES
    for lane in range(lanes):
        out[pl.ds(base + lane, depth, lanes), :] = value[:, lane * LANES : (lane + 1) * LANES]


def vector_at(stage, base, width):
    return jnp.concatenate([stage[base + lane : base + lane + 1, :] for lane in range(width // LANES)], axis=1)


def vector_to(out, base, value):
    for lane in range(value.shape[1] // LANES):
        out[base + lane : base + lane + 1, :] = value[:, lane * LANES : (lane + 1) * LANES]


def fold(values):
    return jnp.sum(values.reshape(values.shape[0] // 8, 8, values.shape[1]), axis=0)


def image_sums(load, phases, width):
    sums = []
    for image in range(IMGS):
        def step(number, carry):
            row = pl.multiple_of(image * LOW + number * 64, 64)
            for phase in range(phases):
                carry = tuple(c + fold(v) for c, v in zip(carry, load(phase, image, row)))
            return carry

        first = load(0, image, image * LOW)
        carry = lax.fori_loop(0, 4, step, tuple(jnp.zeros((8, width), f32) for _ in first))
        sums.append([jnp.sum(c, axis=0, keepdims=True) for c in carry])
    return [jnp.concatenate(list(group), axis=0) for group in zip(*sums)]


def norm_stats(load, phases, width, ones):
    count = LOW * phases * (width // GROUPS)
    (total,) = image_sums(lambda phase, image, row: (load(phase, row),), phases, width)
    center = mm_exact(total, ones) * (1.0 / count)

    def squares(phase, image, row):
        away = load(phase, row) - center[image : image + 1, :]
        return (away * away,)

    (total,) = image_sums(squares, phases, width)
    spread = mm_exact(total, ones) * (1.0 / count)
    return center, lax.rsqrt(spread + norm_eps)


def norm_back_stats(load, phases, width, gain, ones):
    count = LOW * phases * (width // GROUPS)
    shift_sum, gain_sum = image_sums(load, phases, width)
    means = mm_exact(jnp.concatenate([shift_sum * gain, gain_sum * gain], axis=0), ones) * (1.0 / count)
    return (
        jnp.sum(gain_sum, axis=0, keepdims=True),
        jnp.sum(shift_sum, axis=0, keepdims=True),
        means[:IMGS],
        means[IMGS:],
    )


def logistic(values):
    return 1.0 / (1.0 + jnp.exp(-values))


def each_chunk(body, phases=1, size=64):
    for image in range(IMGS):
        def step(number, carry):
            inside = pl.multiple_of(number * size, size)
            for phase in range(phases):
                body(phase, image, inside, image * LOW + inside)
            return carry

        lax.fori_loop(0, LOW // size, step, 0)


def clear_edges(wide):
    for image in range(IMGS):
        wide[image, 0:PAD, :] = jnp.zeros((PAD, wide.shape[2]), wide.dtype)
        wide[image, PAD + LOW : PADDED, :] = jnp.zeros((PAD, wide.shape[2]), wide.dtype)


def put_shifted(wide, image, inside, value):
    width = value.shape[1]
    at = pl.ds(PAD + inside, value.shape[0])
    wide[image, at, 0:width] = row_shift(value, -1).astype(bf16)
    wide[image, at, width : 2 * width] = value.astype(bf16)
    wide[image, at, 2 * width : 3 * width] = row_shift(value, 1).astype(bf16)


def wide_rows(wide, row_off, lo, hi):
    begin = PAD + 16 * row_off
    return wide[:, begin : begin + LOW, lo:hi].reshape(ROWS, hi - lo)


def conv_low(wide, kern):
    width = wide.shape[2]
    total = None
    for tap in range(3):
        part = mm(wide_rows(wide, tap - 1, 0, width), kern[tap * width : (tap + 1) * width, :])
        total = part if total is None else total + part
    return total


def conv_low_back(wide, kern):
    width = wide.shape[2] // 3
    total = None
    for row_tap in range(3):
        for col_tap in range(3):
            tap = row_tap * 3 + col_tap
            part = mm_nt(
                wide_rows(wide, 1 - row_tap, (2 - col_tap) * width, (3 - col_tap) * width),
                kern[tap * C2 : (tap + 1) * C2, :],
            )
            total = part if total is None else total + part
    return total


def conv_low_grad(source, wide, out, base):
    for row_tap in range(3):
        product = mm_tn(source[...], wide_rows(wide, 1 - row_tap, 0, 3 * C2))
        for col_tap in range(3):
            tap = row_tap * 3 + col_tap
            matrix_to(out, base + tap * 2 * C2, product[:, (2 - col_tap) * C2 : (3 - col_tap) * C2])


def lane_masks(width):
    place = lax.broadcasted_iota(jnp.int32, (8, width), 1)
    row, column = (place >> 4) & 15, place & 15

    def valid(row_off, col_off):
        keep = None
        for at, off in ((row, row_off), (column, col_off)):
            if off:
                inside = at != (0 if off < 0 else 15)
                keep = inside if keep is None else keep & inside
        return keep

    return {(r, c): valid(r, c) for r in (-1, 0, 1) for c in (-1, 0, 1)}


def lane_shift(values, row_off, col_off, masks):
    step = 16 * row_off + col_off
    if step == 0:
        return values
    moved = pltpu.roll(values, (-step) % values.shape[1], 1)
    return jnp.where(masks[(row_off, col_off)], moved, 0.0)


def tap_source(phase, tap_off):
    row, col = phase // 2 + tap_off[0], phase % 2 + tap_off[1]
    return (row % 2) * 2 + col % 2, row // 2, col // 2


TAPS = tuple((row - 1, col - 1) for row in range(3) for col in range(3))


def taps_on_lanes(source, out, masks, sign):
    for phase in range(4):
        for tap, off in enumerate(TAPS):
            other, row_off, col_off = tap_source(phase, (sign * off[0], sign * off[1]))
            out[8 * tap : 8 * tap + 8, phase * ROWS : (phase + 1) * ROWS] = lane_shift(
                source[:, other * ROWS : (other + 1) * ROWS], row_off, col_off, masks
            )


def down_wide(load, wide_one, wide_zero):
    clear_edges(wide_one)

    def body(phase, image, inside, row):
        at = pl.ds(PAD + inside, 64)
        for wide, row_phase in ((wide_one, 1), (wide_zero, 0)):
            right = load(row_phase * 2 + 1, row)
            left = load(row_phase * 2, row)
            wide[image, at, 0:C1] = row_shift(right, -1).astype(bf16)
            wide[image, at, C1 : 2 * C1] = left.astype(bf16)
            wide[image, at, 2 * C1 : 3 * C1] = right.astype(bf16)

    each_chunk(body)


def stem_forward(places, me, gathered, noisy, top, down, kern_down, stage, taps, wide_one, wide_zero):
    at = STEM_AT
    widen(gathered, places, me[0], stage)
    matrix_from(stage, at["kern_down"], kern_down, 9 * C1, C2)
    masks = lane_masks(ROWS)
    taps_on_lanes(noisy, taps, masks, 1)
    kern_in = jnp.concatenate(
        [
            jnp.concatenate([stage[3 * tap : 3 * tap + 3, :], jnp.zeros((5, LANES), f32)], axis=0)
            for tap in range(9)
        ],
        axis=0,
    ).astype(bf16)
    bias_in = stage[at["bias_in"] : at["bias_in"] + 1, :]
    for phase in range(4):
        top[phase] = mm_tn(taps[:, phase * ROWS : (phase + 1) * ROWS].astype(bf16), kern_in) + bias_in
    down_wide(lambda phase, row: top[phase, pl.ds(row, 64), :], wide_one, wide_zero)
    width = 3 * C1
    source = jnp.concatenate(
        [wide_rows(wide_one, -1, 0, width), wide_rows(wide_zero, 0, 0, width), wide_rows(wide_one, 0, 0, width)],
        axis=1,
    )
    down[...] = mm(source, kern_down[...]) + vector_at(stage, at["bias_down"], C2)


def stem_backward(leaving, me, noisy, top, skip, grad_down, kern_down, sent, out, taps, wide_one, wide_zero, wide_grad, low_grad):
    at = STEM_AT
    taps_on_lanes(noisy, taps, lane_masks(ROWS), 1)
    down_wide(lambda phase, row: top[phase, pl.ds(row, 64), :], wide_one, wide_zero)
    clear_edges(wide_grad)

    def body(phase, image, inside, row):
        value = grad_down[pl.ds(row, 64), :].astype(bf16).astype(f32)
        here = pl.ds(PAD + inside, 64)
        wide_grad[image, here, 0:C2] = value.astype(bf16)
        wide_grad[image, here, C2 : 2 * C2] = row_shift(value, 1).astype(bf16)

    each_chunk(body)
    bias_down = jnp.zeros((8, C2), f32)
    bias_down = lax.fori_loop(
        0,
        ROWS // 64,
        lambda n, c: c + fold(grad_down[pl.ds(pl.multiple_of(n * 64, 64), 64), :].astype(bf16).astype(f32)),
        bias_down,
    )
    vector_to(out, at["bias_down"], jnp.sum(bias_down, axis=0, keepdims=True))
    center = wide_rows(wide_grad, 0, 0, C2)
    width = 3 * C1
    for row_tap, (wide, row_off) in enumerate(((wide_one, -1), (wide_zero, 0), (wide_one, 0))):
        product = mm_tn(wide_rows(wide, row_off, 0, width), center)
        matrix_to(out, at["kern_down"] + row_tap * 2 * width, product)

    def taps_rows(first, count):
        return kern_down[first * C1 : (first + count) * C1, :]

    moved = wide_rows(wide_grad, 0, C2, 2 * C2)
    below = wide_rows(wide_grad, 1, 0, C2)
    below_moved = wide_rows(wide_grad, 1, C2, 2 * C2)
    first_pair = mm_nt(center, taps_rows(4, 2))
    second_pair = mm_nt(center, taps_rows(7, 2)) + mm_nt(below, taps_rows(1, 2))
    grads = (
        first_pair[:, :C1],
        first_pair[:, C1:] + mm_nt(moved, taps_rows(3, 1)),
        second_pair[:, :C1],
        second_pair[:, C1:] + mm_nt(moved, taps_rows(6, 1)) + mm_nt(below_moved, taps_rows(0, 1)),
    )
    bias_in = jnp.zeros((8, C1), f32)
    for phase in range(4):
        low_grad[phase] = (skip[phase] + grads[phase]).astype(bf16)
        bias_in = bias_in + fold(low_grad[phase].astype(f32))
    vector_to(out, at["bias_in"], jnp.sum(bias_in, axis=0, keepdims=True))
    kern_in = None
    for phase in range(4):
        part = mm(taps[:, phase * ROWS : (phase + 1) * ROWS].astype(bf16), low_grad[phase])
        kern_in = part if kern_in is None else kern_in + part
    for tap in range(9):
        out[3 * tap : 3 * tap + 3, :] = kern_in[8 * tap : 8 * tap + 3, :]
    out[at["end"] :, :] = jnp.zeros((STEM_ROWS - at["end"], LANES), f32)
    narrow_out(out, me[0], sent, leaving)


def res_forward(
    places, me, gathered, down, embed,
    inner, res_out, act_one, act_two, kern_first, kern_second, dense_two, hidden_pre, stats, gains,
    stage, dense_one, wide,
):
    at = RES_AT
    widen(gathered, places, me[0], stage)
    matrix_from(stage, at["dense_one"], dense_one, TDIM, TEMB)
    matrix_from(stage, at["dense_two"], dense_two, TEMB, C2)
    matrix_from(stage, at["kern_first"], kern_first, 9 * C2, C2)
    matrix_from(stage, at["kern_second"], kern_second, 9 * C2, C2)
    pre = jnp.dot(embed[...], dense_one[...].astype(f32), precision=highest) + vector_at(stage, at["bias_one"], TEMB)
    hidden_pre[...] = pre
    hidden = pre * logistic(pre)
    time_proj = jnp.dot(hidden, dense_two[...].astype(f32), precision=highest) + vector_at(stage, at["bias_two"], C2)
    ones = same_group(C2)
    clear_edges(wide)
    gain = vector_at(stage, at["gain_first"], C2)
    shift = vector_at(stage, at["shift_first"], C2)
    gain_two = vector_at(stage, at["gain_second"], C2)
    shift_two = vector_at(stage, at["shift_second"], C2)
    gains[...] = jnp.concatenate([gain, shift, gain_two, shift_two, jnp.zeros((4, C2), f32)], axis=0)

    def normalize(source, place, gain, shift, keep):
        center, scale = norm_stats(lambda phase, row: source[pl.ds(row, 64), :], 1, C2, ones)
        stats[place : place + IMGS, :] = center
        stats[place + IMGS : place + 2 * IMGS, :] = scale

        def body(phase, image, inside, row):
            value = (source[pl.ds(row, 64), :] - center[image : image + 1, :]) * scale[image : image + 1, :]
            value = value * gain + shift
            value = value * logistic(value)
            keep[pl.ds(row, 64), :] = value.astype(bf16)
            put_shifted(wide, image, inside, value.astype(bf16).astype(f32))

        each_chunk(body)

    normalize(down, 0, gain, shift, act_one)
    bias = vector_at(stage, at["bias_first"], C2)
    product = conv_low(wide, kern_first)
    for image in range(IMGS):
        inner[image * LOW : (image + 1) * LOW, :] = (
            product[image * LOW : (image + 1) * LOW, :] + bias + time_proj[image : image + 1, :]
        )
    normalize(inner, 2 * IMGS, gain_two, shift_two, act_two)
    res_out[...] = down[...] + conv_low(wide, kern_second) + vector_at(stage, at["bias_second"], C2)


def norm_back(load_grad, source, center, scale, gain, shift, ones, active, store):
    def pieces(image, row):
        xhat = (source[pl.ds(row, 64), :] - center[image : image + 1, :]) * scale[image : image + 1, :]
        grad = load_grad(row)
        if active:
            value = xhat * gain + shift
            gate = logistic(value)
            grad = grad * (gate * (1.0 + value * (1.0 - gate)))
        return grad, xhat

    def load(phase, image, row):
        grad, xhat = pieces(image, row)
        return grad, grad * xhat

    gain_grad, shift_grad, mean_one, mean_two = norm_back_stats(load, 1, C2, gain, ones)

    def body(phase, image, inside, row):
        grad, xhat = pieces(image, row)
        store(
            image,
            inside,
            row,
            scale[image : image + 1, :]
            * (grad * gain - mean_one[image : image + 1, :] - xhat * mean_two[image : image + 1, :]),
        )

    each_chunk(body)
    return gain_grad, shift_grad


def res_backward(
    leaving, me, grad_res, down, inner, act_one, act_two, kern_first, kern_second, dense_two, hidden_pre, stats, gains, embed,
    grad_down, sent, out,
    wide, grad_act,
):
    at = RES_AT
    ones = same_group(C2)
    clear_edges(wide)

    def lower(phase, image, inside, row):
        put_shifted(wide, image, inside, grad_res[pl.ds(row, 64), :].astype(bf16).astype(f32))

    each_chunk(lower)
    sums = image_sums(
        lambda phase, image, row: (grad_res[pl.ds(row, 64), :].astype(bf16).astype(f32),), 1, C2
    )[0]
    vector_to(out, at["bias_second"], jnp.sum(sums, axis=0, keepdims=True))
    grad_act[...] = conv_low_back(wide, kern_second)
    conv_low_grad(act_two, wide, out, at["kern_second"])

    def store_inner(image, inside, row, value):
        put_shifted(wide, image, inside, value.astype(bf16).astype(f32))

    gain_grad, shift_grad = norm_back(
        lambda row: grad_act[pl.ds(row, 64), :], inner, stats[8:12, :], stats[12:16, :],
        gains[2:3, :], gains[3:4, :], ones, True, store_inner,
    )
    vector_to(out, at["gain_second"], gain_grad)
    vector_to(out, at["shift_second"], shift_grad)
    inner_sum = jnp.concatenate(
        [
            jnp.sum(fold(wide[image, PAD : PAD + LOW, C2 : 2 * C2].astype(f32)), axis=0, keepdims=True)
            for image in range(IMGS)
        ]
        + [jnp.zeros((4, C2), f32)],
        axis=0,
    )
    time_sum = jnp.sum(inner_sum, axis=0, keepdims=True)
    vector_to(out, at["bias_first"], time_sum)
    vector_to(out, at["bias_two"], time_sum)
    pre = hidden_pre[...]
    gate = logistic(pre)
    contract = (((0,), (0,)), ((), ()))
    matrix_to(
        out, at["dense_two"],
        lax.dot_general(pre * gate, inner_sum, contract, precision=highest, preferred_element_type=f32),
    )
    grad_pre = lax.dot_general(
        inner_sum, dense_two[...].astype(f32), (((1,), (1,)), ((), ())), precision=highest, preferred_element_type=f32
    ) * (gate * (1.0 + pre * (1.0 - gate)))
    vector_to(out, at["bias_one"], jnp.sum(grad_pre, axis=0, keepdims=True))
    matrix_to(
        out, at["dense_one"],
        lax.dot_general(embed[...], grad_pre, contract, precision=highest, preferred_element_type=f32),
    )
    grad_act[...] = conv_low_back(wide, kern_first)
    conv_low_grad(act_one, wide, out, at["kern_first"])

    def store_down(image, inside, row, value):
        grad_down[pl.ds(row, 64), :] = value + grad_res[pl.ds(row, 64), :]

    gain_grad, shift_grad = norm_back(
        lambda row: grad_act[pl.ds(row, 64), :], down, stats[0:4, :], stats[4:8, :],
        gains[0:1, :], gains[1:2, :], ones, True, store_down,
    )
    vector_to(out, at["gain_first"], gain_grad)
    vector_to(out, at["shift_first"], shift_grad)
    out[at["end"] :, :] = jnp.zeros((RES_ROWS - at["end"], LANES), f32)
    narrow_out(out, me[0], sent, leaving)


def attn_forward(
    places, me, gathered, res_out,
    attn_low, normed, qkv, probs, mixed, kern_qkv, kern_proj, stats, gains,
    stage,
):
    at = ATTN_AT
    widen(gathered, places, me[0], stage)
    matrix_from(stage, at["kern_qkv"], kern_qkv, C2, 3 * C2)
    matrix_from(stage, at["kern_proj"], kern_proj, C2, C2)
    ones = same_group(C2)
    gain = vector_at(stage, at["gain_attn"], C2)
    shift = vector_at(stage, at["shift_attn"], C2)
    gains[...] = jnp.concatenate([gain, shift, jnp.zeros((6, C2), f32)], axis=0)
    center, scale = norm_stats(lambda phase, row: res_out[pl.ds(row, 64), :], 1, C2, ones)
    stats[0:IMGS, :] = center
    stats[IMGS : 2 * IMGS, :] = scale

    def body(phase, image, inside, row):
        value = (res_out[pl.ds(row, 64), :] - center[image : image + 1, :]) * scale[image : image + 1, :]
        normed[pl.ds(row, 64), :] = (value * gain + shift).astype(bf16)

    each_chunk(body)
    qkv[...] = mm(normed[...], kern_qkv[...]).astype(bf16)
    for image in range(IMGS):
        rows = slice(image * LOW, (image + 1) * LOW)
        logits = mm_nt(qkv[rows, 0:C2], qkv[rows, C2 : 2 * C2]) * C2 ** (-0.5)
        powers = jnp.exp(logits - jnp.max(logits, axis=1, keepdims=True))
        weights = powers / jnp.sum(powers, axis=1, keepdims=True)
        probs[image] = weights
        mixed[rows, :] = mm(weights.astype(bf16), qkv[rows, 2 * C2 : 3 * C2]).astype(bf16)
    attn_low[...] = (
        res_out[...] + mm(mixed[...], kern_proj[...]) + vector_at(stage, at["bias_proj"], C2)
    ).astype(bf16)


def attn_backward(
    leaving, me, grad_attn, res_out, normed, qkv, probs, mixed, kern_qkv, kern_proj, stats, gains,
    grad_res, sent, out,
    grad_qkv, grad_mixed, grad_normed, low,
):
    at = ATTN_AT
    ones = same_group(C2)
    low[...] = grad_attn[...].astype(bf16)
    sums = image_sums(lambda phase, image, row: (grad_attn[pl.ds(row, 64), :],), 1, C2)[0]
    vector_to(out, at["bias_proj"], jnp.sum(sums, axis=0, keepdims=True))
    matrix_to(out, at["kern_proj"], mm_tn(mixed[...], low[...]))
    grad_mixed[...] = mm_nt(low[...], kern_proj[...]).astype(bf16)
    scale_by = C2 ** (-0.5)
    for image in range(IMGS):
        rows = slice(image * LOW, (image + 1) * LOW)
        query, keys, value = (qkv[rows, part * C2 : (part + 1) * C2] for part in range(3))
        weights = probs[image]
        grad_probs = mm_nt(grad_mixed[rows, :], value)
        grad_qkv[rows, 2 * C2 : 3 * C2] = mm_tn(weights.astype(bf16), grad_mixed[rows, :]).astype(bf16)
        grad_logits = (
            weights * (grad_probs - jnp.sum(weights * grad_probs, axis=1, keepdims=True))
        ).astype(bf16)
        grad_qkv[rows, 0:C2] = (mm(grad_logits, keys) * scale_by).astype(bf16)
        grad_qkv[rows, C2 : 2 * C2] = (mm_tn(grad_logits, query) * scale_by).astype(bf16)
    matrix_to(out, at["kern_qkv"], mm_tn(normed[...], grad_qkv[...]))
    grad_normed[...] = mm_nt(grad_qkv[...], kern_qkv[...])

    def store(image, inside, row, value):
        grad_res[pl.ds(row, 64), :] = value + grad_attn[pl.ds(row, 64), :]

    gain_grad, shift_grad = norm_back(
        lambda row: grad_normed[pl.ds(row, 64), :], res_out, stats[0:4, :], stats[4:8, :],
        gains[0:1, :], gains[1:2, :], ones, False, store,
    )
    vector_to(out, at["gain_attn"], gain_grad)
    vector_to(out, at["shift_attn"], shift_grad)
    out[at["end"] :, :] = jnp.zeros((ATTN_ROWS - at["end"], LANES), f32)
    narrow_out(out, me[0], sent, leaving)


def pick(row, channel):
    lane = lax.broadcasted_iota(jnp.int32, (LANES, LANES), 0)
    ch = lax.broadcasted_iota(jnp.int32, (LANES, LANES), 1)
    return (row * LANES + lane == CIN * ch + channel).astype(f32).astype(bf16)


def head_step(
    places, leaving, me, gathered, attn_low, top, clean, factor,
    grad_attn, skip, loss, sent, out,
    stage, wide, kern_up, merged, act, taps, narrow, grad_wide_zero, grad_wide_one, boxes,
):
    at = HEAD_AT
    widen(gathered, places, me[0], stage)
    ones = same_group(C1)
    kern_up[...] = jnp.zeros(kern_up.shape, bf16)

    def combine(at_row):
        tap = [[stage[pl.ds((3 * a + b) * C2 + at_row, 64), :] for b in range(3)] for a in range(3)]
        by_row = {(0, 0): tap[0], (0, 1): [tap[1][b] + tap[2][b] for b in range(3)],
                  (1, 0): [tap[0][b] + tap[1][b] for b in range(3)], (1, 1): tap[2]}
        for (row_phase, slot), three in by_row.items():
            for col_off in range(3):
                base = (slot * 3 + col_off) * C2
                here = pl.ds(base + at_row, 64)
                if col_off == 0:
                    kern_up[row_phase, here, 0:C1] = three[0].astype(bf16)
                elif col_off == 1:
                    kern_up[row_phase, here, 0:C1] = (three[1] + three[2]).astype(bf16)
                    kern_up[row_phase, here, C1 : 2 * C1] = (three[0] + three[1]).astype(bf16)
                else:
                    kern_up[row_phase, here, C1 : 2 * C1] = three[2].astype(bf16)

    chunks(C2, 64, combine)
    clear_edges(wide)

    def spread_low(phase, image, inside, row):
        put_shifted(wide, image, inside, attn_low[pl.ds(row, 64), :].astype(f32))

    each_chunk(spread_low)
    bias_up = stage[at["bias_up"] : at["bias_up"] + 1, :]
    for row_phase in range(2):
        product = mm(
            jnp.concatenate(
                [wide_rows(wide, row_phase - 1, 0, 3 * C2), wide_rows(wide, row_phase, 0, 3 * C2)], axis=1
            ),
            kern_up[row_phase],
        )
        for col_phase in range(2):
            phase = row_phase * 2 + col_phase
            merged[phase] = product[:, col_phase * C1 : (col_phase + 1) * C1] + bias_up + top[phase]
    gain = stage[at["gain_out"] : at["gain_out"] + 1, :]
    shift = stage[at["shift_out"] : at["shift_out"] + 1, :]
    center, scale = norm_stats(lambda phase, row: merged[phase, pl.ds(row, 64), :], 4, C1, ones)

    def body(phase, image, inside, row):
        value = (merged[phase, pl.ds(row, 64), :] - center[image : image + 1, :]) * scale[image : image + 1, :]
        value = value * gain + shift
        act[phase, pl.ds(row, 64), :] = (value * logistic(value)).astype(bf16)

    each_chunk(body, 4)
    for channel in range(CIN):
        total = None
        for row in range(3):
            part = mm(stage[pl.ds(at["kern_out"] + row, 9, 3), :].astype(bf16), pick(row, channel))
            total = part if total is None else total + part
        narrow[pl.ds(channel, 9, 8), :] = total
    for channel in range(CIN, 8):
        narrow[pl.ds(channel, 9, 8), :] = jnp.zeros((9, LANES), f32)
    kern_out = narrow[...].astype(bf16)
    masks = lane_masks(ROWS)
    for phase in range(4):
        taps[:, phase * ROWS : (phase + 1) * ROWS] = mm_nt(kern_out, act[phase])
    lane = lax.broadcasted_iota(jnp.int32, (8, LANES), 1)
    channel_at = lax.broadcasted_iota(jnp.int32, (8, LANES), 0)
    bias_out = jnp.sum(
        jnp.where((lane == channel_at) & (channel_at < CIN), stage[at["bias_out"] : at["bias_out"] + 1, :], 0.0),
        axis=1,
        keepdims=True,
    )
    pixel_count = CIN * SIDE * SIDE
    loss_sum = jnp.zeros((8, ROWS), f32)
    bias_grad = jnp.zeros((8, 1), f32)
    grad_lanes = []
    for phase in range(4):
        predict = bias_out
        for tap, off in enumerate(TAPS):
            other, row_off, col_off = tap_source(phase, off)
            predict = predict + lane_shift(
                taps[8 * tap : 8 * tap + 8, other * ROWS : (other + 1) * ROWS], row_off, col_off, masks
            )
        error = predict - clean[:, phase * ROWS : (phase + 1) * ROWS]
        loss_sum = loss_sum + error * error * factor[...]
        grad = ((2.0 / pixel_count) * factor[...] * error).astype(bf16).astype(f32)
        bias_grad = bias_grad + jnp.sum(grad, axis=1, keepdims=True)
        grad_lanes.append(grad)
    loss[...] = jnp.sum(jnp.sum(loss_sum, axis=1, keepdims=True), axis=0, keepdims=True) * (1.0 / pixel_count)
    out[at["bias_out"] : at["bias_out"] + 1, :] = jnp.sum(
        jnp.where((lane == channel_at) & (channel_at < CIN), bias_grad, 0.0), axis=0, keepdims=True
    )
    for phase in range(4):
        for tap, off in enumerate(TAPS):
            other, row_off, col_off = tap_source(phase, (-off[0], -off[1]))
            taps[8 * tap : 8 * tap + 8, phase * ROWS : (phase + 1) * ROWS] = lane_shift(
                grad_lanes[other], row_off, col_off, masks
            )
    kern_grad = None
    for phase in range(4):
        low = taps[:, phase * ROWS : (phase + 1) * ROWS].astype(bf16)
        part = mm(low, act[phase])
        kern_grad = part if kern_grad is None else kern_grad + part
        skip[phase] = mm_tn(low, kern_out)
    narrow[...] = kern_grad
    for row in range(3):
        total = None
        for channel in range(CIN):
            pieces = parts_of(narrow[pl.ds(channel, 9, 8), :])
            part = sum(mm_nt(piece, pick(row, channel)) for piece in pieces)
            total = part if total is None else total + part
        out[pl.ds(at["kern_out"] + row, 9, 3), :] = total

    def pieces(phase, image, row):
        xhat = (merged[phase, pl.ds(row, 64), :] - center[image : image + 1, :]) * scale[image : image + 1, :]
        value = xhat * gain + shift
        gate = logistic(value)
        return skip[phase, pl.ds(row, 64), :] * (gate * (1.0 + value * (1.0 - gate))), xhat

    def load(phase, image, row):
        grad, xhat = pieces(phase, image, row)
        return grad, grad * xhat

    gain_grad, shift_grad, mean_one, mean_two = norm_back_stats(load, 4, C1, gain, ones)
    vector_to(out, at["gain_out"], gain_grad)
    vector_to(out, at["shift_out"], shift_grad)
    clear_edges(grad_wide_zero)
    clear_edges(grad_wide_one)
    clear_edges(boxes)
    wides = (grad_wide_zero, grad_wide_one)

    def back(phase, image, inside, row):
        for row_phase in range(2):
            pair = []
            for col_phase in range(2):
                phase = row_phase * 2 + col_phase
                grad, xhat = pieces(phase, image, row)
                value = scale[image : image + 1, :] * (
                    grad * gain - mean_one[image : image + 1, :] - xhat * mean_two[image : image + 1, :]
                )
                skip[phase, pl.ds(row, 64), :] = value
                pair.append(value.astype(bf16).astype(f32))
            put_shifted(wides[row_phase], image, inside, jnp.concatenate(pair, axis=1))
            here = pl.ds(PAD + inside, 64)
            base = row_phase * 3 * C1
            boxes[image, here, base : base + C1] = pair[1] + row_shift(pair[0], 1)
            boxes[image, here, base + C1 : base + 2 * C1] = pair[0] + pair[1]
            boxes[image, here, base + 2 * C1 : base + 3 * C1] = row_shift(pair[1], -1) + pair[0]

    each_chunk(back)
    bias_sum = jnp.zeros((8, C1), f32)
    for row_phase in range(2):
        for image in range(IMGS):
            both = fold(wides[row_phase][image, PAD : PAD + LOW, C2 : 2 * C2].astype(f32))
            bias_sum = bias_sum + both[:, :C1] + both[:, C1:]
    vector_to(out, at["bias_up"], jnp.sum(bias_sum, axis=0, keepdims=True))
    total = None
    for row_phase in range(2):
        for slot in range(2):
            row_off = row_phase - 1 + slot
            for col_off in range(3):
                part = mm_nt(
                    wide_rows(wides[row_phase], -row_off, (2 - col_off) * C2, (3 - col_off) * C2),
                    kern_up[row_phase, (slot * 3 + col_off) * C2 : (slot * 3 + col_off + 1) * C2, :],
                )
                total = part if total is None else total + part
    grad_attn[...] = total
    width = 3 * C1

    def box_rows(row_off, row_phase):
        return boxes[
            :, PAD + 16 * row_off : PAD + 16 * row_off + LOW, row_phase * width : (row_phase + 1) * width
        ].reshape(ROWS, width)

    summed = (
        box_rows(0, 1) + box_rows(1, 0),
        box_rows(0, 0) + box_rows(0, 1),
        box_rows(-1, 1) + box_rows(0, 0),
    )
    for row_tap in range(3):
        product = mm_tn(attn_low[...], summed[row_tap].astype(bf16))
        for col_tap in range(3):
            tap = row_tap * 3 + col_tap
            out[tap * C2 : (tap + 1) * C2, :] = product[:, col_tap * C1 : (col_tap + 1) * C1]
    out[at["end"] :, :] = jnp.zeros((HEAD_ROWS - at["end"], LANES), f32)
    narrow_out(out, me[0], sent, leaving)


def sds(shape, dtype=f32):
    return jax.ShapeDtypeStruct(shape, dtype)


def run(body, ins, outs, scratch):
    in_leaves, in_tree = jax.tree.flatten(ins)
    out_leaves, out_tree = jax.tree.flatten(outs)

    def kernel(*refs):
        split = len(in_leaves), len(in_leaves) + len(out_leaves)
        body(
            *jax.tree.unflatten(in_tree, refs[: split[0]]),
            *jax.tree.unflatten(out_tree, refs[split[0] : split[1]]),
            *refs[split[1] :],
        )

    whole = pl.BlockSpec(memory_space=pltpu.VMEM)
    results = pl.pallas_call(
        kernel,
        out_shape=out_leaves,
        in_specs=[pl.BlockSpec(memory_space=pltpu.SMEM)] + [whole] * (len(in_leaves) - 1),
        out_specs=[whole] * len(out_leaves),
        scratch_shapes=scratch,
        compiler_params=pltpu.CompilerParams(vmem_limit_bytes=52 * 2**20),
    )(*in_leaves)
    return jax.tree.unflatten(out_tree, results)


def wide_scratch(width, dtype=bf16):
    return pltpu.VMEM((IMGS, PADDED, width), dtype)


def forward_stem(me, weights, noisy):
    arrays, places = weights
    return run(
        partial(stem_forward, places),
        [me, arrays, noisy],
        [sds((4, ROWS, C1)), sds((ROWS, C2)), sds((9 * C1, C2), bf16)],
        [
            pltpu.VMEM((STEM_ROWS, LANES), f32), pltpu.VMEM((72, 4 * ROWS), f32),
            wide_scratch(3 * C1), wide_scratch(3 * C1),
        ],
    )


def forward_res(me, weights, down, embed):
    arrays, places = weights
    return run(
        partial(res_forward, places),
        [me, arrays, down, embed],
        [
            sds((ROWS, C2)), sds((ROWS, C2)), sds((ROWS, C2), bf16), sds((ROWS, C2), bf16),
            sds((9 * C2, C2), bf16), sds((9 * C2, C2), bf16), sds((TEMB, C2), bf16), sds((8, TEMB)),
            sds((16, C2)), sds((8, C2)),
        ],
        [pltpu.VMEM((RES_ROWS, LANES), f32), pltpu.VMEM((TDIM, TEMB), bf16), wide_scratch(3 * C2)],
    )


def forward_attn(me, weights, res_out):
    arrays, places = weights
    return run(
        partial(attn_forward, places),
        [me, arrays, res_out],
        [
            sds((ROWS, C2), bf16), sds((ROWS, C2), bf16), sds((ROWS, 3 * C2), bf16), sds((IMGS, LOW, LOW)),
            sds((ROWS, C2), bf16), sds((C2, 3 * C2), bf16), sds((C2, C2), bf16), sds((8, C2)), sds((8, C2)),
        ],
        [pltpu.VMEM((ATTN_ROWS, LANES), f32)],
    )


def both_head(me, weights, leaving, attn_low, top, clean, factor):
    arrays, places = weights
    shapes, out_places = leaving
    return run(
        partial(head_step, places, out_places),
        [me, arrays, attn_low, top, clean, factor],
        [sds((ROWS, C2)), sds((4, ROWS, C1)), sds((1, 1)), shapes],
        [
            pltpu.VMEM((HEAD_ROWS, LANES), f32),
            pltpu.VMEM((HEAD_ROWS, LANES), f32), wide_scratch(3 * C2), pltpu.VMEM((2, 6 * C2, C2), bf16),
            pltpu.VMEM((4, ROWS, C1), f32), pltpu.VMEM((4, ROWS, C1), bf16), pltpu.VMEM((72, 4 * ROWS), f32),
            pltpu.VMEM((72, LANES), f32), wide_scratch(3 * C2), wide_scratch(3 * C2), wide_scratch(6 * C1, f32),
        ],
    )


def backward_attn(me, leaving, *saved):
    shapes, out_places = leaving
    return run(
        partial(attn_backward, out_places),
        [me, *saved],
        [sds((ROWS, C2)), shapes],
        [
            pltpu.VMEM((ATTN_ROWS, LANES), f32),
            pltpu.VMEM((ROWS, 3 * C2), bf16), pltpu.VMEM((ROWS, C2), bf16), pltpu.VMEM((ROWS, C2), f32),
            pltpu.VMEM((ROWS, C2), bf16),
        ],
    )


def backward_res(me, leaving, *saved):
    shapes, out_places = leaving
    return run(
        partial(res_backward, out_places),
        [me, *saved],
        [sds((ROWS, C2)), shapes],
        [pltpu.VMEM((RES_ROWS, LANES), f32), wide_scratch(3 * C2), pltpu.VMEM((ROWS, C2), f32)],
    )


def backward_stem(me, leaving, *saved):
    shapes, out_places = leaving
    return run(
        partial(stem_backward, out_places),
        [me, *saved],
        [shapes],
        [
            pltpu.VMEM((STEM_ROWS, LANES), f32),
            pltpu.VMEM((72, 4 * ROWS), f32), wide_scratch(3 * C1), wide_scratch(3 * C1), wide_scratch(2 * C2),
            pltpu.VMEM((4, ROWS, C1), bf16),
        ],
    )


def plan(step_counts, time_index, teacher_size):
    position = time_index % step_counts
    time_values = (2 * position + teacher_size).astype(f32) / (2 * step_counts).astype(f32)
    alpha_t = jnp.cos(0.5 * math.pi * time_values)
    sigma_t = jnp.sin(0.5 * math.pi * time_values)
    weight = jnp.maximum(alpha_t * alpha_t / (sigma_t * sigma_t), 1.0)
    return (time_values, alpha_t, sigma_t, weight)


def sinusoid(time_values):
    half_dim = TDIM // 2
    frequency = jnp.exp(-math.log(10000.0) * jnp.arange(half_dim, dtype=f32) / half_dim)
    angles = 1000.0 * time_values[:, None] * frequency[None, :]
    return jnp.concatenate([jnp.sin(angles), jnp.cos(angles)], axis=1)


def by_phase(images):
    split = images.reshape(IMGS, CIN, 16, 2, 16, 2).transpose(1, 3, 5, 0, 2, 4).reshape(CIN, 4 * ROWS)
    return jnp.pad(split, ((0, 8 - CIN), (0, 0)))


def prepare(clean_images, noise_field, step_counts, time_index, teacher_size, image_count, total_live):
    slot_count = clean_images.shape[0]
    time_values, alpha_t, sigma_t, weight = plan(step_counts, time_index, teacher_size)
    live_mask = (jnp.arange(slot_count, dtype=jnp.int32) < image_count).astype(f32)
    factor = live_mask * weight / total_live
    noisy = (alpha_t[:, None, None] * clean_images + sigma_t[:, None, None] * noise_field).astype(bf16).astype(f32)
    embed = jnp.pad(sinusoid(time_values), ((0, 8 - IMGS), (0, 0)))
    factor_lanes = jnp.repeat(factor, LOW)[None, :]
    return by_phase(noisy), by_phase(clean_images), factor_lanes, embed


AXES = ("dp", "fsdp")


def swap(values, mask):
    count = lax.axis_size(AXES)
    return lax.ppermute(values, AXES, [(here, here ^ mask) for here in range(count)])


def axis_rounds(count, swapped):
    bits = [1 << at for at in range(1, count.bit_length() - 1)]
    plane = bits[:2][::-1] if swapped else bits[:2]
    rest = bits[2:]
    return [[bit] for bit in plane], [rest[at : at + 2] for at in range(0, len(rest), 2)]


def spans(bits):
    return [sum(bit for place, bit in enumerate(bits) if number >> place & 1) for number in range(1 << len(bits))]


def gather(shard, swapped):
    count = lax.axis_size(AXES)
    plane, rest = axis_rounds(count, swapped)
    held, masks = shard[None], [0]
    for bits in rest + plane[::-1]:
        reach = spans(bits)[1:]
        arrived = [swap(held, mask) for mask in reach]
        held = jnp.concatenate([held] + arrived, axis=0)
        masks = masks + [mask ^ own for mask in reach for own in masks]
    return [held, swap(held, 1)], [masks, [mask ^ 1 for mask in masks]]


def reduce_masks(count, swapped):
    plane, rest = axis_rounds(count, swapped)
    order = [0]
    for bits in (rest[::-1] + plane[::-1]):
        order = [mask ^ own for mask in spans(bits) for own in order]
    return order


def reduce(kept, sent, swapped):
    count = lax.axis_size(AXES)
    plane, rest = axis_rounds(count, swapped)
    total = kept.astype(f32) + swap(sent, 1).astype(f32)
    for bits in plane + rest:
        reach = spans(bits)
        size = total.shape[0] // len(reach)
        arrived = [swap(total[size * at : size * (at + 1)].astype(bf16), mask) for at, mask in enumerate(reach) if at]
        total = total[:size]
        for piece in arrived:
            total = total + piece.astype(f32)
    return total[0]


BLOCK_ROWS = (STEM_ROWS, RES_ROWS, ATTN_ROWS, HEAD_ROWS)
GATHERS = (
    (((0, 0, 80), (1, 0, 200)), False),
    (((1, 200, 344), (3, 0, 80), (2, 0, 72)), True),
)
REDUCES = (
    ((0, 80, False),),
    ((0, 176, False), (176, 344, True)),
    ((0, 72, True),),
    ((0, 80, False),),
)


def ordered_weights(shards):
    found = []
    for shard, rows in zip(shards, BLOCK_ROWS):
        whole = lax.all_gather(shard.reshape(-1), AXES, axis=0, tiled=True).reshape(1, rows, LANES)
        found.append(([whole], [([0], 0, rows, 0, 0)]))
    return found


def gathered_weights(shards):
    found = [([], []) for _ in shards]
    for members, swapped in GATHERS:
        group = jnp.concatenate([shards[block][lo:hi] for block, lo, hi in members], axis=0)
        arrays, masks = gather(group, swapped)
        at = 0
        for block, lo, hi in members:
            for array, owners in zip(arrays, masks):
                found[block][0].append(array)
                found[block][1].append((owners, at, at + hi - lo, shards[block].shape[0], lo))
            at += hi - lo
    return found


def leaving_shapes(block, count, ordered):
    rows = BLOCK_ROWS[block]
    if ordered:
        return [sds((1, rows, LANES))], [([0], 0, rows, 0, 0)]
    shapes, places = [], []
    for lo, hi, swapped in REDUCES[block]:
        masks = reduce_masks(count, swapped)
        for core in (0, 1):
            shapes.append(sds((count // 2, hi - lo, LANES), bf16))
            places.append(([mask ^ core for mask in masks], 0, hi - lo, rows // count, lo))
    return shapes, places


def reduced(block, leaving, ordered):
    if ordered:
        return lax.psum_scatter(leaving[0].reshape(-1), AXES, scatter_dimension=0, tiled=True)
    parts = []
    for number, (lo, hi, swapped) in enumerate(REDUCES[block]):
        parts.append(reduce(leaving[2 * number], leaving[2 * number + 1], swapped))
    return jnp.concatenate(parts, axis=0).reshape(-1)


def scalar_sums(values):
    count = lax.axis_size(AXES)
    row = jnp.concatenate([value.reshape(1) for value in values] + [jnp.zeros((LANES - len(values),), f32)])
    sent = jnp.broadcast_to(row[None, None, :], (count, 1, LANES))
    arrived = lax.all_to_all(sent, AXES, 0, 0, tiled=True)
    total = jnp.sum(arrived, axis=(0, 1))
    return [total[at] for at in range(len(values))]


def adam_update(master, first, second, gradient, step_value):
    first_new = beta_one * first + (1.0 - beta_one) * gradient
    second_new = beta_two * second + (1.0 - beta_two) * gradient * gradient
    fix_one = 1.0 - jnp.power(jnp.float32(beta_one), step_value)
    fix_two = 1.0 - jnp.power(jnp.float32(beta_two), step_value)
    master_new = master - learn_rate * (
        first_new / fix_one / (jnp.sqrt(second_new / fix_two) + adam_eps) + decay_rate * master
    )
    return (master_new, first_new, second_new, master_new.astype(bf16))


def per_device(
    clean_images, noise_field, step_counts, time_index, teacher_size, image_counts, adam_step,
    stem_master, stem_first, stem_second, res_master, res_first, res_second,
    attn_master, attn_first, attn_second, head_master, head_first, head_second,
):
    masters = (stem_master, res_master, attn_master, head_master)
    firsts = (stem_first, res_first, attn_first, head_first)
    seconds = (stem_second, res_second, attn_second, head_second)
    count = lax.axis_size(AXES)
    ordered = count != 32
    me = lax.axis_index(AXES).astype(jnp.int32).reshape(1)
    shards = [master.astype(bf16).reshape(-1, LANES) for master in masters]
    weights = ordered_weights(shards) if ordered else gathered_weights(shards)
    leaving = [leaving_shapes(block, count, ordered) for block in range(4)]
    (total_live,) = scalar_sums([image_counts[0].astype(f32)])
    noisy, clean, factor, embed = prepare(
        clean_images, noise_field, step_counts, time_index, teacher_size, image_counts[0], total_live
    )
    top, down, kern_down = forward_stem(me, weights[0], noisy)
    inner, res_out, act_one, act_two, kern_first, kern_second, dense_two, hidden_pre, stats, gains = forward_res(
        me, weights[1], down, embed
    )
    attn_low, normed, qkv, probs, mixed, kern_qkv, kern_proj, attn_stats, attn_gains = forward_attn(
        me, weights[2], res_out
    )
    grad_attn, skip, loss_local, head_out = both_head(
        me, weights[3], leaving[3], attn_low, top, clean, factor
    )
    grad_res, attn_out = backward_attn(
        me, leaving[2], grad_attn, res_out, normed, qkv, probs, mixed, kern_qkv, kern_proj, attn_stats, attn_gains
    )
    grad_down, res_out_grads = backward_res(
        me, leaving[1], grad_res, down, inner, act_one, act_two, kern_first, kern_second, dense_two, hidden_pre,
        stats, gains, embed,
    )
    (stem_out,) = backward_stem(me, leaving[0], noisy, top, skip, grad_down, kern_down)
    shard_grads = [
        reduced(block, out, ordered) for block, out in enumerate((stem_out, res_out_grads, attn_out, head_out))
    ]
    sum_local = sum((jnp.sum(jnp.square(gradient)) for gradient in shard_grads))
    loss_value, sum_sq = scalar_sums([loss_local, sum_local])
    grad_norm = jnp.sqrt(sum_sq)
    clip_scale = clip_limit / jnp.maximum(grad_norm, clip_limit)
    step_value = adam_step[0].astype(f32)
    results = [loss_value, grad_norm]
    for block_idx in range(4):
        results.extend(
            adam_update(
                masters[block_idx], firsts[block_idx], seconds[block_idx], shard_grads[block_idx] * clip_scale, step_value
            )
        )
    return tuple(results)


def solution(mesh):
    split = P(("dp", "fsdp"))
    images = P(("dp", "fsdp"), None, None)
    return jax.shard_map(
        per_device,
        mesh=mesh,
        in_specs=(images, images, split, split, split, split, P()) + (split,) * 12,
        out_specs=(P(), P()) + (split,) * 16,
        check_vma=False,
    )
```

```python
from functools import partial
import math

import jax
import jax.numpy as jnp
from jax import lax
from jax.experimental import pallas as pl
from jax.experimental.pallas import tpu as pltpu
from jax.sharding import PartitionSpec as P

C1 = 128
C2 = 256
GROUPS = 32
TDIM = 128
TEMB = 512
CIN = 3
SIDE = 32
LANES = 128
IMGS = 4
LOW = 256
ROWS = IMGS * LOW
PAD = 16
PADDED = LOW + 2 * PAD

clip_limit = 0.05
learn_rate = 0.05
beta_one = 0.9
beta_two = 0.999
adam_eps = 1e-08
decay_rate = 0.01
norm_eps = 1e-05

f32 = jnp.float32
bf16 = jnp.bfloat16
highest = lax.Precision.HIGHEST

STEM_ROWS, RES_ROWS, ATTN_ROWS, HEAD_ROWS = 2560, 11008, 2304, 2560

STEM_AT = dict(kern_in=0, bias_in=27, kern_down=28, bias_down=2332, end=2334)
RES_AT = dict(
    dense_one=0, bias_one=512, dense_two=516, bias_two=1540, gain_first=1542, shift_first=1544,
    kern_first=1546, bias_first=6154, gain_second=6156, shift_second=6158, kern_second=6160,
    bias_second=10768, end=10770,
)
ATTN_AT = dict(gain_attn=0, shift_attn=2, kern_qkv=4, kern_proj=1540, bias_proj=2052, end=2054)
HEAD_AT = dict(kern_up=0, bias_up=2304, gain_out=2305, shift_out=2306, kern_out=2307, bias_out=2334, end=2335)


def mm(a, b):
    return jnp.dot(a, b, preferred_element_type=f32)


def mm_nt(a, b):
    return lax.dot_general(a, b, (((1,), (1,)), ((), ())), preferred_element_type=f32)


def mm_tn(a, b):
    return lax.dot_general(a, b, (((0,), (0,)), ((), ())), preferred_element_type=f32)


def parts_of(values):
    high = values.astype(bf16)
    rest = values - high.astype(f32)
    middle = rest.astype(bf16)
    return high, middle, (rest - middle.astype(f32)).astype(bf16)


def mm_exact(values, matrix):
    return sum(mm(piece, matrix) for piece in parts_of(values))


def same_group(channels):
    size = channels // GROUPS
    down_at = lax.broadcasted_iota(jnp.int32, (channels, channels), 0) // size
    across = lax.broadcasted_iota(jnp.int32, (channels, channels), 1) // size
    return (down_at == across).astype(f32).astype(bf16)


def row_shift(values, step):
    count = values.shape[0]
    moved = pltpu.roll(values, (-step) % count, 0)
    column = lax.broadcasted_iota(jnp.int32, values.shape, 0) & 15
    return jnp.where(column == (0 if step < 0 else 15), 0.0, moved)


def chunks(total, size, body):
    def step(number, carry):
        body(pl.multiple_of(number * size, size))
        return carry

    lax.fori_loop(0, total // size, step, 0, unroll=True)


def widen(pieces, places, me, stage):
    for ref, (masks, lo, hi, per_shard, begin) in zip(pieces, places):
        for number, mask in enumerate(masks):
            owner = me ^ mask
            at = pl.multiple_of(owner * per_shard + begin, 8)
            stage[pl.ds(at, hi - lo), :] = ref[number, lo:hi, :].astype(f32)


def narrow_out(stage, me, outs, places):
    for ref, (masks, lo, hi, per_shard, begin) in zip(outs, places):
        for number, mask in enumerate(masks):
            owner = me ^ mask
            at = pl.multiple_of(owner * per_shard + begin, 8)
            ref[number, lo:hi, :] = stage[pl.ds(at, hi - lo), :].astype(ref.dtype)


def matrix_from(stage, base, out, depth, width):
    lanes = width // LANES

    def copy(at):
        for lane in range(lanes):
            out[pl.ds(at, 128), lane * LANES : (lane + 1) * LANES] = stage[
                pl.ds(base + lanes * at + lane, 128, lanes), :
            ].astype(bf16)

    chunks(depth, 128, copy)


def matrix_to(out, base, value):
    depth, width = value.shape
    lanes = width // LANES
    for lane in range(lanes):
        out[pl.ds(base + lane, depth, lanes), :] = value[:, lane * LANES : (lane + 1) * LANES]


def vector_at(stage, base, width):
    return jnp.concatenate([stage[base + lane : base + lane + 1, :] for lane in range(width // LANES)], axis=1)


def vector_to(out, base, value):
    for lane in range(value.shape[1] // LANES):
        out[base + lane : base + lane + 1, :] = value[:, lane * LANES : (lane + 1) * LANES]


def fold(values):
    return jnp.sum(values.reshape(values.shape[0] // 8, 8, values.shape[1]), axis=0)


def image_sums(load, phases, width):
    sums = []
    for image in range(IMGS):
        def step(number, carry):
            row = pl.multiple_of(image * LOW + number * 64, 64)
            for phase in range(phases):
                carry = tuple(c + fold(v) for c, v in zip(carry, load(phase, image, row)))
            return carry

        first = load(0, image, image * LOW)
        carry = lax.fori_loop(0, 4, step, tuple(jnp.zeros((8, width), f32) for _ in first), unroll=True)
        sums.append([jnp.sum(c, axis=0, keepdims=True) for c in carry])
    return [jnp.concatenate(list(group), axis=0) for group in zip(*sums)]


def norm_stats(load, phases, width, ones):
    count = LOW * phases * (width // GROUPS)
    (total,) = image_sums(lambda phase, image, row: (load(phase, row),), phases, width)
    center = mm_exact(total, ones) * (1.0 / count)

    def squares(phase, image, row):
        away = load(phase, row) - center[image : image + 1, :]
        return (away * away,)

    (total,) = image_sums(squares, phases, width)
    spread = mm_exact(total, ones) * (1.0 / count)
    return center, lax.rsqrt(spread + norm_eps)


def norm_back_stats(load, phases, width, gain, ones):
    count = LOW * phases * (width // GROUPS)
    shift_sum, gain_sum = image_sums(load, phases, width)
    means = mm_exact(jnp.concatenate([shift_sum * gain, gain_sum * gain], axis=0), ones) * (1.0 / count)
    return (
        jnp.sum(gain_sum, axis=0, keepdims=True),
        jnp.sum(shift_sum, axis=0, keepdims=True),
        means[:IMGS],
        means[IMGS:],
    )


def logistic(values):
    return 1.0 / (1.0 + jnp.exp(-values))


def each_chunk(body, phases=1, size=64):
    for image in range(IMGS):
        def step(number, carry):
            inside = pl.multiple_of(number * size, size)
            for phase in range(phases):
                body(phase, image, inside, image * LOW + inside)
            return carry

        lax.fori_loop(0, LOW // size, step, 0, unroll=True)


def clear_edges(wide):
    for image in range(IMGS):
        wide[image, 0:PAD, :] = jnp.zeros((PAD, wide.shape[2]), wide.dtype)
        wide[image, PAD + LOW : PADDED, :] = jnp.zeros((PAD, wide.shape[2]), wide.dtype)


def put_shifted(wide, image, inside, value):
    width = value.shape[1]
    at = pl.ds(PAD + inside, value.shape[0])
    wide[image, at, 0:width] = row_shift(value, -1).astype(bf16)
    wide[image, at, width : 2 * width] = value.astype(bf16)
    wide[image, at, 2 * width : 3 * width] = row_shift(value, 1).astype(bf16)


def wide_rows(wide, row_off, lo, hi):
    begin = PAD + 16 * row_off
    return wide[:, begin : begin + LOW, lo:hi].reshape(ROWS, hi - lo)


def conv_low(wide, kern):
    width = wide.shape[2]
    total = None
    for tap in range(3):
        part = mm(wide_rows(wide, tap - 1, 0, width), kern[tap * width : (tap + 1) * width, :])
        total = part if total is None else total + part
    return total


def conv_low_back(wide, kern):
    total = None
    for row_tap in range(3):
        taps = [kern[(row_tap * 3 + col_tap) * C2 : (row_tap * 3 + col_tap + 1) * C2, :] for col_tap in (2, 1, 0)]
        part = mm_nt(wide_rows(wide, 1 - row_tap, 0, 3 * C2), jnp.concatenate(taps, axis=1))
        total = part if total is None else total + part
    return total


def conv_low_grad(source, wide, out, base):
    for row_tap in range(3):
        product = mm_tn(source[...], wide_rows(wide, 1 - row_tap, 0, 3 * C2))
        for col_tap in range(3):
            tap = row_tap * 3 + col_tap
            matrix_to(out, base + tap * 2 * C2, product[:, (2 - col_tap) * C2 : (3 - col_tap) * C2])


def lane_masks(width):
    place = lax.broadcasted_iota(jnp.int32, (8, width), 1)
    row, column = (place >> 4) & 15, place & 15

    def valid(row_off, col_off):
        keep = None
        for at, off in ((row, row_off), (column, col_off)):
            if off:
                inside = at != (0 if off < 0 else 15)
                keep = inside if keep is None else keep & inside
        return keep

    return {(r, c): valid(r, c) for r in (-1, 0, 1) for c in (-1, 0, 1)}


def lane_shift(values, row_off, col_off, masks):
    step = 16 * row_off + col_off
    if step == 0:
        return values
    moved = pltpu.roll(values, (-step) % values.shape[1], 1)
    return jnp.where(masks[(row_off, col_off)], moved, 0.0)


def tap_source(phase, tap_off):
    row, col = phase // 2 + tap_off[0], phase % 2 + tap_off[1]
    return (row % 2) * 2 + col % 2, row // 2, col // 2


TAPS = tuple((row - 1, col - 1) for row in range(3) for col in range(3))


def taps_on_lanes(source, out, masks, sign):
    for phase in range(4):
        for tap, off in enumerate(TAPS):
            other, row_off, col_off = tap_source(phase, (sign * off[0], sign * off[1]))
            out[8 * tap : 8 * tap + 8, phase * ROWS : (phase + 1) * ROWS] = lane_shift(
                source[:, other * ROWS : (other + 1) * ROWS], row_off, col_off, masks
            )


def down_wide(load, wide_one, wide_zero):
    clear_edges(wide_one)

    def body(phase, image, inside, row):
        at = pl.ds(PAD + inside, 64)
        for wide, row_phase in ((wide_one, 1), (wide_zero, 0)):
            right = load(row_phase * 2 + 1, row)
            left = load(row_phase * 2, row)
            wide[image, at, 0:C1] = row_shift(right, -1).astype(bf16)
            wide[image, at, C1 : 2 * C1] = left.astype(bf16)
            wide[image, at, 2 * C1 : 3 * C1] = right.astype(bf16)

    each_chunk(body)


def stem_forward(places, me, gathered, noisy, top, down, kern_down, stage, taps, wide_one, wide_zero):
    at = STEM_AT
    widen(gathered, places, me[0], stage)
    matrix_from(stage, at["kern_down"], kern_down, 9 * C1, C2)
    masks = lane_masks(ROWS)
    taps_on_lanes(noisy, taps, masks, 1)
    kern_in = jnp.concatenate(
        [
            jnp.concatenate([stage[3 * tap : 3 * tap + 3, :], jnp.zeros((5, LANES), f32)], axis=0)
            for tap in range(9)
        ],
        axis=0,
    ).astype(bf16)
    bias_in = stage[at["bias_in"] : at["bias_in"] + 1, :]
    for phase in range(4):
        top[phase] = mm_tn(taps[:, phase * ROWS : (phase + 1) * ROWS].astype(bf16), kern_in) + bias_in
    down_wide(lambda phase, row: top[phase, pl.ds(row, 64), :], wide_one, wide_zero)
    width = 3 * C1
    source = jnp.concatenate(
        [wide_rows(wide_one, -1, 0, width), wide_rows(wide_zero, 0, 0, width), wide_rows(wide_one, 0, 0, width)],
        axis=1,
    )
    down[...] = mm(source, kern_down[...]) + vector_at(stage, at["bias_down"], C2)


def stem_backward(leaving, me, noisy, top, skip, grad_down, kern_down, sent, out, taps, wide_one, wide_zero, wide_grad, low_grad):
    at = STEM_AT
    taps_on_lanes(noisy, taps, lane_masks(ROWS), 1)
    down_wide(lambda phase, row: top[phase, pl.ds(row, 64), :], wide_one, wide_zero)
    clear_edges(wide_grad)

    def body(phase, image, inside, row):
        value = grad_down[pl.ds(row, 64), :].astype(bf16).astype(f32)
        here = pl.ds(PAD + inside, 64)
        wide_grad[image, here, 0:C2] = value.astype(bf16)
        wide_grad[image, here, C2 : 2 * C2] = row_shift(value, 1).astype(bf16)

    each_chunk(body)
    bias_down = jnp.zeros((8, C2), f32)
    bias_down = lax.fori_loop(
        0,
        ROWS // 64,
        lambda n, c: c + fold(grad_down[pl.ds(pl.multiple_of(n * 64, 64), 64), :].astype(bf16).astype(f32)),
        bias_down,
    )
    vector_to(out, at["bias_down"], jnp.sum(bias_down, axis=0, keepdims=True))
    center = wide_rows(wide_grad, 0, 0, C2)
    width = 3 * C1
    for row_tap, (wide, row_off) in enumerate(((wide_one, -1), (wide_zero, 0), (wide_one, 0))):
        product = mm_tn(wide_rows(wide, row_off, 0, width), center)
        matrix_to(out, at["kern_down"] + row_tap * 2 * width, product)

    def taps_rows(first, count):
        return kern_down[first * C1 : (first + count) * C1, :]

    moved = wide_rows(wide_grad, 0, C2, 2 * C2)
    below = wide_rows(wide_grad, 1, 0, C2)
    below_moved = wide_rows(wide_grad, 1, C2, 2 * C2)
    first_pair = mm_nt(center, taps_rows(4, 2))
    second_pair = mm_nt(center, taps_rows(7, 2)) + mm_nt(below, taps_rows(1, 2))
    grads = (
        first_pair[:, :C1],
        first_pair[:, C1:] + mm_nt(moved, taps_rows(3, 1)),
        second_pair[:, :C1],
        second_pair[:, C1:] + mm_nt(moved, taps_rows(6, 1)) + mm_nt(below_moved, taps_rows(0, 1)),
    )
    bias_in = jnp.zeros((8, C1), f32)
    for phase in range(4):
        low_grad[phase] = (skip[phase] + grads[phase]).astype(bf16)
        bias_in = bias_in + fold(low_grad[phase].astype(f32))
    vector_to(out, at["bias_in"], jnp.sum(bias_in, axis=0, keepdims=True))
    kern_in = None
    for phase in range(4):
        part = mm(taps[:, phase * ROWS : (phase + 1) * ROWS].astype(bf16), low_grad[phase])
        kern_in = part if kern_in is None else kern_in + part
    for tap in range(9):
        out[3 * tap : 3 * tap + 3, :] = kern_in[8 * tap : 8 * tap + 3, :]
    out[at["end"] :, :] = jnp.zeros((STEM_ROWS - at["end"], LANES), f32)
    narrow_out(out, me[0], sent, leaving)


def res_forward(
    places, me, gathered, down, embed,
    inner, res_out, act_one, act_two, kern_first, kern_second, dense_two, hidden_pre, stats, gains,
    stage, dense_one, wide,
):
    at = RES_AT
    widen(gathered, places, me[0], stage)
    matrix_from(stage, at["dense_one"], dense_one, TDIM, TEMB)
    matrix_from(stage, at["dense_two"], dense_two, TEMB, C2)
    matrix_from(stage, at["kern_first"], kern_first, 9 * C2, C2)
    matrix_from(stage, at["kern_second"], kern_second, 9 * C2, C2)
    pre = jnp.dot(embed[...], dense_one[...].astype(f32), precision=highest) + vector_at(stage, at["bias_one"], TEMB)
    hidden_pre[...] = pre
    hidden = pre * logistic(pre)
    time_proj = jnp.dot(hidden, dense_two[...].astype(f32), precision=highest) + vector_at(stage, at["bias_two"], C2)
    ones = same_group(C2)
    clear_edges(wide)
    gain = vector_at(stage, at["gain_first"], C2)
    shift = vector_at(stage, at["shift_first"], C2)
    gain_two = vector_at(stage, at["gain_second"], C2)
    shift_two = vector_at(stage, at["shift_second"], C2)
    gains[...] = jnp.concatenate([gain, shift, gain_two, shift_two, jnp.zeros((4, C2), f32)], axis=0)

    def normalize(source, place, gain, shift, keep):
        center, scale = norm_stats(lambda phase, row: source[pl.ds(row, 64), :], 1, C2, ones)
        stats[place : place + IMGS, :] = center
        stats[place + IMGS : place + 2 * IMGS, :] = scale

        def body(phase, image, inside, row):
            value = (source[pl.ds(row, 64), :] - center[image : image + 1, :]) * scale[image : image + 1, :]
            value = value * gain + shift
            value = value * logistic(value)
            keep[pl.ds(row, 64), :] = value.astype(bf16)
            put_shifted(wide, image, inside, value.astype(bf16).astype(f32))

        each_chunk(body)

    normalize(down, 0, gain, shift, act_one)
    bias = vector_at(stage, at["bias_first"], C2)
    product = conv_low(wide, kern_first)
    for image in range(IMGS):
        inner[image * LOW : (image + 1) * LOW, :] = (
            product[image * LOW : (image + 1) * LOW, :] + bias + time_proj[image : image + 1, :]
        )
    normalize(inner, 2 * IMGS, gain_two, shift_two, act_two)
    res_out[...] = down[...] + conv_low(wide, kern_second) + vector_at(stage, at["bias_second"], C2)


def norm_back(load_grad, source, center, scale, gain, shift, ones, active, store):
    def pieces(image, row):
        xhat = (source[pl.ds(row, 64), :] - center[image : image + 1, :]) * scale[image : image + 1, :]
        grad = load_grad(row)
        if active:
            value = xhat * gain + shift
            gate = logistic(value)
            grad = grad * (gate * (1.0 + value * (1.0 - gate)))
        return grad, xhat

    def load(phase, image, row):
        grad, xhat = pieces(image, row)
        return grad, grad * xhat

    gain_grad, shift_grad, mean_one, mean_two = norm_back_stats(load, 1, C2, gain, ones)

    def body(phase, image, inside, row):
        grad, xhat = pieces(image, row)
        store(
            image,
            inside,
            row,
            scale[image : image + 1, :]
            * (grad * gain - mean_one[image : image + 1, :] - xhat * mean_two[image : image + 1, :]),
        )

    each_chunk(body)
    return gain_grad, shift_grad


def res_backward(
    leaving, me, grad_res, down, inner, act_one, act_two, kern_first, kern_second, dense_two, hidden_pre, stats, gains, embed,
    grad_down, sent, out,
    wide, grad_act,
):
    at = RES_AT
    ones = same_group(C2)
    clear_edges(wide)

    def lower(phase, image, inside, row):
        put_shifted(wide, image, inside, grad_res[pl.ds(row, 64), :].astype(bf16).astype(f32))

    each_chunk(lower)
    sums = image_sums(
        lambda phase, image, row: (grad_res[pl.ds(row, 64), :].astype(bf16).astype(f32),), 1, C2
    )[0]
    vector_to(out, at["bias_second"], jnp.sum(sums, axis=0, keepdims=True))
    grad_act[...] = conv_low_back(wide, kern_second)
    conv_low_grad(act_two, wide, out, at["kern_second"])

    def store_inner(image, inside, row, value):
        put_shifted(wide, image, inside, value.astype(bf16).astype(f32))

    gain_grad, shift_grad = norm_back(
        lambda row: grad_act[pl.ds(row, 64), :], inner, stats[8:12, :], stats[12:16, :],
        gains[2:3, :], gains[3:4, :], ones, True, store_inner,
    )
    vector_to(out, at["gain_second"], gain_grad)
    vector_to(out, at["shift_second"], shift_grad)
    inner_sum = jnp.concatenate(
        [
            jnp.sum(fold(wide[image, PAD : PAD + LOW, C2 : 2 * C2].astype(f32)), axis=0, keepdims=True)
            for image in range(IMGS)
        ]
        + [jnp.zeros((4, C2), f32)],
        axis=0,
    )
    time_sum = jnp.sum(inner_sum, axis=0, keepdims=True)
    vector_to(out, at["bias_first"], time_sum)
    vector_to(out, at["bias_two"], time_sum)
    pre = hidden_pre[...]
    gate = logistic(pre)
    contract = (((0,), (0,)), ((), ()))
    matrix_to(
        out, at["dense_two"],
        lax.dot_general(pre * gate, inner_sum, contract, precision=highest, preferred_element_type=f32),
    )
    grad_pre = lax.dot_general(
        inner_sum, dense_two[...].astype(f32), (((1,), (1,)), ((), ())), precision=highest, preferred_element_type=f32
    ) * (gate * (1.0 + pre * (1.0 - gate)))
    vector_to(out, at["bias_one"], jnp.sum(grad_pre, axis=0, keepdims=True))
    matrix_to(
        out, at["dense_one"],
        lax.dot_general(embed[...], grad_pre, contract, precision=highest, preferred_element_type=f32),
    )
    grad_act[...] = conv_low_back(wide, kern_first)
    conv_low_grad(act_one, wide, out, at["kern_first"])

    def store_down(image, inside, row, value):
        grad_down[pl.ds(row, 64), :] = value + grad_res[pl.ds(row, 64), :]

    gain_grad, shift_grad = norm_back(
        lambda row: grad_act[pl.ds(row, 64), :], down, stats[0:4, :], stats[4:8, :],
        gains[0:1, :], gains[1:2, :], ones, True, store_down,
    )
    vector_to(out, at["gain_first"], gain_grad)
    vector_to(out, at["shift_first"], shift_grad)
    out[at["end"] :, :] = jnp.zeros((RES_ROWS - at["end"], LANES), f32)
    narrow_out(out, me[0], sent, leaving)


def attn_forward(
    places, me, gathered, res_out,
    attn_low, normed, qkv, probs, mixed, kern_qkv, kern_proj, stats, gains,
    stage,
):
    at = ATTN_AT
    widen(gathered, places, me[0], stage)
    matrix_from(stage, at["kern_qkv"], kern_qkv, C2, 3 * C2)
    matrix_from(stage, at["kern_proj"], kern_proj, C2, C2)
    ones = same_group(C2)
    gain = vector_at(stage, at["gain_attn"], C2)
    shift = vector_at(stage, at["shift_attn"], C2)
    gains[...] = jnp.concatenate([gain, shift, jnp.zeros((6, C2), f32)], axis=0)
    center, scale = norm_stats(lambda phase, row: res_out[pl.ds(row, 64), :], 1, C2, ones)
    stats[0:IMGS, :] = center
    stats[IMGS : 2 * IMGS, :] = scale

    def body(phase, image, inside, row):
        value = (res_out[pl.ds(row, 64), :] - center[image : image + 1, :]) * scale[image : image + 1, :]
        normed[pl.ds(row, 64), :] = (value * gain + shift).astype(bf16)

    each_chunk(body)
    qkv[...] = mm(normed[...], kern_qkv[...]).astype(bf16)
    for image in range(IMGS):
        rows = slice(image * LOW, (image + 1) * LOW)
        logits = mm_nt(qkv[rows, 0:C2], qkv[rows, C2 : 2 * C2]) * C2 ** (-0.5)
        powers = jnp.exp(logits - jnp.max(logits, axis=1, keepdims=True))
        weights = powers / jnp.sum(powers, axis=1, keepdims=True)
        probs[image] = weights
        mixed[rows, :] = mm(weights.astype(bf16), qkv[rows, 2 * C2 : 3 * C2]).astype(bf16)
    attn_low[...] = (
        res_out[...] + mm(mixed[...], kern_proj[...]) + vector_at(stage, at["bias_proj"], C2)
    ).astype(bf16)


def attn_backward(
    leaving, me, grad_attn, res_out, normed, qkv, probs, mixed, kern_qkv, kern_proj, stats, gains,
    grad_res, sent, out,
    grad_qkv, grad_mixed, grad_normed, low,
):
    at = ATTN_AT
    ones = same_group(C2)
    low[...] = grad_attn[...].astype(bf16)
    sums = image_sums(lambda phase, image, row: (grad_attn[pl.ds(row, 64), :],), 1, C2)[0]
    vector_to(out, at["bias_proj"], jnp.sum(sums, axis=0, keepdims=True))
    matrix_to(out, at["kern_proj"], mm_tn(mixed[...], low[...]))
    grad_mixed[...] = mm_nt(low[...], kern_proj[...]).astype(bf16)
    scale_by = C2 ** (-0.5)
    for image in range(IMGS):
        rows = slice(image * LOW, (image + 1) * LOW)
        query, keys, value = (qkv[rows, part * C2 : (part + 1) * C2] for part in range(3))
        weights = probs[image]
        grad_probs = mm_nt(grad_mixed[rows, :], value)
        grad_qkv[rows, 2 * C2 : 3 * C2] = mm_tn(weights.astype(bf16), grad_mixed[rows, :]).astype(bf16)
        grad_logits = (
            weights * (grad_probs - jnp.sum(weights * grad_probs, axis=1, keepdims=True))
        ).astype(bf16)
        grad_qkv[rows, 0:C2] = (mm(grad_logits, keys) * scale_by).astype(bf16)
        grad_qkv[rows, C2 : 2 * C2] = (mm_tn(grad_logits, query) * scale_by).astype(bf16)
    matrix_to(out, at["kern_qkv"], mm_tn(normed[...], grad_qkv[...]))
    grad_normed[...] = mm_nt(grad_qkv[...], kern_qkv[...])

    def store(image, inside, row, value):
        grad_res[pl.ds(row, 64), :] = value + grad_attn[pl.ds(row, 64), :]

    gain_grad, shift_grad = norm_back(
        lambda row: grad_normed[pl.ds(row, 64), :], res_out, stats[0:4, :], stats[4:8, :],
        gains[0:1, :], gains[1:2, :], ones, False, store,
    )
    vector_to(out, at["gain_attn"], gain_grad)
    vector_to(out, at["shift_attn"], shift_grad)
    out[at["end"] :, :] = jnp.zeros((ATTN_ROWS - at["end"], LANES), f32)
    narrow_out(out, me[0], sent, leaving)


def pick(row, channel):
    lane = lax.broadcasted_iota(jnp.int32, (LANES, LANES), 0)
    ch = lax.broadcasted_iota(jnp.int32, (LANES, LANES), 1)
    return (row * LANES + lane == CIN * ch + channel).astype(f32).astype(bf16)


def head_step(
    places, leaving, me, gathered, attn_low, top, clean, factor,
    grad_attn, skip, loss, sent, out,
    stage, wide, kern_up, merged, act, taps, narrow, grad_wide_zero, grad_wide_one, boxes,
):
    at = HEAD_AT
    widen(gathered, places, me[0], stage)
    ones = same_group(C1)
    kern_up[...] = jnp.zeros(kern_up.shape, bf16)

    def combine(at_row):
        tap = [[stage[pl.ds((3 * a + b) * C2 + at_row, 64), :] for b in range(3)] for a in range(3)]
        by_row = {(0, 0): tap[0], (0, 1): [tap[1][b] + tap[2][b] for b in range(3)],
                  (1, 0): [tap[0][b] + tap[1][b] for b in range(3)], (1, 1): tap[2]}
        for (row_phase, slot), three in by_row.items():
            for col_off in range(3):
                base = (slot * 3 + col_off) * C2
                here = pl.ds(base + at_row, 64)
                if col_off == 0:
                    kern_up[row_phase, here, 0:C1] = three[0].astype(bf16)
                elif col_off == 1:
                    kern_up[row_phase, here, 0:C1] = (three[1] + three[2]).astype(bf16)
                    kern_up[row_phase, here, C1 : 2 * C1] = (three[0] + three[1]).astype(bf16)
                else:
                    kern_up[row_phase, here, C1 : 2 * C1] = three[2].astype(bf16)

    chunks(C2, 64, combine)
    clear_edges(wide)

    def spread_low(phase, image, inside, row):
        put_shifted(wide, image, inside, attn_low[pl.ds(row, 64), :].astype(f32))

    each_chunk(spread_low)
    bias_up = stage[at["bias_up"] : at["bias_up"] + 1, :]
    for row_phase in range(2):
        product = mm(
            jnp.concatenate(
                [wide_rows(wide, row_phase - 1, 0, 3 * C2), wide_rows(wide, row_phase, 0, 3 * C2)], axis=1
            ),
            kern_up[row_phase],
        )
        for col_phase in range(2):
            phase = row_phase * 2 + col_phase
            merged[phase] = product[:, col_phase * C1 : (col_phase + 1) * C1] + bias_up + top[phase]
    gain = stage[at["gain_out"] : at["gain_out"] + 1, :]
    shift = stage[at["shift_out"] : at["shift_out"] + 1, :]
    center, scale = norm_stats(lambda phase, row: merged[phase, pl.ds(row, 64), :], 4, C1, ones)

    def body(phase, image, inside, row):
        value = (merged[phase, pl.ds(row, 64), :] - center[image : image + 1, :]) * scale[image : image + 1, :]
        value = value * gain + shift
        act[phase, pl.ds(row, 64), :] = (value * logistic(value)).astype(bf16)

    each_chunk(body, 4)
    for channel in range(CIN):
        total = None
        for row in range(3):
            part = mm(stage[pl.ds(at["kern_out"] + row, 9, 3), :].astype(bf16), pick(row, channel))
            total = part if total is None else total + part
        narrow[pl.ds(channel, 9, 8), :] = total
    for channel in range(CIN, 8):
        narrow[pl.ds(channel, 9, 8), :] = jnp.zeros((9, LANES), f32)
    kern_out = narrow[...].astype(bf16)
    masks = lane_masks(ROWS)
    for phase in range(4):
        taps[:, phase * ROWS : (phase + 1) * ROWS] = mm_nt(kern_out, act[phase])
    lane = lax.broadcasted_iota(jnp.int32, (8, LANES), 1)
    channel_at = lax.broadcasted_iota(jnp.int32, (8, LANES), 0)
    bias_out = jnp.sum(
        jnp.where((lane == channel_at) & (channel_at < CIN), stage[at["bias_out"] : at["bias_out"] + 1, :], 0.0),
        axis=1,
        keepdims=True,
    )
    pixel_count = CIN * SIDE * SIDE
    loss_sum = jnp.zeros((8, ROWS), f32)
    bias_grad = jnp.zeros((8, 1), f32)
    grad_lanes = []
    for phase in range(4):
        predict = bias_out
        for tap, off in enumerate(TAPS):
            other, row_off, col_off = tap_source(phase, off)
            predict = predict + lane_shift(
                taps[8 * tap : 8 * tap + 8, other * ROWS : (other + 1) * ROWS], row_off, col_off, masks
            )
        error = predict - clean[:, phase * ROWS : (phase + 1) * ROWS]
        loss_sum = loss_sum + error * error * factor[...]
        grad = ((2.0 / pixel_count) * factor[...] * error).astype(bf16).astype(f32)
        bias_grad = bias_grad + jnp.sum(grad, axis=1, keepdims=True)
        grad_lanes.append(grad)
    loss[...] = jnp.sum(jnp.sum(loss_sum, axis=1, keepdims=True), axis=0, keepdims=True) * (1.0 / pixel_count)
    out[at["bias_out"] : at["bias_out"] + 1, :] = jnp.sum(
        jnp.where((lane == channel_at) & (channel_at < CIN), bias_grad, 0.0), axis=0, keepdims=True
    )
    for phase in range(4):
        for tap, off in enumerate(TAPS):
            other, row_off, col_off = tap_source(phase, (-off[0], -off[1]))
            taps[8 * tap : 8 * tap + 8, phase * ROWS : (phase + 1) * ROWS] = lane_shift(
                grad_lanes[other], row_off, col_off, masks
            )
    kern_grad = None
    for phase in range(4):
        low = taps[:, phase * ROWS : (phase + 1) * ROWS].astype(bf16)
        part = mm(low, act[phase])
        kern_grad = part if kern_grad is None else kern_grad + part
        skip[phase] = mm_tn(low, kern_out)
    narrow[...] = kern_grad
    for row in range(3):
        total = None
        for channel in range(CIN):
            pieces = parts_of(narrow[pl.ds(channel, 9, 8), :])
            part = sum(mm_nt(piece, pick(row, channel)) for piece in pieces)
            total = part if total is None else total + part
        out[pl.ds(at["kern_out"] + row, 9, 3), :] = total

    def pieces(phase, image, row):
        xhat = (merged[phase, pl.ds(row, 64), :] - center[image : image + 1, :]) * scale[image : image + 1, :]
        value = xhat * gain + shift
        gate = logistic(value)
        return skip[phase, pl.ds(row, 64), :] * (gate * (1.0 + value * (1.0 - gate))), xhat

    def load(phase, image, row):
        grad, xhat = pieces(phase, image, row)
        return grad, grad * xhat

    gain_grad, shift_grad, mean_one, mean_two = norm_back_stats(load, 4, C1, gain, ones)
    vector_to(out, at["gain_out"], gain_grad)
    vector_to(out, at["shift_out"], shift_grad)
    clear_edges(grad_wide_zero)
    clear_edges(grad_wide_one)
    clear_edges(boxes)
    wides = (grad_wide_zero, grad_wide_one)

    def back(phase, image, inside, row):
        for row_phase in range(2):
            pair = []
            for col_phase in range(2):
                phase = row_phase * 2 + col_phase
                grad, xhat = pieces(phase, image, row)
                value = scale[image : image + 1, :] * (
                    grad * gain - mean_one[image : image + 1, :] - xhat * mean_two[image : image + 1, :]
                )
                skip[phase, pl.ds(row, 64), :] = value
                pair.append(value.astype(bf16).astype(f32))
            put_shifted(wides[row_phase], image, inside, jnp.concatenate(pair, axis=1))
            here = pl.ds(PAD + inside, 64)
            base = row_phase * 3 * C1
            boxes[image, here, base : base + C1] = pair[1] + row_shift(pair[0], 1)
            boxes[image, here, base + C1 : base + 2 * C1] = pair[0] + pair[1]
            boxes[image, here, base + 2 * C1 : base + 3 * C1] = row_shift(pair[1], -1) + pair[0]

    each_chunk(back)
    bias_sum = jnp.zeros((8, C1), f32)
    for row_phase in range(2):
        for image in range(IMGS):
            both = fold(wides[row_phase][image, PAD : PAD + LOW, C2 : 2 * C2].astype(f32))
            bias_sum = bias_sum + both[:, :C1] + both[:, C1:]
    vector_to(out, at["bias_up"], jnp.sum(bias_sum, axis=0, keepdims=True))
    total = None
    for row_phase in range(2):
        for slot in range(2):
            base = slot * 3 * C2
            taps = [kern_up[row_phase, base + at * C2 : base + (at + 1) * C2, :] for at in (2, 1, 0)]
            part = mm_nt(wide_rows(wides[row_phase], 1 - row_phase - slot, 0, 3 * C2), jnp.concatenate(taps, axis=1))
            total = part if total is None else total + part
    grad_attn[...] = total
    width = 3 * C1

    def box_rows(row_off, row_phase):
        return boxes[
            :, PAD + 16 * row_off : PAD + 16 * row_off + LOW, row_phase * width : (row_phase + 1) * width
        ].reshape(ROWS, width)

    summed = (
        box_rows(0, 1) + box_rows(1, 0),
        box_rows(0, 0) + box_rows(0, 1),
        box_rows(-1, 1) + box_rows(0, 0),
    )
    for row_tap in range(3):
        product = mm_tn(attn_low[...], summed[row_tap].astype(bf16))
        for col_tap in range(3):
            tap = row_tap * 3 + col_tap
            out[tap * C2 : (tap + 1) * C2, :] = product[:, col_tap * C1 : (col_tap + 1) * C1]
    out[at["end"] :, :] = jnp.zeros((HEAD_ROWS - at["end"], LANES), f32)
    narrow_out(out, me[0], sent, leaving)


def sds(shape, dtype=f32):
    return jax.ShapeDtypeStruct(shape, dtype)


def run(body, ins, outs, scratch):
    in_leaves, in_tree = jax.tree.flatten(ins)
    out_leaves, out_tree = jax.tree.flatten(outs)

    def kernel(*refs):
        split = len(in_leaves), len(in_leaves) + len(out_leaves)
        body(
            *jax.tree.unflatten(in_tree, refs[: split[0]]),
            *jax.tree.unflatten(out_tree, refs[split[0] : split[1]]),
            *refs[split[1] :],
        )

    whole = pl.BlockSpec(memory_space=pltpu.VMEM)
    results = pl.pallas_call(
        kernel,
        out_shape=out_leaves,
        in_specs=[pl.BlockSpec(memory_space=pltpu.SMEM)] + [whole] * (len(in_leaves) - 1),
        out_specs=[whole] * len(out_leaves),
        scratch_shapes=scratch,
        compiler_params=pltpu.CompilerParams(vmem_limit_bytes=62 * 2**20),
    )(*in_leaves)
    return jax.tree.unflatten(out_tree, results)


def wide_scratch(width, dtype=bf16):
    return pltpu.VMEM((IMGS, PADDED, width), dtype)


SAVED = dict(
    stage=((RES_ROWS, LANES), f32), block_out=((HEAD_ROWS, LANES), f32),
    taps=((72, 4 * ROWS), f32), low_taps=((72, 4 * ROWS), f32), narrow=((72, LANES), f32),
    top=((4, ROWS, C1), f32), down=((ROWS, C2), f32), inner=((ROWS, C2), f32), res_out=((ROWS, C2), f32),
    act_one=((ROWS, C2), bf16), act_two=((ROWS, C2), bf16), attn_low=((ROWS, C2), bf16), normed=((ROWS, C2), bf16),
    qkv=((ROWS, 3 * C2), bf16), probs=((IMGS, LOW, LOW), f32), mixed=((ROWS, C2), bf16),
    merged=((4, ROWS, C1), f32), act=((4, ROWS, C1), bf16), skip=((4, ROWS, C1), f32),
    grad_attn=((ROWS, C2), f32), grad_res=((ROWS, C2), f32), grad_act=((ROWS, C2), f32),
    grad_low=((ROWS, C2), bf16), grad_mixed=((ROWS, C2), bf16), grad_qkv=((ROWS, 3 * C2), bf16),
    dense_one=((TDIM, TEMB), bf16), dense_two=((TEMB, C2), bf16), kern_down=((9 * C1, C2), bf16),
    kern_first=((9 * C2, C2), bf16), kern_second=((9 * C2, C2), bf16), kern_qkv=((C2, 3 * C2), bf16),
    kern_proj=((C2, C2), bf16), kern_up=((2, 6 * C2, C2), bf16),
    hidden_pre=((8, TEMB), f32), res_stats=((16, C2), f32), res_gains=((8, C2), f32),
    attn_stats=((8, C2), f32), attn_gains=((8, C2), f32),
    wide=((IMGS, PADDED, 3 * C2), bf16), wide_zero=((IMGS, PADDED, 3 * C2), bf16),
    wide_one=((IMGS, PADDED, 3 * C2), bf16), boxes=((IMGS, PADDED, 6 * C1), f32),
)


class Named:
    def __init__(self, names, refs):
        self.__dict__.update(zip(names, refs))


def whole_step(places, leaving, me, gathered, noisy, clean, factor, embed, loss, sent, *refs):
    own = Named(SAVED, refs)
    stem_wide, stem_wide_zero = own.wide.at[:, :, 0 : 3 * C1], own.wide_zero.at[:, :, 0 : 3 * C1]
    stem_forward(
        places[0], me, gathered[0], noisy, own.top, own.down, own.kern_down, own.stage, own.taps, stem_wide, stem_wide_zero
    )
    res_forward(
        places[1], me, gathered[1], own.down, embed,
        own.inner, own.res_out, own.act_one, own.act_two, own.kern_first, own.kern_second, own.dense_two,
        own.hidden_pre, own.res_stats, own.res_gains,
        own.stage, own.dense_one, own.wide,
    )
    attn_forward(
        places[2], me, gathered[2], own.res_out,
        own.attn_low, own.normed, own.qkv, own.probs, own.mixed, own.kern_qkv, own.kern_proj,
        own.attn_stats, own.attn_gains,
        own.stage,
    )
    head_step(
        places[3], leaving[3], me, gathered[3], own.attn_low, own.top, clean, factor,
        own.grad_attn, own.skip, loss, sent[3], own.block_out,
        own.stage, own.wide, own.kern_up, own.merged, own.act, own.low_taps, own.narrow,
        own.wide_zero, own.wide_one, own.boxes,
    )
    attn_backward(
        leaving[2], me, own.grad_attn, own.res_out, own.normed, own.qkv, own.probs, own.mixed,
        own.kern_qkv, own.kern_proj, own.attn_stats, own.attn_gains,
        own.grad_res, sent[2], own.block_out.at[0:ATTN_ROWS],
        own.grad_qkv, own.grad_mixed, own.grad_act, own.grad_low,
    )
    res_backward(
        leaving[1], me, own.grad_res, own.down, own.inner, own.act_one, own.act_two, own.kern_first, own.kern_second,
        own.dense_two, own.hidden_pre, own.res_stats, own.res_gains, embed,
        own.grad_attn, sent[1], own.stage,
        own.wide, own.grad_act,
    )
    stem_backward(
        leaving[0], me, noisy, own.top, own.skip, own.grad_attn, own.kern_down, sent[0], own.block_out,
        own.taps, stem_wide, stem_wide_zero, own.wide_one.at[:, :, 0 : 2 * C2], own.act,
    )


def local_step(me, arrays, places, shapes, out_places, noisy, clean, factor, embed):
    def body(me, arrays, noisy, clean, factor, embed, loss, sent, *refs):
        gathered = [[arrays[place[0]] for place in block] for block in places]
        leaving = [[sent[place[0]] for place in block] for block in out_places]
        rest = [[place[1:] for place in block] for block in places]
        out_rest = [[place[1:] for place in block] for block in out_places]
        whole_step(rest, out_rest, me, gathered, noisy, clean, factor, embed, loss, leaving, *refs)

    return run(
        body,
        [me, arrays, noisy, clean, factor, embed],
        [sds((1, 1)), shapes],
        [pltpu.VMEM(shape, dtype) for shape, dtype in SAVED.values()],
    )


def plan(step_counts, time_index, teacher_size):
    position = time_index % step_counts
    time_values = (2 * position + teacher_size).astype(f32) / (2 * step_counts).astype(f32)
    alpha_t = jnp.cos(0.5 * math.pi * time_values)
    sigma_t = jnp.sin(0.5 * math.pi * time_values)
    weight = jnp.maximum(alpha_t * alpha_t / (sigma_t * sigma_t), 1.0)
    return (time_values, alpha_t, sigma_t, weight)


def sinusoid(time_values):
    half_dim = TDIM // 2
    frequency = jnp.exp(-math.log(10000.0) * jnp.arange(half_dim, dtype=f32) / half_dim)
    angles = 1000.0 * time_values[:, None] * frequency[None, :]
    return jnp.concatenate([jnp.sin(angles), jnp.cos(angles)], axis=1)


def by_phase(images):
    split = images.reshape(IMGS, CIN, 16, 2, 16, 2).transpose(1, 3, 5, 0, 2, 4).reshape(CIN, 4 * ROWS)
    return jnp.pad(split, ((0, 8 - CIN), (0, 0)))


def prepare(clean_images, noise_field, step_counts, time_index, teacher_size, image_count):
    slot_count = clean_images.shape[0]
    time_values, alpha_t, sigma_t, weight = plan(step_counts, time_index, teacher_size)
    live_mask = (jnp.arange(slot_count, dtype=jnp.int32) < image_count).astype(f32)
    factor = live_mask * weight
    noisy = (alpha_t[:, None, None] * clean_images + sigma_t[:, None, None] * noise_field).astype(bf16).astype(f32)
    embed = jnp.pad(sinusoid(time_values), ((0, 8 - IMGS), (0, 0)))
    factor_lanes = jnp.repeat(factor, LOW)[None, :]
    return by_phase(noisy), by_phase(clean_images), factor_lanes, embed


AXES = ("dp", "fsdp")
BLOCK_ROWS = (STEM_ROWS, RES_ROWS, ATTN_ROWS, HEAD_ROWS)
SHARD_ROWS = (80, 344, 72, 80)
SPAN = 32
HALVES = (
    (((0, 0, 80), (1, 0, 200)), (2, 4)),
    (((1, 200, 344), (3, 0, 80), (2, 0, 72)), (4, 2)),
)
HALF_ROWS = tuple(sum(hi - lo for _, lo, hi in members) for members, _ in HALVES)
LINE = (0, 8, 16, 24)


def swap(values, mask):
    return lax.ppermute(values, AXES, [(here, here ^ mask) for here in range(SPAN)])


def half_places(number, array, masks):
    at, found = 0, []
    for block, lo, hi in HALVES[number][0]:
        found.append((block, (array, masks, at, at + hi - lo, SHARD_ROWS[block], lo)))
        at += hi - lo
    return found


def gather_halves(shards):
    own = jnp.concatenate(
        [shards[block][lo:hi] for members, _ in HALVES for block, lo, hi in members], axis=0
    )
    line = [own] + [swap(own, mask) for mask in LINE[1:]]
    arrays, places = [], [[] for _ in shards]

    def add(number, array, masks):
        for block, place in half_places(number, len(arrays), masks):
            places[block].append(place)
        arrays.append(array)

    held = []
    for number, (_, (last, first)) in enumerate(HALVES):
        begin = number * HALF_ROWS[0]
        near = jnp.stack([piece[begin : begin + HALF_ROWS[number]] for piece in line], axis=0)
        held.append(jnp.concatenate([near, swap(near, first)], axis=0))
    for number, (_, (last, first)) in enumerate(HALVES):
        masks = [a ^ b for a in (0, first) for b in LINE]
        far = swap(held[number], last)
        add(number, held[number], masks)
        add(number, far, [mask ^ last for mask in masks])
        add(number, swap(held[number], 1), [mask ^ 1 for mask in masks])
        add(number, swap(far, 1), [mask ^ last ^ 1 for mask in masks])
    return arrays, places


def leaving_halves():
    shapes, places = [], [[] for _ in SHARD_ROWS]
    for number, (_, (first, last)) in enumerate(HALVES):
        for core in (0, 1):
            for side in (0, first):
                masks = [core ^ side ^ a ^ b for a in (0, last) for b in LINE]
                for block, place in half_places(number, len(shapes), masks):
                    places[block].append(place)
                shapes.append(sds((8, HALF_ROWS[number], LANES), bf16))
    return shapes, places


def reduce_halves(leaving):
    totals = []
    crossed = [[None, None], [None, None]]
    for side in (1, 0):
        for number in (0, 1):
            kept, sent = leaving[4 * number + side], leaving[4 * number + 2 + side]
            crossed[number][side] = kept.astype(f32) + swap(sent, 1).astype(f32)
    for number, (_, (first, last)) in enumerate(HALVES):
        near, far = crossed[number]
        totals.append(near + swap(far.astype(bf16), first).astype(f32))
    for number, (_, (first, last)) in enumerate(HALVES):
        total = totals[number]
        totals[number] = total[:4] + swap(total[4:].astype(bf16), last).astype(f32)
    whole = jnp.concatenate(totals, axis=1)
    result = whole[0]
    for number, mask in enumerate(LINE[1:]):
        result = result + swap(whole[number + 1].astype(bf16), mask).astype(f32)
    pieces, at = [[] for _ in SHARD_ROWS], 0
    for members, _ in HALVES:
        for block, lo, hi in members:
            pieces[block].append(result[at : at + hi - lo])
            at += hi - lo
    return [jnp.concatenate(piece, axis=0).reshape(-1) for piece in pieces]


def gather_whole(shards):
    arrays = [
        lax.all_gather(shard.reshape(-1), AXES, axis=0, tiled=True).reshape(1, rows, LANES)
        for shard, rows in zip(shards, BLOCK_ROWS)
    ]
    return arrays, [[(block, (0,), 0, rows, 0, 0)] for block, rows in enumerate(BLOCK_ROWS)]


def leaving_whole():
    shapes = [sds((1, rows, LANES), bf16) for rows in BLOCK_ROWS]
    return shapes, [[(block, (0,), 0, rows, 0, 0)] for block, rows in enumerate(BLOCK_ROWS)]


def reduce_whole(leaving):
    return [
        lax.psum_scatter(array.astype(f32).reshape(-1), AXES, scatter_dimension=0, tiled=True) for array in leaving
    ]


def scalar_sums(values):
    count = lax.axis_size(AXES)
    row = jnp.concatenate([value.reshape(1) for value in values] + [jnp.zeros((LANES - len(values),), f32)])
    sent = jnp.broadcast_to(row[None, None, :], (count, 1, LANES))
    arrived = lax.all_to_all(sent, AXES, 0, 0, tiled=True)
    total = jnp.sum(arrived, axis=(0, 1))
    return [total[at] for at in range(len(values))]


def adam_update(master, first, second, gradient, step_value):
    first_new = beta_one * first + (1.0 - beta_one) * gradient
    second_new = beta_two * second + (1.0 - beta_two) * gradient * gradient
    fix_one = 1.0 - jnp.power(jnp.float32(beta_one), step_value)
    fix_two = 1.0 - jnp.power(jnp.float32(beta_two), step_value)
    master_new = master - learn_rate * (
        first_new / fix_one / (jnp.sqrt(second_new / fix_two) + adam_eps) + decay_rate * master
    )
    return (master_new, first_new, second_new, master_new.astype(bf16))


def per_device(
    clean_images, noise_field, step_counts, time_index, teacher_size, image_counts, adam_step,
    stem_master, stem_first, stem_second, res_master, res_first, res_second,
    attn_master, attn_first, attn_second, head_master, head_first, head_second,
):
    masters = (stem_master, res_master, attn_master, head_master)
    firsts = (stem_first, res_first, attn_first, head_first)
    seconds = (stem_second, res_second, attn_second, head_second)
    me = lax.axis_index(AXES).astype(jnp.int32).reshape(1)
    shards = [master.astype(bf16).reshape(-1, LANES) for master in masters]
    laid_out = lax.axis_size(AXES) == SPAN and tuple(shard.shape[0] for shard in shards) == SHARD_ROWS
    arrays, places = gather_halves(shards) if laid_out else gather_whole(shards)
    shapes, out_places = leaving_halves() if laid_out else leaving_whole()
    noisy, clean, factor, embed = prepare(
        clean_images, noise_field, step_counts, time_index, teacher_size, image_counts[0]
    )
    loss_local, leaving = local_step(me, arrays, places, shapes, out_places, noisy, clean, factor, embed)
    shard_grads = reduce_halves(leaving) if laid_out else reduce_whole(leaving)
    sum_local = sum((jnp.sum(jnp.square(gradient)) for gradient in shard_grads))
    loss_sum, sum_sq, total_live = scalar_sums([loss_local, sum_local, image_counts[0].astype(f32)])
    loss_value = loss_sum / total_live
    grad_norm = jnp.sqrt(sum_sq) / total_live
    clip_scale = clip_limit / jnp.maximum(grad_norm, clip_limit) / total_live
    step_value = adam_step[0].astype(f32)
    results = [loss_value, grad_norm]
    for block_idx in range(4):
        results.extend(
            adam_update(
                masters[block_idx], firsts[block_idx], seconds[block_idx], shard_grads[block_idx] * clip_scale, step_value
            )
        )
    return tuple(results)


def solution(mesh):
    split = P(("dp", "fsdp"))
    images = P(("dp", "fsdp"), None, None)
    return jax.shard_map(
        per_device,
        mesh=mesh,
        in_specs=(images, images, split, split, split, split, P()) + (split,) * 12,
        out_specs=(P(), P()) + (split,) * 16,
        check_vma=False,
    )
```

```python
from functools import partial
import math

import jax
import jax.numpy as jnp
from jax import lax
from jax.experimental import pallas as pl
from jax.experimental.pallas import tpu as pltpu
from jax.sharding import PartitionSpec as P

C1 = 128
C2 = 256
GROUPS = 32
TDIM = 128
TEMB = 512
CIN = 3
SIDE = 32
LANES = 128
IMGS = 4
LOW = 256
ROWS = IMGS * LOW
PAD = 16
PADDED = LOW + 2 * PAD

clip_limit = 0.05
learn_rate = 0.05
beta_one = 0.9
beta_two = 0.999
adam_eps = 1e-08
decay_rate = 0.01
norm_eps = 1e-05

f32 = jnp.float32
bf16 = jnp.bfloat16
highest = lax.Precision.HIGHEST

STEM_ROWS, RES_ROWS, ATTN_ROWS, HEAD_ROWS = 2560, 11008, 2304, 2560

STEM_AT = dict(kern_in=0, bias_in=27, kern_down=28, bias_down=2332, end=2334)
RES_AT = dict(
    dense_one=0, bias_one=512, dense_two=516, bias_two=1540, gain_first=1542, shift_first=1544,
    kern_first=1546, bias_first=6154, gain_second=6156, shift_second=6158, kern_second=6160,
    bias_second=10768, end=10770,
)
ATTN_AT = dict(gain_attn=0, shift_attn=2, kern_qkv=4, kern_proj=1540, bias_proj=2052, end=2054)
HEAD_AT = dict(kern_up=0, bias_up=2304, gain_out=2305, shift_out=2306, kern_out=2307, bias_out=2334, end=2335)


def mm(a, b):
    return jnp.dot(a, b, preferred_element_type=f32)


def mm_nt(a, b):
    return lax.dot_general(a, b, (((1,), (1,)), ((), ())), preferred_element_type=f32)


def mm_tn(a, b):
    return lax.dot_general(a, b, (((0,), (0,)), ((), ())), preferred_element_type=f32)


def parts_of(values):
    high = values.astype(bf16)
    rest = values - high.astype(f32)
    middle = rest.astype(bf16)
    return high, middle, (rest - middle.astype(f32)).astype(bf16)


def mm_exact(values, matrix):
    return sum(mm(piece, matrix) for piece in parts_of(values))


def same_group(channels):
    size = channels // GROUPS
    down_at = lax.broadcasted_iota(jnp.int32, (channels, channels), 0) // size
    across = lax.broadcasted_iota(jnp.int32, (channels, channels), 1) // size
    return (down_at == across).astype(f32).astype(bf16)


def row_shift(values, step):
    count = values.shape[0]
    moved = pltpu.roll(values, (-step) % count, 0)
    column = lax.broadcasted_iota(jnp.int32, values.shape, 0) & 15
    return jnp.where(column == (0 if step < 0 else 15), 0.0, moved)


def chunks(total, size, body):
    def step(number, carry):
        body(pl.multiple_of(number * size, size))
        return carry

    lax.fori_loop(0, total // size, step, 0, unroll=True)


def widen(pieces, places, me, stage):
    for ref, (masks, lo, hi, per_shard, begin) in zip(pieces, places):
        for number, mask in enumerate(masks):
            owner = me ^ mask
            at = pl.multiple_of(owner * per_shard + begin, 8)
            stage[pl.ds(at, hi - lo), :] = ref[number, lo:hi, :].astype(f32)


def narrow_out(stage, me, outs, places):
    for ref, (masks, lo, hi, per_shard, begin) in zip(outs, places):
        for number, mask in enumerate(masks):
            owner = me ^ mask
            at = pl.multiple_of(owner * per_shard + begin, 8)
            ref[number, lo:hi, :] = stage[pl.ds(at, hi - lo), :].astype(ref.dtype)


def matrix_from(stage, base, out, depth, width):
    lanes = width // LANES

    def copy(at):
        for lane in range(lanes):
            out[pl.ds(at, 128), lane * LANES : (lane + 1) * LANES] = stage[
                pl.ds(base + lanes * at + lane, 128, lanes), :
            ].astype(bf16)

    chunks(depth, 128, copy)


def matrix_to(out, base, value):
    depth, width = value.shape
    lanes = width // LANES
    for lane in range(lanes):
        out[pl.ds(base + lane, depth, lanes), :] = value[:, lane * LANES : (lane + 1) * LANES]


def vector_at(stage, base, width):
    return jnp.concatenate([stage[base + lane : base + lane + 1, :] for lane in range(width // LANES)], axis=1)


def vector_to(out, base, value):
    for lane in range(value.shape[1] // LANES):
        out[base + lane : base + lane + 1, :] = value[:, lane * LANES : (lane + 1) * LANES]


def fold(values):
    return jnp.sum(values.reshape(values.shape[0] // 8, 8, values.shape[1]), axis=0)


def image_sums(load, phases, width):
    sums = []
    for image in range(IMGS):
        def step(number, carry):
            row = pl.multiple_of(image * LOW + number * 64, 64)
            for phase in range(phases):
                carry = tuple(c + fold(v) for c, v in zip(carry, load(phase, image, row)))
            return carry

        first = load(0, image, image * LOW)
        carry = lax.fori_loop(0, 4, step, tuple(jnp.zeros((8, width), f32) for _ in first), unroll=True)
        sums.append([jnp.sum(c, axis=0, keepdims=True) for c in carry])
    return [jnp.concatenate(list(group), axis=0) for group in zip(*sums)]


def norm_stats(load, phases, width, ones):
    count = LOW * phases * (width // GROUPS)
    (total,) = image_sums(lambda phase, image, row: (load(phase, row),), phases, width)
    center = mm_exact(total, ones) * (1.0 / count)

    def squares(phase, image, row):
        away = load(phase, row) - center[image : image + 1, :]
        return (away * away,)

    (total,) = image_sums(squares, phases, width)
    spread = mm_exact(total, ones) * (1.0 / count)
    return center, lax.rsqrt(spread + norm_eps)


def norm_back_stats(load, phases, width, gain, ones):
    count = LOW * phases * (width // GROUPS)
    shift_sum, gain_sum = image_sums(load, phases, width)
    means = mm_exact(jnp.concatenate([shift_sum * gain, gain_sum * gain], axis=0), ones) * (1.0 / count)
    return (
        jnp.sum(gain_sum, axis=0, keepdims=True),
        jnp.sum(shift_sum, axis=0, keepdims=True),
        means[:IMGS],
        means[IMGS:],
    )


def logistic(values):
    return 1.0 / (1.0 + jnp.exp(-values))


def each_chunk(body, phases=1, size=64):
    for image in range(IMGS):
        def step(number, carry):
            inside = pl.multiple_of(number * size, size)
            for phase in range(phases):
                body(phase, image, inside, image * LOW + inside)
            return carry

        lax.fori_loop(0, LOW // size, step, 0, unroll=True)


def clear_edges(wide):
    for image in range(IMGS):
        wide[image, 0:PAD, :] = jnp.zeros((PAD, wide.shape[2]), wide.dtype)
        wide[image, PAD + LOW : PADDED, :] = jnp.zeros((PAD, wide.shape[2]), wide.dtype)


def put_shifted(wide, image, inside, value):
    width = value.shape[1]
    at = pl.ds(PAD + inside, value.shape[0])
    wide[image, at, 0:width] = row_shift(value, -1).astype(bf16)
    wide[image, at, width : 2 * width] = value.astype(bf16)
    wide[image, at, 2 * width : 3 * width] = row_shift(value, 1).astype(bf16)


def wide_rows(wide, row_off, lo, hi):
    begin = PAD + 16 * row_off
    return wide[:, begin : begin + LOW, lo:hi].reshape(ROWS, hi - lo)


def conv_low(wide, kern):
    width = wide.shape[2]
    total = None
    for tap in range(3):
        part = mm(wide_rows(wide, tap - 1, 0, width), kern[tap * width : (tap + 1) * width, :])
        total = part if total is None else total + part
    return total


def conv_low_back(wide, kern):
    total = None
    for row_tap in range(3):
        taps = [kern[(row_tap * 3 + col_tap) * C2 : (row_tap * 3 + col_tap + 1) * C2, :] for col_tap in (2, 1, 0)]
        part = mm_nt(wide_rows(wide, 1 - row_tap, 0, 3 * C2), jnp.concatenate(taps, axis=1))
        total = part if total is None else total + part
    return total


def conv_low_grad(source, wide, out, base):
    for row_tap in range(3):
        product = mm_tn(source[...], wide_rows(wide, 1 - row_tap, 0, 3 * C2))
        for col_tap in range(3):
            tap = row_tap * 3 + col_tap
            matrix_to(out, base + tap * 2 * C2, product[:, (2 - col_tap) * C2 : (3 - col_tap) * C2])


def lane_masks(width):
    place = lax.broadcasted_iota(jnp.int32, (8, width), 1)
    row, column = (place >> 4) & 15, place & 15

    def valid(row_off, col_off):
        keep = None
        for at, off in ((row, row_off), (column, col_off)):
            if off:
                inside = at != (0 if off < 0 else 15)
                keep = inside if keep is None else keep & inside
        return keep

    return {(r, c): valid(r, c) for r in (-1, 0, 1) for c in (-1, 0, 1)}


def lane_shift(values, row_off, col_off, masks):
    step = 16 * row_off + col_off
    if step == 0:
        return values
    moved = pltpu.roll(values, (-step) % values.shape[1], 1)
    return jnp.where(masks[(row_off, col_off)], moved, 0.0)


def tap_source(phase, tap_off):
    row, col = phase // 2 + tap_off[0], phase % 2 + tap_off[1]
    return (row % 2) * 2 + col % 2, row // 2, col // 2


TAPS = tuple((row - 1, col - 1) for row in range(3) for col in range(3))


def taps_on_lanes(source, out, masks, sign):
    for phase in range(4):
        for tap, off in enumerate(TAPS):
            other, row_off, col_off = tap_source(phase, (sign * off[0], sign * off[1]))
            out[8 * tap : 8 * tap + 8, phase * ROWS : (phase + 1) * ROWS] = lane_shift(
                source[:, other * ROWS : (other + 1) * ROWS], row_off, col_off, masks
            )


def down_wide(load, wide_one, wide_zero):
    clear_edges(wide_one)

    def body(phase, image, inside, row):
        at = pl.ds(PAD + inside, 64)
        for wide, row_phase in ((wide_one, 1), (wide_zero, 0)):
            right = load(row_phase * 2 + 1, row)
            left = load(row_phase * 2, row)
            wide[image, at, 0:C1] = row_shift(right, -1).astype(bf16)
            wide[image, at, C1 : 2 * C1] = left.astype(bf16)
            wide[image, at, 2 * C1 : 3 * C1] = right.astype(bf16)

    each_chunk(body)


def stem_forward(places, me, gathered, noisy, top, down, kern_down, stage, taps, wide_one, wide_zero):
    at = STEM_AT
    widen(gathered, places, me[0], stage)
    matrix_from(stage, at["kern_down"], kern_down, 9 * C1, C2)
    masks = lane_masks(ROWS)
    taps_on_lanes(noisy, taps, masks, 1)
    kern_in = jnp.concatenate(
        [
            jnp.concatenate([stage[3 * tap : 3 * tap + 3, :], jnp.zeros((5, LANES), f32)], axis=0)
            for tap in range(9)
        ],
        axis=0,
    ).astype(bf16)
    bias_in = stage[at["bias_in"] : at["bias_in"] + 1, :]
    for phase in range(4):
        top[phase] = mm_tn(taps[:, phase * ROWS : (phase + 1) * ROWS].astype(bf16), kern_in) + bias_in
    down_wide(lambda phase, row: top[phase, pl.ds(row, 64), :], wide_one, wide_zero)
    width = 3 * C1
    source = jnp.concatenate(
        [wide_rows(wide_one, -1, 0, width), wide_rows(wide_zero, 0, 0, width), wide_rows(wide_one, 0, 0, width)],
        axis=1,
    )
    down[...] = mm(source, kern_down[...]) + vector_at(stage, at["bias_down"], C2)


def stem_backward(leaving, me, noisy, top, skip, grad_down, kern_down, sent, out, taps, wide_one, wide_zero, wide_grad, low_grad):
    at = STEM_AT
    taps_on_lanes(noisy, taps, lane_masks(ROWS), 1)
    down_wide(lambda phase, row: top[phase, pl.ds(row, 64), :], wide_one, wide_zero)
    clear_edges(wide_grad)

    def body(phase, image, inside, row):
        value = grad_down[pl.ds(row, 64), :].astype(bf16).astype(f32)
        here = pl.ds(PAD + inside, 64)
        wide_grad[image, here, 0:C2] = value.astype(bf16)
        wide_grad[image, here, C2 : 2 * C2] = row_shift(value, 1).astype(bf16)

    each_chunk(body)
    bias_down = jnp.zeros((8, C2), f32)
    bias_down = lax.fori_loop(
        0,
        ROWS // 64,
        lambda n, c: c + fold(grad_down[pl.ds(pl.multiple_of(n * 64, 64), 64), :].astype(bf16).astype(f32)),
        bias_down,
    )
    vector_to(out, at["bias_down"], jnp.sum(bias_down, axis=0, keepdims=True))
    center = wide_rows(wide_grad, 0, 0, C2)
    width = 3 * C1
    for row_tap, (wide, row_off) in enumerate(((wide_one, -1), (wide_zero, 0), (wide_one, 0))):
        product = mm_tn(wide_rows(wide, row_off, 0, width), center)
        matrix_to(out, at["kern_down"] + row_tap * 2 * width, product)

    def taps_rows(first, count):
        return kern_down[first * C1 : (first + count) * C1, :]

    moved = wide_rows(wide_grad, 0, C2, 2 * C2)
    below = wide_rows(wide_grad, 1, 0, C2)
    below_moved = wide_rows(wide_grad, 1, C2, 2 * C2)
    first_pair = mm_nt(center, taps_rows(4, 2))
    second_pair = mm_nt(center, taps_rows(7, 2)) + mm_nt(below, taps_rows(1, 2))
    grads = (
        first_pair[:, :C1],
        first_pair[:, C1:] + mm_nt(moved, taps_rows(3, 1)),
        second_pair[:, :C1],
        second_pair[:, C1:] + mm_nt(moved, taps_rows(6, 1)) + mm_nt(below_moved, taps_rows(0, 1)),
    )
    bias_in = jnp.zeros((8, C1), f32)
    for phase in range(4):
        low_grad[phase] = (skip[phase] + grads[phase]).astype(bf16)
        bias_in = bias_in + fold(low_grad[phase].astype(f32))
    vector_to(out, at["bias_in"], jnp.sum(bias_in, axis=0, keepdims=True))
    kern_in = None
    for phase in range(4):
        part = mm(taps[:, phase * ROWS : (phase + 1) * ROWS].astype(bf16), low_grad[phase])
        kern_in = part if kern_in is None else kern_in + part
    for tap in range(9):
        out[3 * tap : 3 * tap + 3, :] = kern_in[8 * tap : 8 * tap + 3, :]
    out[at["end"] :, :] = jnp.zeros((STEM_ROWS - at["end"], LANES), f32)
    narrow_out(out, me[0], sent, leaving)


def res_forward(
    places, me, gathered, down, embed,
    inner, res_out, act_one, act_two, kern_first, kern_second, dense_two, hidden_pre, stats, gains,
    stage, dense_one, wide,
):
    at = RES_AT
    widen(gathered, places, me[0], stage)
    matrix_from(stage, at["dense_one"], dense_one, TDIM, TEMB)
    matrix_from(stage, at["dense_two"], dense_two, TEMB, C2)
    matrix_from(stage, at["kern_first"], kern_first, 9 * C2, C2)
    matrix_from(stage, at["kern_second"], kern_second, 9 * C2, C2)
    pre = jnp.dot(embed[...], dense_one[...].astype(f32), precision=highest) + vector_at(stage, at["bias_one"], TEMB)
    hidden_pre[...] = pre
    hidden = pre * logistic(pre)
    time_proj = jnp.dot(hidden, dense_two[...].astype(f32), precision=highest) + vector_at(stage, at["bias_two"], C2)
    ones = same_group(C2)
    clear_edges(wide)
    gain = vector_at(stage, at["gain_first"], C2)
    shift = vector_at(stage, at["shift_first"], C2)
    gain_two = vector_at(stage, at["gain_second"], C2)
    shift_two = vector_at(stage, at["shift_second"], C2)
    gains[...] = jnp.concatenate([gain, shift, gain_two, shift_two, jnp.zeros((4, C2), f32)], axis=0)

    def normalize(source, place, gain, shift, keep):
        center, scale = norm_stats(lambda phase, row: source[pl.ds(row, 64), :], 1, C2, ones)
        stats[place : place + IMGS, :] = center
        stats[place + IMGS : place + 2 * IMGS, :] = scale

        def body(phase, image, inside, row):
            value = (source[pl.ds(row, 64), :] - center[image : image + 1, :]) * scale[image : image + 1, :]
            value = value * gain + shift
            value = value * logistic(value)
            keep[pl.ds(row, 64), :] = value.astype(bf16)
            put_shifted(wide, image, inside, value.astype(bf16).astype(f32))

        each_chunk(body)

    normalize(down, 0, gain, shift, act_one)
    bias = vector_at(stage, at["bias_first"], C2)
    product = conv_low(wide, kern_first)
    for image in range(IMGS):
        inner[image * LOW : (image + 1) * LOW, :] = (
            product[image * LOW : (image + 1) * LOW, :] + bias + time_proj[image : image + 1, :]
        )
    normalize(inner, 2 * IMGS, gain_two, shift_two, act_two)
    res_out[...] = down[...] + conv_low(wide, kern_second) + vector_at(stage, at["bias_second"], C2)


def norm_back(load_grad, source, center, scale, gain, shift, ones, active, store):
    def pieces(image, row):
        xhat = (source[pl.ds(row, 64), :] - center[image : image + 1, :]) * scale[image : image + 1, :]
        grad = load_grad(row)
        if active:
            value = xhat * gain + shift
            gate = logistic(value)
            grad = grad * (gate * (1.0 + value * (1.0 - gate)))
        return grad, xhat

    def load(phase, image, row):
        grad, xhat = pieces(image, row)
        return grad, grad * xhat

    gain_grad, shift_grad, mean_one, mean_two = norm_back_stats(load, 1, C2, gain, ones)

    def body(phase, image, inside, row):
        grad, xhat = pieces(image, row)
        store(
            image,
            inside,
            row,
            scale[image : image + 1, :]
            * (grad * gain - mean_one[image : image + 1, :] - xhat * mean_two[image : image + 1, :]),
        )

    each_chunk(body)
    return gain_grad, shift_grad


def res_backward(
    leaving, me, grad_res, down, inner, act_one, act_two, kern_first, kern_second, dense_two, hidden_pre, stats, gains, embed,
    grad_down, sent, out,
    wide, grad_act,
):
    at = RES_AT
    ones = same_group(C2)
    clear_edges(wide)

    def lower(phase, image, inside, row):
        put_shifted(wide, image, inside, grad_res[pl.ds(row, 64), :].astype(bf16).astype(f32))

    each_chunk(lower)
    sums = image_sums(
        lambda phase, image, row: (grad_res[pl.ds(row, 64), :].astype(bf16).astype(f32),), 1, C2
    )[0]
    vector_to(out, at["bias_second"], jnp.sum(sums, axis=0, keepdims=True))
    grad_act[...] = conv_low_back(wide, kern_second)
    conv_low_grad(act_two, wide, out, at["kern_second"])

    def store_inner(image, inside, row, value):
        put_shifted(wide, image, inside, value.astype(bf16).astype(f32))

    gain_grad, shift_grad = norm_back(
        lambda row: grad_act[pl.ds(row, 64), :], inner, stats[8:12, :], stats[12:16, :],
        gains[2:3, :], gains[3:4, :], ones, True, store_inner,
    )
    vector_to(out, at["gain_second"], gain_grad)
    vector_to(out, at["shift_second"], shift_grad)
    inner_sum = jnp.concatenate(
        [
            jnp.sum(fold(wide[image, PAD : PAD + LOW, C2 : 2 * C2].astype(f32)), axis=0, keepdims=True)
            for image in range(IMGS)
        ]
        + [jnp.zeros((4, C2), f32)],
        axis=0,
    )
    time_sum = jnp.sum(inner_sum, axis=0, keepdims=True)
    vector_to(out, at["bias_first"], time_sum)
    vector_to(out, at["bias_two"], time_sum)
    pre = hidden_pre[...]
    gate = logistic(pre)
    contract = (((0,), (0,)), ((), ()))
    matrix_to(
        out, at["dense_two"],
        lax.dot_general(pre * gate, inner_sum, contract, precision=highest, preferred_element_type=f32),
    )
    grad_pre = lax.dot_general(
        inner_sum, dense_two[...].astype(f32), (((1,), (1,)), ((), ())), precision=highest, preferred_element_type=f32
    ) * (gate * (1.0 + pre * (1.0 - gate)))
    vector_to(out, at["bias_one"], jnp.sum(grad_pre, axis=0, keepdims=True))
    matrix_to(
        out, at["dense_one"],
        lax.dot_general(embed[...], grad_pre, contract, precision=highest, preferred_element_type=f32),
    )
    grad_act[...] = conv_low_back(wide, kern_first)
    conv_low_grad(act_one, wide, out, at["kern_first"])

    def store_down(image, inside, row, value):
        grad_down[pl.ds(row, 64), :] = value + grad_res[pl.ds(row, 64), :]

    gain_grad, shift_grad = norm_back(
        lambda row: grad_act[pl.ds(row, 64), :], down, stats[0:4, :], stats[4:8, :],
        gains[0:1, :], gains[1:2, :], ones, True, store_down,
    )
    vector_to(out, at["gain_first"], gain_grad)
    vector_to(out, at["shift_first"], shift_grad)
    out[at["end"] :, :] = jnp.zeros((RES_ROWS - at["end"], LANES), f32)
    narrow_out(out, me[0], sent, leaving)


def attn_forward(
    places, me, gathered, res_out,
    attn_low, normed, qkv, probs, mixed, kern_qkv, kern_proj, stats, gains,
    stage,
):
    at = ATTN_AT
    widen(gathered, places, me[0], stage)
    matrix_from(stage, at["kern_qkv"], kern_qkv, C2, 3 * C2)
    matrix_from(stage, at["kern_proj"], kern_proj, C2, C2)
    ones = same_group(C2)
    gain = vector_at(stage, at["gain_attn"], C2)
    shift = vector_at(stage, at["shift_attn"], C2)
    gains[...] = jnp.concatenate([gain, shift, jnp.zeros((6, C2), f32)], axis=0)
    center, scale = norm_stats(lambda phase, row: res_out[pl.ds(row, 64), :], 1, C2, ones)
    stats[0:IMGS, :] = center
    stats[IMGS : 2 * IMGS, :] = scale

    def body(phase, image, inside, row):
        value = (res_out[pl.ds(row, 64), :] - center[image : image + 1, :]) * scale[image : image + 1, :]
        normed[pl.ds(row, 64), :] = (value * gain + shift).astype(bf16)

    each_chunk(body)
    qkv[...] = mm(normed[...], kern_qkv[...]).astype(bf16)
    for image in range(IMGS):
        rows = slice(image * LOW, (image + 1) * LOW)
        logits = mm_nt(qkv[rows, 0:C2], qkv[rows, C2 : 2 * C2]) * C2 ** (-0.5)
        powers = jnp.exp(logits - jnp.max(logits, axis=1, keepdims=True))
        weights = powers / jnp.sum(powers, axis=1, keepdims=True)
        probs[image] = weights
        mixed[rows, :] = mm(weights.astype(bf16), qkv[rows, 2 * C2 : 3 * C2]).astype(bf16)
    attn_low[...] = (
        res_out[...] + mm(mixed[...], kern_proj[...]) + vector_at(stage, at["bias_proj"], C2)
    ).astype(bf16)


def attn_backward(
    leaving, me, grad_attn, res_out, normed, qkv, probs, mixed, kern_qkv, kern_proj, stats, gains,
    grad_res, sent, out,
    grad_qkv, grad_mixed, grad_normed, low,
):
    at = ATTN_AT
    ones = same_group(C2)
    low[...] = grad_attn[...].astype(bf16)
    sums = image_sums(lambda phase, image, row: (grad_attn[pl.ds(row, 64), :],), 1, C2)[0]
    vector_to(out, at["bias_proj"], jnp.sum(sums, axis=0, keepdims=True))
    matrix_to(out, at["kern_proj"], mm_tn(mixed[...], low[...]))
    grad_mixed[...] = mm_nt(low[...], kern_proj[...]).astype(bf16)
    scale_by = C2 ** (-0.5)
    for image in range(IMGS):
        rows = slice(image * LOW, (image + 1) * LOW)
        query, keys, value = (qkv[rows, part * C2 : (part + 1) * C2] for part in range(3))
        weights = probs[image]
        grad_probs = mm_nt(grad_mixed[rows, :], value)
        grad_qkv[rows, 2 * C2 : 3 * C2] = mm_tn(weights.astype(bf16), grad_mixed[rows, :]).astype(bf16)
        grad_logits = (
            weights * (grad_probs - jnp.sum(weights * grad_probs, axis=1, keepdims=True))
        ).astype(bf16)
        grad_qkv[rows, 0:C2] = (mm(grad_logits, keys) * scale_by).astype(bf16)
        grad_qkv[rows, C2 : 2 * C2] = (mm_tn(grad_logits, query) * scale_by).astype(bf16)
    matrix_to(out, at["kern_qkv"], mm_tn(normed[...], grad_qkv[...]))
    grad_normed[...] = mm_nt(grad_qkv[...], kern_qkv[...])

    def store(image, inside, row, value):
        grad_res[pl.ds(row, 64), :] = value + grad_attn[pl.ds(row, 64), :]

    gain_grad, shift_grad = norm_back(
        lambda row: grad_normed[pl.ds(row, 64), :], res_out, stats[0:4, :], stats[4:8, :],
        gains[0:1, :], gains[1:2, :], ones, False, store,
    )
    vector_to(out, at["gain_attn"], gain_grad)
    vector_to(out, at["shift_attn"], shift_grad)
    out[at["end"] :, :] = jnp.zeros((ATTN_ROWS - at["end"], LANES), f32)
    narrow_out(out, me[0], sent, leaving)


def pick(row, channel):
    lane = lax.broadcasted_iota(jnp.int32, (LANES, LANES), 0)
    ch = lax.broadcasted_iota(jnp.int32, (LANES, LANES), 1)
    return (row * LANES + lane == CIN * ch + channel).astype(f32).astype(bf16)


def head_step(
    places, leaving, me, gathered, attn_low, top, clean, factor,
    grad_attn, skip, loss, sent, out,
    stage, wide, kern_up, merged, act, taps, narrow, grad_wide_zero, grad_wide_one, boxes,
):
    at = HEAD_AT
    widen(gathered, places, me[0], stage)
    ones = same_group(C1)
    kern_up[...] = jnp.zeros(kern_up.shape, bf16)

    def combine(at_row):
        tap = [[stage[pl.ds((3 * a + b) * C2 + at_row, 64), :] for b in range(3)] for a in range(3)]
        by_row = {(0, 0): tap[0], (0, 1): [tap[1][b] + tap[2][b] for b in range(3)],
                  (1, 0): [tap[0][b] + tap[1][b] for b in range(3)], (1, 1): tap[2]}
        for (row_phase, slot), three in by_row.items():
            for col_off in range(3):
                base = (slot * 3 + col_off) * C2
                here = pl.ds(base + at_row, 64)
                if col_off == 0:
                    kern_up[row_phase, here, 0:C1] = three[0].astype(bf16)
                elif col_off == 1:
                    kern_up[row_phase, here, 0:C1] = (three[1] + three[2]).astype(bf16)
                    kern_up[row_phase, here, C1 : 2 * C1] = (three[0] + three[1]).astype(bf16)
                else:
                    kern_up[row_phase, here, C1 : 2 * C1] = three[2].astype(bf16)

    chunks(C2, 64, combine)
    clear_edges(wide)

    def spread_low(phase, image, inside, row):
        put_shifted(wide, image, inside, attn_low[pl.ds(row, 64), :].astype(f32))

    each_chunk(spread_low)
    bias_up = stage[at["bias_up"] : at["bias_up"] + 1, :]
    for row_phase in range(2):
        product = mm(
            jnp.concatenate(
                [wide_rows(wide, row_phase - 1, 0, 3 * C2), wide_rows(wide, row_phase, 0, 3 * C2)], axis=1
            ),
            kern_up[row_phase],
        )
        for col_phase in range(2):
            phase = row_phase * 2 + col_phase
            merged[phase] = product[:, col_phase * C1 : (col_phase + 1) * C1] + bias_up + top[phase]
    gain = stage[at["gain_out"] : at["gain_out"] + 1, :]
    shift = stage[at["shift_out"] : at["shift_out"] + 1, :]
    center, scale = norm_stats(lambda phase, row: merged[phase, pl.ds(row, 64), :], 4, C1, ones)

    def body(phase, image, inside, row):
        value = (merged[phase, pl.ds(row, 64), :] - center[image : image + 1, :]) * scale[image : image + 1, :]
        value = value * gain + shift
        act[phase, pl.ds(row, 64), :] = (value * logistic(value)).astype(bf16)

    each_chunk(body, 4)
    for channel in range(CIN):
        total = None
        for row in range(3):
            part = mm(stage[pl.ds(at["kern_out"] + row, 9, 3), :].astype(bf16), pick(row, channel))
            total = part if total is None else total + part
        narrow[pl.ds(channel, 9, 8), :] = total
    for channel in range(CIN, 8):
        narrow[pl.ds(channel, 9, 8), :] = jnp.zeros((9, LANES), f32)
    kern_out = narrow[...].astype(bf16)
    masks = lane_masks(ROWS)
    for phase in range(4):
        taps[:, phase * ROWS : (phase + 1) * ROWS] = mm_nt(kern_out, act[phase])
    lane = lax.broadcasted_iota(jnp.int32, (8, LANES), 1)
    channel_at = lax.broadcasted_iota(jnp.int32, (8, LANES), 0)
    bias_out = jnp.sum(
        jnp.where((lane == channel_at) & (channel_at < CIN), stage[at["bias_out"] : at["bias_out"] + 1, :], 0.0),
        axis=1,
        keepdims=True,
    )
    pixel_count = CIN * SIDE * SIDE
    loss_sum = jnp.zeros((8, ROWS), f32)
    bias_grad = jnp.zeros((8, 1), f32)
    grad_lanes = []
    for phase in range(4):
        predict = bias_out
        for tap, off in enumerate(TAPS):
            other, row_off, col_off = tap_source(phase, off)
            predict = predict + lane_shift(
                taps[8 * tap : 8 * tap + 8, other * ROWS : (other + 1) * ROWS], row_off, col_off, masks
            )
        error = predict - clean[:, phase * ROWS : (phase + 1) * ROWS]
        loss_sum = loss_sum + error * error * factor[...]
        grad = ((2.0 / pixel_count) * factor[...] * error).astype(bf16).astype(f32)
        bias_grad = bias_grad + jnp.sum(grad, axis=1, keepdims=True)
        grad_lanes.append(grad)
    loss[...] = jnp.sum(jnp.sum(loss_sum, axis=1, keepdims=True), axis=0, keepdims=True) * (1.0 / pixel_count)
    out[at["bias_out"] : at["bias_out"] + 1, :] = jnp.sum(
        jnp.where((lane == channel_at) & (channel_at < CIN), bias_grad, 0.0), axis=0, keepdims=True
    )
    for phase in range(4):
        for tap, off in enumerate(TAPS):
            other, row_off, col_off = tap_source(phase, (-off[0], -off[1]))
            taps[8 * tap : 8 * tap + 8, phase * ROWS : (phase + 1) * ROWS] = lane_shift(
                grad_lanes[other], row_off, col_off, masks
            )
    kern_grad = None
    for phase in range(4):
        low = taps[:, phase * ROWS : (phase + 1) * ROWS].astype(bf16)
        part = mm(low, act[phase])
        kern_grad = part if kern_grad is None else kern_grad + part
        skip[phase] = mm_tn(low, kern_out)
    narrow[...] = kern_grad
    for row in range(3):
        total = None
        for channel in range(CIN):
            pieces = parts_of(narrow[pl.ds(channel, 9, 8), :])
            part = sum(mm_nt(piece, pick(row, channel)) for piece in pieces)
            total = part if total is None else total + part
        out[pl.ds(at["kern_out"] + row, 9, 3), :] = total

    def pieces(phase, image, row):
        xhat = (merged[phase, pl.ds(row, 64), :] - center[image : image + 1, :]) * scale[image : image + 1, :]
        value = xhat * gain + shift
        gate = logistic(value)
        return skip[phase, pl.ds(row, 64), :] * (gate * (1.0 + value * (1.0 - gate))), xhat

    def load(phase, image, row):
        grad, xhat = pieces(phase, image, row)
        return grad, grad * xhat

    gain_grad, shift_grad, mean_one, mean_two = norm_back_stats(load, 4, C1, gain, ones)
    vector_to(out, at["gain_out"], gain_grad)
    vector_to(out, at["shift_out"], shift_grad)
    clear_edges(grad_wide_zero)
    clear_edges(grad_wide_one)
    clear_edges(boxes)
    wides = (grad_wide_zero, grad_wide_one)

    def back(phase, image, inside, row):
        for row_phase in range(2):
            pair = []
            for col_phase in range(2):
                phase = row_phase * 2 + col_phase
                grad, xhat = pieces(phase, image, row)
                value = scale[image : image + 1, :] * (
                    grad * gain - mean_one[image : image + 1, :] - xhat * mean_two[image : image + 1, :]
                )
                skip[phase, pl.ds(row, 64), :] = value
                pair.append(value.astype(bf16).astype(f32))
            put_shifted(wides[row_phase], image, inside, jnp.concatenate(pair, axis=1))
            here = pl.ds(PAD + inside, 64)
            base = row_phase * 3 * C1
            boxes[image, here, base : base + C1] = pair[1] + row_shift(pair[0], 1)
            boxes[image, here, base + C1 : base + 2 * C1] = pair[0] + pair[1]
            boxes[image, here, base + 2 * C1 : base + 3 * C1] = row_shift(pair[1], -1) + pair[0]

    each_chunk(back)
    bias_sum = jnp.zeros((8, C1), f32)
    for row_phase in range(2):
        for image in range(IMGS):
            both = fold(wides[row_phase][image, PAD : PAD + LOW, C2 : 2 * C2].astype(f32))
            bias_sum = bias_sum + both[:, :C1] + both[:, C1:]
    vector_to(out, at["bias_up"], jnp.sum(bias_sum, axis=0, keepdims=True))
    total = None
    for row_phase in range(2):
        for slot in range(2):
            base = slot * 3 * C2
            taps = [kern_up[row_phase, base + at * C2 : base + (at + 1) * C2, :] for at in (2, 1, 0)]
            part = mm_nt(wide_rows(wides[row_phase], 1 - row_phase - slot, 0, 3 * C2), jnp.concatenate(taps, axis=1))
            total = part if total is None else total + part
    grad_attn[...] = total
    width = 3 * C1

    def box_rows(row_off, row_phase):
        return boxes[
            :, PAD + 16 * row_off : PAD + 16 * row_off + LOW, row_phase * width : (row_phase + 1) * width
        ].reshape(ROWS, width)

    summed = (
        box_rows(0, 1) + box_rows(1, 0),
        box_rows(0, 0) + box_rows(0, 1),
        box_rows(-1, 1) + box_rows(0, 0),
    )
    for row_tap in range(3):
        product = mm_tn(attn_low[...], summed[row_tap].astype(bf16))
        for col_tap in range(3):
            tap = row_tap * 3 + col_tap
            out[tap * C2 : (tap + 1) * C2, :] = product[:, col_tap * C1 : (col_tap + 1) * C1]
    out[at["end"] :, :] = jnp.zeros((HEAD_ROWS - at["end"], LANES), f32)
    narrow_out(out, me[0], sent, leaving)


def sds(shape, dtype=f32):
    return jax.ShapeDtypeStruct(shape, dtype)


def run(body, scalars, ins, outs, scratch=(), limit=62):
    in_leaves, in_tree = jax.tree.flatten([*scalars, *ins])
    out_leaves, out_tree = jax.tree.flatten(outs)

    def kernel(*refs):
        split = len(in_leaves), len(in_leaves) + len(out_leaves)
        body(
            *jax.tree.unflatten(in_tree, refs[: split[0]]),
            *jax.tree.unflatten(out_tree, refs[split[0] : split[1]]),
            *refs[split[1] :],
        )

    whole = pl.BlockSpec(memory_space=pltpu.VMEM)
    scalar = pl.BlockSpec(memory_space=pltpu.SMEM)
    results = pl.pallas_call(
        kernel,
        out_shape=out_leaves,
        in_specs=[scalar] * len(scalars) + [whole] * (len(in_leaves) - len(scalars)),
        out_specs=[whole] * len(out_leaves),
        scratch_shapes=scratch,
        compiler_params=pltpu.CompilerParams(vmem_limit_bytes=limit * 2**20),
    )(*in_leaves)
    return jax.tree.unflatten(out_tree, results)


def wide_scratch(width, dtype=bf16):
    return pltpu.VMEM((IMGS, PADDED, width), dtype)


SAVED = dict(
    stage=((RES_ROWS, LANES), f32), block_out=((HEAD_ROWS, LANES), f32),
    taps=((72, 4 * ROWS), f32), low_taps=((72, 4 * ROWS), f32), narrow=((72, LANES), f32),
    top=((4, ROWS, C1), f32), down=((ROWS, C2), f32), inner=((ROWS, C2), f32), res_out=((ROWS, C2), f32),
    act_one=((ROWS, C2), bf16), act_two=((ROWS, C2), bf16), attn_low=((ROWS, C2), bf16), normed=((ROWS, C2), bf16),
    qkv=((ROWS, 3 * C2), bf16), probs=((IMGS, LOW, LOW), f32), mixed=((ROWS, C2), bf16),
    merged=((4, ROWS, C1), f32), act=((4, ROWS, C1), bf16), skip=((4, ROWS, C1), f32),
    grad_attn=((ROWS, C2), f32), grad_res=((ROWS, C2), f32), grad_act=((ROWS, C2), f32),
    grad_low=((ROWS, C2), bf16), grad_mixed=((ROWS, C2), bf16), grad_qkv=((ROWS, 3 * C2), bf16),
    dense_one=((TDIM, TEMB), bf16), dense_two=((TEMB, C2), bf16), kern_down=((9 * C1, C2), bf16),
    kern_first=((9 * C2, C2), bf16), kern_second=((9 * C2, C2), bf16), kern_qkv=((C2, 3 * C2), bf16),
    kern_proj=((C2, C2), bf16), kern_up=((2, 6 * C2, C2), bf16),
    hidden_pre=((8, TEMB), f32), res_stats=((16, C2), f32), res_gains=((8, C2), f32),
    attn_stats=((8, C2), f32), attn_gains=((8, C2), f32),
    wide=((IMGS, PADDED, 3 * C2), bf16), wide_zero=((IMGS, PADDED, 3 * C2), bf16),
    wide_one=((IMGS, PADDED, 3 * C2), bf16), boxes=((IMGS, PADDED, 6 * C1), f32),
)


class Named:
    def __init__(self, names, refs):
        self.__dict__.update(zip(names, refs))


def whole_step(places, leaving, me, gathered, noisy, clean, factor, embed, loss, sent, *refs):
    own = Named(SAVED, refs)
    stem_wide, stem_wide_zero = own.wide.at[:, :, 0 : 3 * C1], own.wide_zero.at[:, :, 0 : 3 * C1]
    stem_forward(
        places[0], me, gathered[0], noisy, own.top, own.down, own.kern_down, own.stage, own.taps, stem_wide, stem_wide_zero
    )
    res_forward(
        places[1], me, gathered[1], own.down, embed,
        own.inner, own.res_out, own.act_one, own.act_two, own.kern_first, own.kern_second, own.dense_two,
        own.hidden_pre, own.res_stats, own.res_gains,
        own.stage, own.dense_one, own.wide,
    )
    attn_forward(
        places[2], me, gathered[2], own.res_out,
        own.attn_low, own.normed, own.qkv, own.probs, own.mixed, own.kern_qkv, own.kern_proj,
        own.attn_stats, own.attn_gains,
        own.stage,
    )
    head_step(
        places[3], leaving[3], me, gathered[3], own.attn_low, own.top, clean, factor,
        own.grad_attn, own.skip, loss, sent[3], own.block_out,
        own.stage, own.wide, own.kern_up, own.merged, own.act, own.low_taps, own.narrow,
        own.wide_zero, own.wide_one, own.boxes,
    )
    attn_backward(
        leaving[2], me, own.grad_attn, own.res_out, own.normed, own.qkv, own.probs, own.mixed,
        own.kern_qkv, own.kern_proj, own.attn_stats, own.attn_gains,
        own.grad_res, sent[2], own.block_out.at[0:ATTN_ROWS],
        own.grad_qkv, own.grad_mixed, own.grad_act, own.grad_low,
    )
    res_backward(
        leaving[1], me, own.grad_res, own.down, own.inner, own.act_one, own.act_two, own.kern_first, own.kern_second,
        own.dense_two, own.hidden_pre, own.res_stats, own.res_gains, embed,
        own.grad_attn, sent[1], own.stage,
        own.wide, own.grad_act,
    )
    stem_backward(
        leaving[0], me, noisy, own.top, own.skip, own.grad_attn, own.kern_down, sent[0], own.block_out,
        own.taps, stem_wide, stem_wide_zero, own.wide_one.at[:, :, 0 : 2 * C2], own.act,
    )


def local_step(me, arrays, places, shapes, out_places, noisy, clean, factor, embed):
    def body(me, arrays, noisy, clean, factor, embed, loss, sent, *refs):
        gathered = [[arrays[place[0]] for place in block] for block in places]
        leaving = [[sent[place[0]] for place in block] for block in out_places]
        rest = [[place[1:] for place in block] for block in places]
        out_rest = [[place[1:] for place in block] for block in out_places]
        whole_step(rest, out_rest, me, gathered, noisy, clean, factor, embed, loss, leaving, *refs)

    return run(
        body,
        [me],
        [arrays, noisy, clean, factor, embed],
        [sds((1, 1)), shapes],
        [pltpu.VMEM(shape, dtype) for shape, dtype in SAVED.values()],
    )


def plan(step_counts, time_index, teacher_size):
    position = time_index % step_counts
    time_values = (2 * position + teacher_size).astype(f32) / (2 * step_counts).astype(f32)
    alpha_t = jnp.cos(0.5 * math.pi * time_values)
    sigma_t = jnp.sin(0.5 * math.pi * time_values)
    weight = jnp.maximum(alpha_t * alpha_t / (sigma_t * sigma_t), 1.0)
    return (time_values, alpha_t, sigma_t, weight)


def sinusoid(time_values):
    half_dim = TDIM // 2
    frequency = jnp.exp(-math.log(10000.0) * jnp.arange(half_dim, dtype=f32) / half_dim)
    angles = 1000.0 * time_values[:, None] * frequency[None, :]
    return jnp.concatenate([jnp.sin(angles), jnp.cos(angles)], axis=1)


def by_phase(images):
    split = images.reshape(IMGS, CIN, 16, 2, 16, 2).transpose(1, 3, 5, 0, 2, 4).reshape(CIN, 4 * ROWS)
    return jnp.pad(split, ((0, 8 - CIN), (0, 0)))


def prepare(clean_images, noise_field, step_counts, time_index, teacher_size, image_count):
    slot_count = clean_images.shape[0]
    time_values, alpha_t, sigma_t, weight = plan(step_counts, time_index, teacher_size)
    live_mask = (jnp.arange(slot_count, dtype=jnp.int32) < image_count).astype(f32)
    factor = live_mask * weight
    noisy = (alpha_t[:, None, None] * clean_images + sigma_t[:, None, None] * noise_field).astype(bf16).astype(f32)
    embed = jnp.pad(sinusoid(time_values), ((0, 8 - IMGS), (0, 0)))
    factor_lanes = jnp.repeat(factor, LOW)[None, :]
    return by_phase(noisy), by_phase(clean_images), factor_lanes, embed


AXES = ("dp", "fsdp")
BLOCK_ROWS = (STEM_ROWS, RES_ROWS, ATTN_ROWS, HEAD_ROWS)
SHARD_ROWS = (80, 344, 72, 80)
SPAN = 32
HALVES = (
    (((0, 0, 80), (1, 0, 200)), (2, 4)),
    (((1, 200, 344), (3, 0, 80), (2, 0, 72)), (4, 2)),
)
HALF_ROWS = tuple(sum(hi - lo for _, lo, hi in members) for members, _ in HALVES)
LINE = (0, 8, 16, 24)


def swap(values, mask):
    return lax.ppermute(values, AXES, [(here, here ^ mask) for here in range(SPAN)])


def pack_rows(masters):
    def body(refs, out):
        at = 0
        for members, _ in HALVES:
            for block, lo, hi in members:
                out[at : at + hi - lo, :] = refs[block][lo:hi, :].astype(bf16)
                at += hi - lo

    return run(body, [], [masters], [sds((sum(HALF_ROWS), LANES), bf16)], limit=8)[0]


def half_places(number, array, masks):
    at, found = 0, []
    for block, lo, hi in HALVES[number][0]:
        found.append((block, (array, masks, at, at + hi - lo, SHARD_ROWS[block], lo)))
        at += hi - lo
    return found


def gather_halves(own, prepared):
    line = [own] + [swap(own, mask) for mask in LINE[1:]]
    line, prepared = lax.optimization_barrier((line, prepared))
    arrays, places = [], [[] for _ in SHARD_ROWS]

    def add(number, array, masks):
        for block, place in half_places(number, len(arrays), masks):
            places[block].append(place)
        arrays.append(array)

    held = []
    for number, (_, (last, first)) in enumerate(HALVES):
        begin = number * HALF_ROWS[0]
        near = jnp.stack([piece[begin : begin + HALF_ROWS[number]] for piece in line], axis=0)
        held.append(jnp.concatenate([near, swap(near, first)], axis=0))
    for number, (_, (last, first)) in enumerate(HALVES):
        masks = [a ^ b for a in (0, first) for b in LINE]
        far = swap(held[number], last)
        add(number, held[number], masks)
        add(number, far, [mask ^ last for mask in masks])
        add(number, swap(held[number], 1), [mask ^ 1 for mask in masks])
        add(number, swap(far, 1), [mask ^ last ^ 1 for mask in masks])
    return arrays, places, prepared


def leaving_halves():
    shapes, places = [], [[] for _ in SHARD_ROWS]
    for number, (_, (first, last)) in enumerate(HALVES):
        for core in (0, 1):
            for side in (0, first):
                masks = [core ^ side ^ a ^ b for a in (0, last) for b in LINE]
                for block, place in half_places(number, len(shapes), masks):
                    places[block].append(place)
                shapes.append(sds((8, HALF_ROWS[number], LANES), bf16))
    return shapes, places


def reduce_halves(leaving):
    totals = []
    crossed = [[None, None], [None, None]]
    for side in (1, 0):
        for number in (0, 1):
            kept, sent = leaving[4 * number + side], leaving[4 * number + 2 + side]
            crossed[number][side] = kept.astype(f32) + swap(sent, 1).astype(f32)
    for number, (_, (first, last)) in enumerate(HALVES):
        near, far = crossed[number]
        totals.append(near + swap(far.astype(bf16), first).astype(f32))
    for number, (_, (first, last)) in enumerate(HALVES):
        total = totals[number]
        totals[number] = total[:4] + swap(total[4:].astype(bf16), last).astype(f32)
    whole = jnp.concatenate(totals, axis=1)
    return [whole[0]] + [swap(whole[number + 1].astype(bf16), mask) for number, mask in enumerate(LINE[1:])]


def last_sum(image_counts, count, loss, pieces):
    def body(live, loss, pieces, total, row):
        value = pieces[0][...].astype(f32)
        for piece in pieces[1:]:
            value = value + piece[...].astype(f32)
        total[...] = value
        square = jnp.sum(fold(value * value), axis=0, keepdims=True)
        square = jnp.sum(square, axis=1, keepdims=True)
        lane = lax.broadcasted_iota(jnp.int32, (1, LANES), 1)
        scalars = jnp.where(lane == 0, loss[...], jnp.where(lane == 1, square, live[0].astype(f32)))
        row[...] = jnp.broadcast_to(scalars[None], row.shape)

    rows = pieces[0].shape[0]
    return run(body, [image_counts], [loss, pieces], [sds((rows, LANES)), sds((count, 1, LANES))], limit=16)


def update(adam_step, arrived, gradient, masters, firsts, seconds, places):
    def body(step, arrived, gradient, masters, firsts, seconds, loss, norm, outs):
        sums = jnp.sum(arrived[...], axis=0)
        live = 1.0 / sums[:, 2:3]
        loss[...] = sums[:, 0:1] * live
        size = jnp.sqrt(sums[:, 1:2]) * live
        norm[...] = size
        scale = clip_limit / jnp.maximum(size, clip_limit) * live
        powers = lax.fori_loop(
            0, step[0], lambda _, held: (held[0] * beta_one, held[1] * beta_two), (jnp.float32(1.0), jnp.float32(1.0))
        )
        fix_one, fix_two = 1.0 - powers[0], 1.0 - powers[1]
        at = 0
        for block, lo, hi in places:
            grad = gradient[at : at + hi - lo, :] * scale
            at += hi - lo
            master, first, second = (refs[block][lo:hi, :] for refs in (masters, firsts, seconds))
            first_new = beta_one * first + (1.0 - beta_one) * grad
            second_new = beta_two * second + (1.0 - beta_two) * grad * grad
            master_new = master - learn_rate * (
                first_new / fix_one / (jnp.sqrt(second_new / fix_two) + adam_eps) + decay_rate * master
            )
            for ref, value in zip(outs[block], (master_new, first_new, second_new, master_new.astype(bf16))):
                ref[lo:hi, :] = value

    shapes = [[sds(m.shape), sds(m.shape), sds(m.shape), sds(m.shape, bf16)] for m in masters]
    return run(
        body, [adam_step], [arrived, gradient, masters, firsts, seconds], [sds((1, 1)), sds((1, 1)), shapes], limit=24
    )


def gather_whole(shards):
    arrays = [
        lax.all_gather(shard.reshape(-1), AXES, axis=0, tiled=True).reshape(1, rows, LANES)
        for shard, rows in zip(shards, BLOCK_ROWS)
    ]
    return arrays, [[(block, (0,), 0, rows, 0, 0)] for block, rows in enumerate(BLOCK_ROWS)]


def leaving_whole():
    shapes = [sds((1, rows, LANES), bf16) for rows in BLOCK_ROWS]
    return shapes, [[(block, (0,), 0, rows, 0, 0)] for block, rows in enumerate(BLOCK_ROWS)]


def reduce_whole(leaving):
    sums = [
        lax.psum_scatter(array.astype(f32).reshape(-1), AXES, scatter_dimension=0, tiled=True) for array in leaving
    ]
    return [jnp.concatenate([one.reshape(-1, LANES) for one in sums], axis=0)]


def per_device(
    clean_images, noise_field, step_counts, time_index, teacher_size, image_counts, adam_step,
    stem_master, stem_first, stem_second, res_master, res_first, res_second,
    attn_master, attn_first, attn_second, head_master, head_first, head_second,
):
    blocks = [
        [block.reshape(-1, LANES) for block in state]
        for state in (
            (stem_master, res_master, attn_master, head_master),
            (stem_first, res_first, attn_first, head_first),
            (stem_second, res_second, attn_second, head_second),
        )
    ]
    masters = blocks[0]
    count = lax.axis_size(AXES)
    me = lax.axis_index(AXES).astype(jnp.int32).reshape(1)
    laid_out = count == SPAN and tuple(master.shape[0] for master in masters) == SHARD_ROWS
    prepared = prepare(clean_images, noise_field, step_counts, time_index, teacher_size, image_counts[0])
    if laid_out:
        arrays, places, prepared = gather_halves(pack_rows(masters), prepared)
        shapes, out_places = leaving_halves()
        order = [member for members, _ in HALVES for member in members]
    else:
        arrays, places = gather_whole([master.astype(bf16) for master in masters])
        shapes, out_places = leaving_whole()
        order = [(block, 0, master.shape[0]) for block, master in enumerate(masters)]
    loss, leaving = local_step(me, arrays, places, shapes, out_places, *prepared)
    pieces = reduce_halves(leaving) if laid_out else reduce_whole(leaving)
    gradient, row = last_sum(image_counts, count, loss, pieces)
    arrived = lax.all_to_all(row, AXES, 0, 0, tiled=True)
    loss, norm, outs = update(adam_step, arrived, gradient, *blocks, order)
    return (loss[0, 0], norm[0, 0]) + tuple(value.reshape(-1) for block in outs for value in block)


def solution(mesh):
    split = P(("dp", "fsdp"))
    images = P(("dp", "fsdp"), None, None)
    return jax.shard_map(
        per_device,
        mesh=mesh,
        in_specs=(images, images, split, split, split, split, P()) + (split,) * 12,
        out_specs=(P(), P()) + (split,) * 16,
        check_vma=False,
    )
```

```python
from functools import partial
import math

import jax
import jax.numpy as jnp
from jax import lax
from jax.experimental import pallas as pl
from jax.experimental.pallas import tpu as pltpu
from jax.sharding import PartitionSpec as P

C1 = 128
C2 = 256
GROUPS = 32
TDIM = 128
TEMB = 512
CIN = 3
SIDE = 32
LANES = 128
IMGS = 4
LOW = 256
ROWS = IMGS * LOW
PAD = 16
PADDED = LOW + 2 * PAD

clip_limit = 0.05
learn_rate = 0.05
beta_one = 0.9
beta_two = 0.999
adam_eps = 1e-08
decay_rate = 0.01
norm_eps = 1e-05

f32 = jnp.float32
bf16 = jnp.bfloat16
highest = lax.Precision.HIGHEST

STEM_ROWS, RES_ROWS, ATTN_ROWS, HEAD_ROWS = 2560, 11008, 2304, 2560

STEM_AT = dict(kern_in=0, bias_in=27, kern_down=28, bias_down=2332, end=2334)
RES_AT = dict(
    dense_one=0, bias_one=512, dense_two=516, bias_two=1540, gain_first=1542, shift_first=1544,
    kern_first=1546, bias_first=6154, gain_second=6156, shift_second=6158, kern_second=6160,
    bias_second=10768, end=10770,
)
ATTN_AT = dict(gain_attn=0, shift_attn=2, kern_qkv=4, kern_proj=1540, bias_proj=2052, end=2054)
HEAD_AT = dict(kern_up=0, bias_up=2304, gain_out=2305, shift_out=2306, kern_out=2307, bias_out=2334, end=2335)


def mm(a, b):
    return jnp.dot(a, b, preferred_element_type=f32)


def mm_nt(a, b):
    return lax.dot_general(a, b, (((1,), (1,)), ((), ())), preferred_element_type=f32)


def mm_tn(a, b):
    return lax.dot_general(a, b, (((0,), (0,)), ((), ())), preferred_element_type=f32)


def parts_of(values):
    high = values.astype(bf16)
    rest = values - high.astype(f32)
    middle = rest.astype(bf16)
    return high, middle, (rest - middle.astype(f32)).astype(bf16)


def mm_exact(values, matrix):
    return sum(mm(piece, matrix) for piece in parts_of(values))


def same_group(channels):
    size = channels // GROUPS
    down_at = lax.broadcasted_iota(jnp.int32, (channels, channels), 0) // size
    across = lax.broadcasted_iota(jnp.int32, (channels, channels), 1) // size
    return (down_at == across).astype(f32).astype(bf16)


def row_shift(values, step):
    count = values.shape[0]
    moved = pltpu.roll(values, (-step) % count, 0)
    column = lax.broadcasted_iota(jnp.int32, values.shape, 0) & 15
    return jnp.where(column == (0 if step < 0 else 15), 0.0, moved)


def chunks(total, size, body):
    def step(number, carry):
        body(pl.multiple_of(number * size, size))
        return carry

    lax.fori_loop(0, total // size, step, 0, unroll=True)


def widen(pieces, places, me, stage):
    for ref, (masks, lo, hi, per_shard, begin) in zip(pieces, places):
        for number, mask in enumerate(masks):
            owner = me ^ mask
            at = pl.multiple_of(owner * per_shard + begin, 8)
            stage[pl.ds(at, hi - lo), :] = ref[number, lo:hi, :].astype(f32)


def narrow_out(stage, me, outs, places):
    for ref, (masks, lo, hi, per_shard, begin) in zip(outs, places):
        for number, mask in enumerate(masks):
            owner = me ^ mask
            at = pl.multiple_of(owner * per_shard + begin, 8)
            ref[number, lo:hi, :] = stage[pl.ds(at, hi - lo), :].astype(ref.dtype)


def matrix_from(stage, base, out, depth, width):
    lanes = width // LANES

    def copy(at):
        for lane in range(lanes):
            out[pl.ds(at, 128), lane * LANES : (lane + 1) * LANES] = stage[
                pl.ds(base + lanes * at + lane, 128, lanes), :
            ].astype(bf16)

    chunks(depth, 128, copy)


def matrix_to(out, base, value):
    depth, width = value.shape
    lanes = width // LANES
    for lane in range(lanes):
        out[pl.ds(base + lane, depth, lanes), :] = value[:, lane * LANES : (lane + 1) * LANES]


def vector_at(stage, base, width):
    return jnp.concatenate([stage[base + lane : base + lane + 1, :] for lane in range(width // LANES)], axis=1)


def vector_to(out, base, value):
    for lane in range(value.shape[1] // LANES):
        out[base + lane : base + lane + 1, :] = value[:, lane * LANES : (lane + 1) * LANES]


def fold(values):
    return jnp.sum(values.reshape(values.shape[0] // 8, 8, values.shape[1]), axis=0)


def image_sums(load, phases, width):
    sums = []
    for image in range(IMGS):
        def step(number, carry):
            row = pl.multiple_of(image * LOW + number * 64, 64)
            for phase in range(phases):
                carry = tuple(c + fold(v) for c, v in zip(carry, load(phase, image, row)))
            return carry

        first = load(0, image, image * LOW)
        carry = lax.fori_loop(0, 4, step, tuple(jnp.zeros((8, width), f32) for _ in first), unroll=True)
        sums.append([jnp.sum(c, axis=0, keepdims=True) for c in carry])
    return [jnp.concatenate(list(group), axis=0) for group in zip(*sums)]


def norm_stats(load, phases, width, ones):
    count = LOW * phases * (width // GROUPS)
    (total,) = image_sums(lambda phase, image, row: (load(phase, row),), phases, width)
    center = mm_exact(total, ones) * (1.0 / count)

    def squares(phase, image, row):
        away = load(phase, row) - center[image : image + 1, :]
        return (away * away,)

    (total,) = image_sums(squares, phases, width)
    spread = mm_exact(total, ones) * (1.0 / count)
    return center, lax.rsqrt(spread + norm_eps)


def norm_back_stats(load, phases, width, gain, ones):
    count = LOW * phases * (width // GROUPS)
    shift_sum, gain_sum = image_sums(load, phases, width)
    means = mm_exact(jnp.concatenate([shift_sum * gain, gain_sum * gain], axis=0), ones) * (1.0 / count)
    return (
        jnp.sum(gain_sum, axis=0, keepdims=True),
        jnp.sum(shift_sum, axis=0, keepdims=True),
        means[:IMGS],
        means[IMGS:],
    )


def logistic(values):
    return 0.5 * jnp.tanh(0.5 * values) + 0.5


def each_chunk(body, phases=1, size=64):
    for image in range(IMGS):
        def step(number, carry):
            inside = pl.multiple_of(number * size, size)
            for phase in range(phases):
                body(phase, image, inside, image * LOW + inside)
            return carry

        lax.fori_loop(0, LOW // size, step, 0, unroll=True)


def clear_edges(wide):
    for image in range(IMGS):
        wide[image, 0:PAD, :] = jnp.zeros((PAD, wide.shape[2]), wide.dtype)
        wide[image, PAD + LOW : PADDED, :] = jnp.zeros((PAD, wide.shape[2]), wide.dtype)


def put_shifted(wide, image, inside, value):
    width = value.shape[1]
    at = pl.ds(PAD + inside, value.shape[0])
    wide[image, at, 0:width] = row_shift(value, -1).astype(bf16)
    wide[image, at, width : 2 * width] = value.astype(bf16)
    wide[image, at, 2 * width : 3 * width] = row_shift(value, 1).astype(bf16)


def wide_rows(wide, row_off, lo, hi):
    begin = PAD + 16 * row_off
    return wide[:, begin : begin + LOW, lo:hi].reshape(ROWS, hi - lo)


def conv_low(wide, kern):
    width = wide.shape[2]
    total = None
    for tap in range(3):
        part = mm(wide_rows(wide, tap - 1, 0, width), kern[tap * width : (tap + 1) * width, :])
        total = part if total is None else total + part
    return total


def conv_low_back(wide, kern):
    total = None
    for row_tap in range(3):
        taps = [kern[(row_tap * 3 + col_tap) * C2 : (row_tap * 3 + col_tap + 1) * C2, :] for col_tap in (2, 1, 0)]
        part = mm_nt(wide_rows(wide, 1 - row_tap, 0, 3 * C2), jnp.concatenate(taps, axis=1))
        total = part if total is None else total + part
    return total


def conv_low_grad(source, wide, out, base):
    for row_tap in range(3):
        product = mm_tn(source[...], wide_rows(wide, 1 - row_tap, 0, 3 * C2))
        for col_tap in range(3):
            tap = row_tap * 3 + col_tap
            matrix_to(out, base + tap * 2 * C2, product[:, (2 - col_tap) * C2 : (3 - col_tap) * C2])


def lane_masks(width):
    place = lax.broadcasted_iota(jnp.int32, (8, width), 1)
    row, column = (place >> 4) & 15, place & 15

    def valid(row_off, col_off):
        keep = None
        for at, off in ((row, row_off), (column, col_off)):
            if off:
                inside = at != (0 if off < 0 else 15)
                keep = inside if keep is None else keep & inside
        return keep

    return {(r, c): valid(r, c) for r in (-1, 0, 1) for c in (-1, 0, 1)}


def lane_shift(values, row_off, col_off, masks):
    step = 16 * row_off + col_off
    if step == 0:
        return values
    moved = pltpu.roll(values, (-step) % values.shape[1], 1)
    return jnp.where(masks[(row_off, col_off)], moved, 0.0)


def tap_source(phase, tap_off):
    row, col = phase // 2 + tap_off[0], phase % 2 + tap_off[1]
    return (row % 2) * 2 + col % 2, row // 2, col // 2


TAPS = tuple((row - 1, col - 1) for row in range(3) for col in range(3))


def taps_on_lanes(source, out, masks, sign):
    for phase in range(4):
        for tap, off in enumerate(TAPS):
            other, row_off, col_off = tap_source(phase, (sign * off[0], sign * off[1]))
            out[8 * tap : 8 * tap + 8, phase * ROWS : (phase + 1) * ROWS] = lane_shift(
                source[:, other * ROWS : (other + 1) * ROWS], row_off, col_off, masks
            )


def down_wide(load, wide_one, wide_zero):
    clear_edges(wide_one)

    def body(phase, image, inside, row):
        at = pl.ds(PAD + inside, 64)
        for wide, row_phase in ((wide_one, 1), (wide_zero, 0)):
            right = load(row_phase * 2 + 1, row)
            left = load(row_phase * 2, row)
            wide[image, at, 0:C1] = row_shift(right, -1).astype(bf16)
            wide[image, at, C1 : 2 * C1] = left.astype(bf16)
            wide[image, at, 2 * C1 : 3 * C1] = right.astype(bf16)

    each_chunk(body)


def stem_forward(places, me, gathered, noisy, top, down, kern_down, stage, taps, wide_one, wide_zero):
    at = STEM_AT
    widen(gathered, places, me[0], stage)
    matrix_from(stage, at["kern_down"], kern_down, 9 * C1, C2)
    masks = lane_masks(ROWS)
    taps_on_lanes(noisy, taps, masks, 1)
    kern_in = jnp.concatenate(
        [
            jnp.concatenate([stage[3 * tap : 3 * tap + 3, :], jnp.zeros((5, LANES), f32)], axis=0)
            for tap in range(9)
        ],
        axis=0,
    ).astype(bf16)
    bias_in = stage[at["bias_in"] : at["bias_in"] + 1, :]
    for phase in range(4):
        top[phase] = mm_tn(taps[:, phase * ROWS : (phase + 1) * ROWS].astype(bf16), kern_in) + bias_in
    down_wide(lambda phase, row: top[phase, pl.ds(row, 64), :], wide_one, wide_zero)
    width = 3 * C1
    source = jnp.concatenate(
        [wide_rows(wide_one, -1, 0, width), wide_rows(wide_zero, 0, 0, width), wide_rows(wide_one, 0, 0, width)],
        axis=1,
    )
    down[...] = mm(source, kern_down[...]) + vector_at(stage, at["bias_down"], C2)


def stem_backward(leaving, me, noisy, top, skip, grad_down, kern_down, sent, out, taps, wide_one, wide_zero, wide_grad, low_grad):
    at = STEM_AT
    taps_on_lanes(noisy, taps, lane_masks(ROWS), 1)
    down_wide(lambda phase, row: top[phase, pl.ds(row, 64), :], wide_one, wide_zero)
    clear_edges(wide_grad)

    def body(phase, image, inside, row):
        value = grad_down[pl.ds(row, 64), :].astype(bf16).astype(f32)
        here = pl.ds(PAD + inside, 64)
        wide_grad[image, here, 0:C2] = value.astype(bf16)
        wide_grad[image, here, C2 : 2 * C2] = row_shift(value, 1).astype(bf16)

    each_chunk(body)
    bias_down = jnp.zeros((8, C2), f32)
    bias_down = lax.fori_loop(
        0,
        ROWS // 64,
        lambda n, c: c + fold(grad_down[pl.ds(pl.multiple_of(n * 64, 64), 64), :].astype(bf16).astype(f32)),
        bias_down,
    )
    vector_to(out, at["bias_down"], jnp.sum(bias_down, axis=0, keepdims=True))
    center = wide_rows(wide_grad, 0, 0, C2)
    width = 3 * C1
    for row_tap, (wide, row_off) in enumerate(((wide_one, -1), (wide_zero, 0), (wide_one, 0))):
        product = mm_tn(wide_rows(wide, row_off, 0, width), center)
        matrix_to(out, at["kern_down"] + row_tap * 2 * width, product)

    def taps_rows(first, count):
        return kern_down[first * C1 : (first + count) * C1, :]

    moved = wide_rows(wide_grad, 0, C2, 2 * C2)
    below = wide_rows(wide_grad, 1, 0, C2)
    below_moved = wide_rows(wide_grad, 1, C2, 2 * C2)
    first_pair = mm_nt(center, taps_rows(4, 2))
    second_pair = mm_nt(center, taps_rows(7, 2)) + mm_nt(below, taps_rows(1, 2))
    grads = (
        first_pair[:, :C1],
        first_pair[:, C1:] + mm_nt(moved, taps_rows(3, 1)),
        second_pair[:, :C1],
        second_pair[:, C1:] + mm_nt(moved, taps_rows(6, 1)) + mm_nt(below_moved, taps_rows(0, 1)),
    )
    bias_in = jnp.zeros((8, C1), f32)
    for phase in range(4):
        low_grad[phase] = (skip[phase] + grads[phase]).astype(bf16)
        bias_in = bias_in + fold(low_grad[phase].astype(f32))
    vector_to(out, at["bias_in"], jnp.sum(bias_in, axis=0, keepdims=True))
    kern_in = None
    for phase in range(4):
        part = mm(taps[:, phase * ROWS : (phase + 1) * ROWS].astype(bf16), low_grad[phase])
        kern_in = part if kern_in is None else kern_in + part
    for tap in range(9):
        out[3 * tap : 3 * tap + 3, :] = kern_in[8 * tap : 8 * tap + 3, :]
    out[at["end"] :, :] = jnp.zeros((STEM_ROWS - at["end"], LANES), f32)
    narrow_out(out, me[0], sent, leaving)


def res_forward(
    places, me, gathered, down, embed,
    inner, res_out, act_one, act_two, kern_first, kern_second, dense_two, hidden_pre, stats, gains,
    stage, dense_one, wide,
):
    at = RES_AT
    widen(gathered, places, me[0], stage)
    matrix_from(stage, at["dense_one"], dense_one, TDIM, TEMB)
    matrix_from(stage, at["dense_two"], dense_two, TEMB, C2)
    matrix_from(stage, at["kern_first"], kern_first, 9 * C2, C2)
    matrix_from(stage, at["kern_second"], kern_second, 9 * C2, C2)
    pre = jnp.dot(embed[...], dense_one[...].astype(f32), precision=highest) + vector_at(stage, at["bias_one"], TEMB)
    hidden_pre[...] = pre
    hidden = pre * logistic(pre)
    time_proj = jnp.dot(hidden, dense_two[...].astype(f32), precision=highest) + vector_at(stage, at["bias_two"], C2)
    ones = same_group(C2)
    clear_edges(wide)
    gain = vector_at(stage, at["gain_first"], C2)
    shift = vector_at(stage, at["shift_first"], C2)
    gain_two = vector_at(stage, at["gain_second"], C2)
    shift_two = vector_at(stage, at["shift_second"], C2)
    gains[...] = jnp.concatenate([gain, shift, gain_two, shift_two, jnp.zeros((4, C2), f32)], axis=0)

    def normalize(source, place, gain, shift, keep):
        center, scale = norm_stats(lambda phase, row: source[pl.ds(row, 64), :], 1, C2, ones)
        stats[place : place + IMGS, :] = center
        stats[place + IMGS : place + 2 * IMGS, :] = scale

        def body(phase, image, inside, row):
            value = (source[pl.ds(row, 64), :] - center[image : image + 1, :]) * scale[image : image + 1, :]
            value = value * gain + shift
            value = value * logistic(value)
            keep[pl.ds(row, 64), :] = value.astype(bf16)
            put_shifted(wide, image, inside, value.astype(bf16).astype(f32))

        each_chunk(body)

    normalize(down, 0, gain, shift, act_one)
    bias = vector_at(stage, at["bias_first"], C2)
    product = conv_low(wide, kern_first)
    for image in range(IMGS):
        inner[image * LOW : (image + 1) * LOW, :] = (
            product[image * LOW : (image + 1) * LOW, :] + bias + time_proj[image : image + 1, :]
        )
    normalize(inner, 2 * IMGS, gain_two, shift_two, act_two)
    res_out[...] = down[...] + conv_low(wide, kern_second) + vector_at(stage, at["bias_second"], C2)


def norm_back(load_grad, source, center, scale, gain, shift, ones, active, store):
    def pieces(image, row):
        xhat = (source[pl.ds(row, 64), :] - center[image : image + 1, :]) * scale[image : image + 1, :]
        grad = load_grad(row)
        if active:
            value = xhat * gain + shift
            gate = logistic(value)
            grad = grad * (gate * (1.0 + value * (1.0 - gate)))
        return grad, xhat

    def load(phase, image, row):
        grad, xhat = pieces(image, row)
        return grad, grad * xhat

    gain_grad, shift_grad, mean_one, mean_two = norm_back_stats(load, 1, C2, gain, ones)

    def body(phase, image, inside, row):
        grad, xhat = pieces(image, row)
        store(
            image,
            inside,
            row,
            scale[image : image + 1, :]
            * (grad * gain - mean_one[image : image + 1, :] - xhat * mean_two[image : image + 1, :]),
        )

    each_chunk(body)
    return gain_grad, shift_grad


def res_backward(
    leaving, me, grad_res, down, inner, act_one, act_two, kern_first, kern_second, dense_two, hidden_pre, stats, gains, embed,
    grad_down, sent, out,
    wide, grad_act,
):
    at = RES_AT
    ones = same_group(C2)
    clear_edges(wide)

    def lower(phase, image, inside, row):
        put_shifted(wide, image, inside, grad_res[pl.ds(row, 64), :].astype(bf16).astype(f32))

    each_chunk(lower)
    sums = image_sums(
        lambda phase, image, row: (grad_res[pl.ds(row, 64), :].astype(bf16).astype(f32),), 1, C2
    )[0]
    vector_to(out, at["bias_second"], jnp.sum(sums, axis=0, keepdims=True))
    grad_act[...] = conv_low_back(wide, kern_second)
    conv_low_grad(act_two, wide, out, at["kern_second"])

    def store_inner(image, inside, row, value):
        put_shifted(wide, image, inside, value.astype(bf16).astype(f32))

    gain_grad, shift_grad = norm_back(
        lambda row: grad_act[pl.ds(row, 64), :], inner, stats[8:12, :], stats[12:16, :],
        gains[2:3, :], gains[3:4, :], ones, True, store_inner,
    )
    vector_to(out, at["gain_second"], gain_grad)
    vector_to(out, at["shift_second"], shift_grad)
    inner_sum = jnp.concatenate(
        [
            jnp.sum(fold(wide[image, PAD : PAD + LOW, C2 : 2 * C2].astype(f32)), axis=0, keepdims=True)
            for image in range(IMGS)
        ]
        + [jnp.zeros((4, C2), f32)],
        axis=0,
    )
    time_sum = jnp.sum(inner_sum, axis=0, keepdims=True)
    vector_to(out, at["bias_first"], time_sum)
    vector_to(out, at["bias_two"], time_sum)
    pre = hidden_pre[...]
    gate = logistic(pre)
    contract = (((0,), (0,)), ((), ()))
    matrix_to(
        out, at["dense_two"],
        lax.dot_general(pre * gate, inner_sum, contract, precision=highest, preferred_element_type=f32),
    )
    grad_pre = lax.dot_general(
        inner_sum, dense_two[...].astype(f32), (((1,), (1,)), ((), ())), precision=highest, preferred_element_type=f32
    ) * (gate * (1.0 + pre * (1.0 - gate)))
    vector_to(out, at["bias_one"], jnp.sum(grad_pre, axis=0, keepdims=True))
    matrix_to(
        out, at["dense_one"],
        lax.dot_general(embed[...], grad_pre, contract, precision=highest, preferred_element_type=f32),
    )
    grad_act[...] = conv_low_back(wide, kern_first)
    conv_low_grad(act_one, wide, out, at["kern_first"])

    def store_down(image, inside, row, value):
        grad_down[pl.ds(row, 64), :] = value + grad_res[pl.ds(row, 64), :]

    gain_grad, shift_grad = norm_back(
        lambda row: grad_act[pl.ds(row, 64), :], down, stats[0:4, :], stats[4:8, :],
        gains[0:1, :], gains[1:2, :], ones, True, store_down,
    )
    vector_to(out, at["gain_first"], gain_grad)
    vector_to(out, at["shift_first"], shift_grad)
    out[at["end"] :, :] = jnp.zeros((RES_ROWS - at["end"], LANES), f32)
    narrow_out(out, me[0], sent, leaving)


def attn_forward(
    places, me, gathered, res_out,
    attn_low, normed, qkv, probs, mixed, kern_qkv, kern_proj, stats, gains,
    stage,
):
    at = ATTN_AT
    widen(gathered, places, me[0], stage)
    matrix_from(stage, at["kern_qkv"], kern_qkv, C2, 3 * C2)
    matrix_from(stage, at["kern_proj"], kern_proj, C2, C2)
    ones = same_group(C2)
    gain = vector_at(stage, at["gain_attn"], C2)
    shift = vector_at(stage, at["shift_attn"], C2)
    gains[...] = jnp.concatenate([gain, shift, jnp.zeros((6, C2), f32)], axis=0)
    center, scale = norm_stats(lambda phase, row: res_out[pl.ds(row, 64), :], 1, C2, ones)
    stats[0:IMGS, :] = center
    stats[IMGS : 2 * IMGS, :] = scale

    def body(phase, image, inside, row):
        value = (res_out[pl.ds(row, 64), :] - center[image : image + 1, :]) * scale[image : image + 1, :]
        normed[pl.ds(row, 64), :] = (value * gain + shift).astype(bf16)

    each_chunk(body)
    qkv[...] = mm(normed[...], kern_qkv[...]).astype(bf16)
    for image in range(IMGS):
        rows = slice(image * LOW, (image + 1) * LOW)
        logits = mm_nt(qkv[rows, 0:C2], qkv[rows, C2 : 2 * C2]) * C2 ** (-0.5)
        powers = jnp.exp(logits - jnp.max(logits, axis=1, keepdims=True))
        weights = powers / jnp.sum(powers, axis=1, keepdims=True)
        probs[image] = weights
        mixed[rows, :] = mm(weights.astype(bf16), qkv[rows, 2 * C2 : 3 * C2]).astype(bf16)
    attn_low[...] = (
        res_out[...] + mm(mixed[...], kern_proj[...]) + vector_at(stage, at["bias_proj"], C2)
    ).astype(bf16)


def attn_backward(
    leaving, me, grad_attn, res_out, normed, qkv, probs, mixed, kern_qkv, kern_proj, stats, gains,
    grad_res, sent, out,
    grad_qkv, grad_mixed, grad_normed, low,
):
    at = ATTN_AT
    ones = same_group(C2)
    low[...] = grad_attn[...].astype(bf16)
    sums = image_sums(lambda phase, image, row: (grad_attn[pl.ds(row, 64), :],), 1, C2)[0]
    vector_to(out, at["bias_proj"], jnp.sum(sums, axis=0, keepdims=True))
    matrix_to(out, at["kern_proj"], mm_tn(mixed[...], low[...]))
    grad_mixed[...] = mm_nt(low[...], kern_proj[...]).astype(bf16)
    scale_by = C2 ** (-0.5)
    for image in range(IMGS):
        rows = slice(image * LOW, (image + 1) * LOW)
        query, keys, value = (qkv[rows, part * C2 : (part + 1) * C2] for part in range(3))
        weights = probs[image]
        grad_probs = mm_nt(grad_mixed[rows, :], value)
        grad_qkv[rows, 2 * C2 : 3 * C2] = mm_tn(weights.astype(bf16), grad_mixed[rows, :]).astype(bf16)
        grad_logits = (
            weights * (grad_probs - jnp.sum(weights * grad_probs, axis=1, keepdims=True))
        ).astype(bf16)
        grad_qkv[rows, 0:C2] = (mm(grad_logits, keys) * scale_by).astype(bf16)
        grad_qkv[rows, C2 : 2 * C2] = (mm_tn(grad_logits, query) * scale_by).astype(bf16)
    matrix_to(out, at["kern_qkv"], mm_tn(normed[...], grad_qkv[...]))
    grad_normed[...] = mm_nt(grad_qkv[...], kern_qkv[...])

    def store(image, inside, row, value):
        grad_res[pl.ds(row, 64), :] = value + grad_attn[pl.ds(row, 64), :]

    gain_grad, shift_grad = norm_back(
        lambda row: grad_normed[pl.ds(row, 64), :], res_out, stats[0:4, :], stats[4:8, :],
        gains[0:1, :], gains[1:2, :], ones, False, store,
    )
    vector_to(out, at["gain_attn"], gain_grad)
    vector_to(out, at["shift_attn"], shift_grad)
    out[at["end"] :, :] = jnp.zeros((ATTN_ROWS - at["end"], LANES), f32)
    narrow_out(out, me[0], sent, leaving)


def pick(row, channel):
    lane = lax.broadcasted_iota(jnp.int32, (LANES, LANES), 0)
    ch = lax.broadcasted_iota(jnp.int32, (LANES, LANES), 1)
    return (row * LANES + lane == CIN * ch + channel).astype(f32).astype(bf16)


def head_step(
    places, leaving, me, gathered, attn_low, top, clean, factor,
    grad_attn, skip, loss, sent, out,
    stage, wide, kern_up, merged, act, taps, narrow, grad_wide_zero, grad_wide_one, boxes,
):
    at = HEAD_AT
    widen(gathered, places, me[0], stage)
    ones = same_group(C1)
    kern_up[...] = jnp.zeros(kern_up.shape, bf16)

    def combine(at_row):
        tap = [[stage[pl.ds((3 * a + b) * C2 + at_row, 64), :] for b in range(3)] for a in range(3)]
        by_row = {(0, 0): tap[0], (0, 1): [tap[1][b] + tap[2][b] for b in range(3)],
                  (1, 0): [tap[0][b] + tap[1][b] for b in range(3)], (1, 1): tap[2]}
        for (row_phase, slot), three in by_row.items():
            for col_off in range(3):
                base = (slot * 3 + col_off) * C2
                here = pl.ds(base + at_row, 64)
                if col_off == 0:
                    kern_up[row_phase, here, 0:C1] = three[0].astype(bf16)
                elif col_off == 1:
                    kern_up[row_phase, here, 0:C1] = (three[1] + three[2]).astype(bf16)
                    kern_up[row_phase, here, C1 : 2 * C1] = (three[0] + three[1]).astype(bf16)
                else:
                    kern_up[row_phase, here, C1 : 2 * C1] = three[2].astype(bf16)

    chunks(C2, 64, combine)
    clear_edges(wide)

    def spread_low(phase, image, inside, row):
        put_shifted(wide, image, inside, attn_low[pl.ds(row, 64), :].astype(f32))

    each_chunk(spread_low)
    bias_up = stage[at["bias_up"] : at["bias_up"] + 1, :]
    for row_phase in range(2):
        product = mm(
            jnp.concatenate(
                [wide_rows(wide, row_phase - 1, 0, 3 * C2), wide_rows(wide, row_phase, 0, 3 * C2)], axis=1
            ),
            kern_up[row_phase],
        )
        for col_phase in range(2):
            phase = row_phase * 2 + col_phase
            merged[phase] = product[:, col_phase * C1 : (col_phase + 1) * C1] + bias_up + top[phase]
    gain = stage[at["gain_out"] : at["gain_out"] + 1, :]
    shift = stage[at["shift_out"] : at["shift_out"] + 1, :]
    center, scale = norm_stats(lambda phase, row: merged[phase, pl.ds(row, 64), :], 4, C1, ones)

    def body(phase, image, inside, row):
        value = (merged[phase, pl.ds(row, 64), :] - center[image : image + 1, :]) * scale[image : image + 1, :]
        value = value * gain + shift
        act[phase, pl.ds(row, 64), :] = (value * logistic(value)).astype(bf16)

    each_chunk(body, 4)
    for channel in range(CIN):
        total = None
        for row in range(3):
            part = mm(stage[pl.ds(at["kern_out"] + row, 9, 3), :].astype(bf16), pick(row, channel))
            total = part if total is None else total + part
        narrow[pl.ds(channel, 9, 8), :] = total
    for channel in range(CIN, 8):
        narrow[pl.ds(channel, 9, 8), :] = jnp.zeros((9, LANES), f32)
    kern_out = narrow[...].astype(bf16)
    masks = lane_masks(ROWS)
    for phase in range(4):
        taps[:, phase * ROWS : (phase + 1) * ROWS] = mm_nt(kern_out, act[phase])
    lane = lax.broadcasted_iota(jnp.int32, (8, LANES), 1)
    channel_at = lax.broadcasted_iota(jnp.int32, (8, LANES), 0)
    bias_out = jnp.sum(
        jnp.where((lane == channel_at) & (channel_at < CIN), stage[at["bias_out"] : at["bias_out"] + 1, :], 0.0),
        axis=1,
        keepdims=True,
    )
    pixel_count = CIN * SIDE * SIDE
    loss_sum = jnp.zeros((8, ROWS), f32)
    bias_grad = jnp.zeros((8, 1), f32)
    grad_lanes = []
    for phase in range(4):
        predict = bias_out
        for tap, off in enumerate(TAPS):
            other, row_off, col_off = tap_source(phase, off)
            predict = predict + lane_shift(
                taps[8 * tap : 8 * tap + 8, other * ROWS : (other + 1) * ROWS], row_off, col_off, masks
            )
        error = predict - clean[:, phase * ROWS : (phase + 1) * ROWS]
        loss_sum = loss_sum + error * error * factor[...]
        grad = ((2.0 / pixel_count) * factor[...] * error).astype(bf16).astype(f32)
        bias_grad = bias_grad + jnp.sum(grad, axis=1, keepdims=True)
        grad_lanes.append(grad)
    loss[...] = jnp.sum(jnp.sum(loss_sum, axis=1, keepdims=True), axis=0, keepdims=True) * (1.0 / pixel_count)
    out[at["bias_out"] : at["bias_out"] + 1, :] = jnp.sum(
        jnp.where((lane == channel_at) & (channel_at < CIN), bias_grad, 0.0), axis=0, keepdims=True
    )
    for phase in range(4):
        for tap, off in enumerate(TAPS):
            other, row_off, col_off = tap_source(phase, (-off[0], -off[1]))
            taps[8 * tap : 8 * tap + 8, phase * ROWS : (phase + 1) * ROWS] = lane_shift(
                grad_lanes[other], row_off, col_off, masks
            )
    kern_grad = None
    for phase in range(4):
        low = taps[:, phase * ROWS : (phase + 1) * ROWS].astype(bf16)
        part = mm(low, act[phase])
        kern_grad = part if kern_grad is None else kern_grad + part
        skip[phase] = mm_tn(low, kern_out)
    narrow[...] = kern_grad
    for row in range(3):
        total = None
        for channel in range(CIN):
            pieces = parts_of(narrow[pl.ds(channel, 9, 8), :])
            part = sum(mm_nt(piece, pick(row, channel)) for piece in pieces)
            total = part if total is None else total + part
        out[pl.ds(at["kern_out"] + row, 9, 3), :] = total

    def pieces(phase, image, row):
        xhat = (merged[phase, pl.ds(row, 64), :] - center[image : image + 1, :]) * scale[image : image + 1, :]
        value = xhat * gain + shift
        gate = logistic(value)
        return skip[phase, pl.ds(row, 64), :] * (gate * (1.0 + value * (1.0 - gate))), xhat

    def load(phase, image, row):
        grad, xhat = pieces(phase, image, row)
        return grad, grad * xhat

    gain_grad, shift_grad, mean_one, mean_two = norm_back_stats(load, 4, C1, gain, ones)
    vector_to(out, at["gain_out"], gain_grad)
    vector_to(out, at["shift_out"], shift_grad)
    clear_edges(grad_wide_zero)
    clear_edges(grad_wide_one)
    clear_edges(boxes)
    wides = (grad_wide_zero, grad_wide_one)

    def back(phase, image, inside, row):
        for row_phase in range(2):
            pair = []
            for col_phase in range(2):
                phase = row_phase * 2 + col_phase
                grad, xhat = pieces(phase, image, row)
                value = scale[image : image + 1, :] * (
                    grad * gain - mean_one[image : image + 1, :] - xhat * mean_two[image : image + 1, :]
                )
                skip[phase, pl.ds(row, 64), :] = value
                pair.append(value.astype(bf16).astype(f32))
            put_shifted(wides[row_phase], image, inside, jnp.concatenate(pair, axis=1))
            here = pl.ds(PAD + inside, 64)
            base = row_phase * 3 * C1
            boxes[image, here, base : base + C1] = pair[1] + row_shift(pair[0], 1)
            boxes[image, here, base + C1 : base + 2 * C1] = pair[0] + pair[1]
            boxes[image, here, base + 2 * C1 : base + 3 * C1] = row_shift(pair[1], -1) + pair[0]

    each_chunk(back)
    bias_sum = jnp.zeros((8, C1), f32)
    for row_phase in range(2):
        for image in range(IMGS):
            both = fold(wides[row_phase][image, PAD : PAD + LOW, C2 : 2 * C2].astype(f32))
            bias_sum = bias_sum + both[:, :C1] + both[:, C1:]
    vector_to(out, at["bias_up"], jnp.sum(bias_sum, axis=0, keepdims=True))
    total = None
    for row_phase in range(2):
        for slot in range(2):
            base = slot * 3 * C2
            taps = [kern_up[row_phase, base + at * C2 : base + (at + 1) * C2, :] for at in (2, 1, 0)]
            part = mm_nt(wide_rows(wides[row_phase], 1 - row_phase - slot, 0, 3 * C2), jnp.concatenate(taps, axis=1))
            total = part if total is None else total + part
    grad_attn[...] = total
    width = 3 * C1

    def box_rows(row_off, row_phase):
        return boxes[
            :, PAD + 16 * row_off : PAD + 16 * row_off + LOW, row_phase * width : (row_phase + 1) * width
        ].reshape(ROWS, width)

    summed = (
        box_rows(0, 1) + box_rows(1, 0),
        box_rows(0, 0) + box_rows(0, 1),
        box_rows(-1, 1) + box_rows(0, 0),
    )
    for row_tap in range(3):
        product = mm_tn(attn_low[...], summed[row_tap].astype(bf16))
        for col_tap in range(3):
            tap = row_tap * 3 + col_tap
            out[tap * C2 : (tap + 1) * C2, :] = product[:, col_tap * C1 : (col_tap + 1) * C1]
    out[at["end"] :, :] = jnp.zeros((HEAD_ROWS - at["end"], LANES), f32)
    narrow_out(out, me[0], sent, leaving)


def sds(shape, dtype=f32):
    return jax.ShapeDtypeStruct(shape, dtype)


def run(body, scalars, ins, outs, scratch=(), limit=62):
    in_leaves, in_tree = jax.tree.flatten([*scalars, *ins])
    out_leaves, out_tree = jax.tree.flatten(outs)

    def kernel(*refs):
        split = len(in_leaves), len(in_leaves) + len(out_leaves)
        body(
            *jax.tree.unflatten(in_tree, refs[: split[0]]),
            *jax.tree.unflatten(out_tree, refs[split[0] : split[1]]),
            *refs[split[1] :],
        )

    whole = pl.BlockSpec(memory_space=pltpu.VMEM)
    scalar = pl.BlockSpec(memory_space=pltpu.SMEM)
    results = pl.pallas_call(
        kernel,
        out_shape=out_leaves,
        in_specs=[scalar] * len(scalars) + [whole] * (len(in_leaves) - len(scalars)),
        out_specs=[whole] * len(out_leaves),
        scratch_shapes=scratch,
        compiler_params=pltpu.CompilerParams(vmem_limit_bytes=limit * 2**20),
    )(*in_leaves)
    return jax.tree.unflatten(out_tree, results)


def wide_scratch(width, dtype=bf16):
    return pltpu.VMEM((IMGS, PADDED, width), dtype)


SAVED = dict(
    stage=((RES_ROWS, LANES), f32), block_out=((HEAD_ROWS, LANES), f32),
    taps=((72, 4 * ROWS), f32), low_taps=((72, 4 * ROWS), f32), narrow=((72, LANES), f32),
    top=((4, ROWS, C1), f32), down=((ROWS, C2), f32), inner=((ROWS, C2), f32), res_out=((ROWS, C2), f32),
    act_one=((ROWS, C2), bf16), act_two=((ROWS, C2), bf16), attn_low=((ROWS, C2), bf16), normed=((ROWS, C2), bf16),
    qkv=((ROWS, 3 * C2), bf16), probs=((IMGS, LOW, LOW), f32), mixed=((ROWS, C2), bf16),
    merged=((4, ROWS, C1), f32), act=((4, ROWS, C1), bf16), skip=((4, ROWS, C1), f32),
    grad_attn=((ROWS, C2), f32), grad_res=((ROWS, C2), f32), grad_act=((ROWS, C2), f32),
    grad_low=((ROWS, C2), bf16), grad_mixed=((ROWS, C2), bf16), grad_qkv=((ROWS, 3 * C2), bf16),
    dense_one=((TDIM, TEMB), bf16), dense_two=((TEMB, C2), bf16), kern_down=((9 * C1, C2), bf16),
    kern_first=((9 * C2, C2), bf16), kern_second=((9 * C2, C2), bf16), kern_qkv=((C2, 3 * C2), bf16),
    kern_proj=((C2, C2), bf16), kern_up=((2, 6 * C2, C2), bf16),
    hidden_pre=((8, TEMB), f32), res_stats=((16, C2), f32), res_gains=((8, C2), f32),
    attn_stats=((8, C2), f32), attn_gains=((8, C2), f32),
    wide=((IMGS, PADDED, 3 * C2), bf16), wide_zero=((IMGS, PADDED, 3 * C2), bf16),
    wide_one=((IMGS, PADDED, 3 * C2), bf16), boxes=((IMGS, PADDED, 6 * C1), f32),
)


class Named:
    def __init__(self, names, refs):
        self.__dict__.update(zip(names, refs))


def whole_step(places, leaving, me, gathered, noisy, clean, factor, embed, loss, sent, *refs):
    own = Named(SAVED, refs)
    stem_wide, stem_wide_zero = own.wide.at[:, :, 0 : 3 * C1], own.wide_zero.at[:, :, 0 : 3 * C1]
    stem_forward(
        places[0], me, gathered[0], noisy, own.top, own.down, own.kern_down, own.stage, own.taps, stem_wide, stem_wide_zero
    )
    res_forward(
        places[1], me, gathered[1], own.down, embed,
        own.inner, own.res_out, own.act_one, own.act_two, own.kern_first, own.kern_second, own.dense_two,
        own.hidden_pre, own.res_stats, own.res_gains,
        own.stage, own.dense_one, own.wide,
    )
    attn_forward(
        places[2], me, gathered[2], own.res_out,
        own.attn_low, own.normed, own.qkv, own.probs, own.mixed, own.kern_qkv, own.kern_proj,
        own.attn_stats, own.attn_gains,
        own.stage,
    )
    head_step(
        places[3], leaving[3], me, gathered[3], own.attn_low, own.top, clean, factor,
        own.grad_attn, own.skip, loss, sent[3], own.block_out,
        own.stage, own.wide, own.kern_up, own.merged, own.act, own.low_taps, own.narrow,
        own.wide_zero, own.wide_one, own.boxes,
    )
    attn_backward(
        leaving[2], me, own.grad_attn, own.res_out, own.normed, own.qkv, own.probs, own.mixed,
        own.kern_qkv, own.kern_proj, own.attn_stats, own.attn_gains,
        own.grad_res, sent[2], own.block_out.at[0:ATTN_ROWS],
        own.grad_qkv, own.grad_mixed, own.grad_act, own.grad_low,
    )
    res_backward(
        leaving[1], me, own.grad_res, own.down, own.inner, own.act_one, own.act_two, own.kern_first, own.kern_second,
        own.dense_two, own.hidden_pre, own.res_stats, own.res_gains, embed,
        own.grad_attn, sent[1], own.stage,
        own.wide, own.grad_act,
    )
    stem_backward(
        leaving[0], me, noisy, own.top, own.skip, own.grad_attn, own.kern_down, sent[0], own.block_out,
        own.taps, stem_wide, stem_wide_zero, own.wide_one.at[:, :, 0 : 2 * C2], own.act,
    )


def local_step(me, arrays, places, shapes, out_places, noisy, clean, factor, embed):
    def body(me, arrays, noisy, clean, factor, embed, loss, sent, *refs):
        gathered = [[arrays[place[0]] for place in block] for block in places]
        leaving = [[sent[place[0]] for place in block] for block in out_places]
        rest = [[place[1:] for place in block] for block in places]
        out_rest = [[place[1:] for place in block] for block in out_places]
        whole_step(rest, out_rest, me, gathered, noisy, clean, factor, embed, loss, leaving, *refs)

    return run(
        body,
        [me],
        [arrays, noisy, clean, factor, embed],
        [sds((1, 1)), shapes],
        [pltpu.VMEM(shape, dtype) for shape, dtype in SAVED.values()],
    )


def plan(step_counts, time_index, teacher_size):
    position = time_index % step_counts
    time_values = (2 * position + teacher_size).astype(f32) / (2 * step_counts).astype(f32)
    alpha_t = jnp.cos(0.5 * math.pi * time_values)
    sigma_t = jnp.sin(0.5 * math.pi * time_values)
    weight = jnp.maximum(alpha_t * alpha_t / (sigma_t * sigma_t), 1.0)
    return (time_values, alpha_t, sigma_t, weight)


def sinusoid(time_values):
    half_dim = TDIM // 2
    frequency = jnp.exp(-math.log(10000.0) * jnp.arange(half_dim, dtype=f32) / half_dim)
    angles = 1000.0 * time_values[:, None] * frequency[None, :]
    return jnp.concatenate([jnp.sin(angles), jnp.cos(angles)], axis=1)


def arrange(clean_images, noise_field, levels):
    def body(levels, clean, noise, noisy_out, clean_out, factor_out):
        image = lax.broadcasted_iota(jnp.int32, (IMGS, 1), 0)

        def column(kind):
            value = jnp.zeros((IMGS, 1), f32)
            for number in range(IMGS):
                value = jnp.where(image == number, levels[kind, number], value)
            return value

        alpha, sigma = column(1), column(2)
        mixed = [(alpha * clean[c] + sigma * noise[c]).astype(bf16).astype(f32) for c in range(CIN)]
        pieces = [piece.astype(f32) for piece in parts_of(jnp.concatenate([clean[c] for c in range(CIN)], axis=0))]
        rows = jnp.concatenate(mixed + pieces, axis=0).astype(bf16)
        held = CIN * IMGS
        noisy_out[...] = jnp.zeros(noisy_out.shape, f32)
        clean_out[...] = jnp.zeros(clean_out.shape, f32)
        for phase in range(4):
            place = lax.broadcasted_iota(jnp.int32, (SIDE * SIDE, LOW), 1)
            source = ((place >> 4) * 2 + phase // 2) * SIDE + (place & 15) * 2 + phase % 2
            chosen = lax.broadcasted_iota(jnp.int32, (SIDE * SIDE, LOW), 0) == source
            moved = mm(rows, chosen.astype(f32).astype(bf16))
            exact = moved[held : 2 * held] + moved[2 * held : 3 * held] + moved[3 * held : 4 * held]
            for number in range(IMGS):
                lanes = slice(phase * ROWS + number * LOW, phase * ROWS + (number + 1) * LOW)
                for c in range(CIN):
                    at = c * IMGS + number
                    noisy_out[c : c + 1, lanes] = moved[at : at + 1]
                    clean_out[c : c + 1, lanes] = exact[at : at + 1]
        for number in range(IMGS):
            factor_out[:, number * LOW : (number + 1) * LOW] = jnp.full((1, LOW), levels[0, number], f32)

    return run(
        body,
        [levels],
        [clean_images.transpose(1, 0, 2), noise_field.transpose(1, 0, 2)],
        [sds((8, 4 * ROWS)), sds((8, 4 * ROWS)), sds((1, ROWS))],
        limit=12,
    )


def prepare(clean_images, noise_field, step_counts, time_index, teacher_size, image_count):
    time_values, alpha_t, sigma_t, weight = plan(step_counts, time_index, teacher_size)
    live_mask = (jnp.arange(clean_images.shape[0], dtype=jnp.int32) < image_count).astype(f32)
    levels = jnp.stack([live_mask * weight, alpha_t, sigma_t], axis=0)
    embed = jnp.pad(sinusoid(time_values), ((0, 8 - IMGS), (0, 0)))
    return [*arrange(clean_images, noise_field, levels), embed]


AXES = ("dp", "fsdp")
BLOCK_ROWS = (STEM_ROWS, RES_ROWS, ATTN_ROWS, HEAD_ROWS)
SHARD_ROWS = (80, 344, 72, 80)
SPAN = 32
PARTS = (
    ((0, 0, 80), (1, 32, 184)),
    ((1, 184, 344), (2, 0, 72)),
    ((3, 0, 80), (1, 0, 32)),
)
PART_ROWS = tuple(sum(hi - lo for _, lo, hi in members) for members in PARTS)
TURNS = ((2, 4), (4, 2))
PLANE = (0, 2, 4, 6)
LINE = (0, 8, 16, 24)


def swap(values, mask):
    return lax.ppermute(values, AXES, [(here, here ^ mask) for here in range(SPAN)])


def pack_rows(masters):
    def body(refs, out):
        at = 0
        for members in PARTS:
            for block, lo, hi in members:
                out[at : at + hi - lo, :] = refs[block][lo:hi, :].astype(bf16)
                at += hi - lo

    return run(body, [], [masters], [sds((sum(PART_ROWS), LANES), bf16)], limit=8)[0]


def part_places(number, array, masks):
    at, found = 0, []
    for block, lo, hi in PARTS[number]:
        found.append((block, (array, masks, at, at + hi - lo, SHARD_ROWS[block], lo)))
        at += hi - lo
    return found


def gather_parts(own, prepared):
    split = sum(PART_ROWS[:2])
    *images, embed = prepared
    line = [own[:split]] + [swap(own[:split], mask) for mask in LINE[1:]]
    near = jnp.stack([own[split:], swap(own[split:], PLANE[1])], axis=0)
    near = jnp.concatenate([near, swap(near, PLANE[2])], axis=0)
    arrays, places = [], [[] for _ in SHARD_ROWS]

    def add(number, array, masks):
        for block, place in part_places(number, len(arrays), masks):
            places[block].append(place)
        arrays.append(array)

    held = []
    for number, (last, first) in enumerate(TURNS):
        begin = number * PART_ROWS[0]
        piece = jnp.stack([rows[begin : begin + PART_ROWS[number]] for rows in line], axis=0)
        held.append(jnp.concatenate([piece, swap(piece, first)], axis=0))
    held, near, images = lax.optimization_barrier((held, near, images))
    far = [swap(held[number], last) for number, (last, first) in enumerate(TURNS)]
    third = jnp.concatenate([near] + [swap(near, mask) for mask in LINE[1:]], axis=0)
    far, third, embed = lax.optimization_barrier((far, third, embed))
    for number, (last, first) in enumerate(TURNS):
        masks = [a ^ b for a in (0, first) for b in LINE]
        add(number, held[number], masks)
        add(number, far[number], [mask ^ last for mask in masks])
        add(number, swap(held[number], 1), [mask ^ 1 for mask in masks])
        add(number, swap(far[number], 1), [mask ^ last ^ 1 for mask in masks])
    masks = [a ^ b for b in LINE for a in PLANE]
    add(2, third, masks)
    add(2, swap(third, 1), [mask ^ 1 for mask in masks])
    return arrays, places, (*images, embed)


def leaving_parts():
    shapes, places = [], [[] for _ in SHARD_ROWS]

    def add(number, masks):
        for block, place in part_places(number, len(shapes), masks):
            places[block].append(place)
        shapes.append(sds((len(masks), PART_ROWS[number], LANES), bf16))

    for number, (first, last) in enumerate(TURNS):
        for core in (0, 1):
            for side in (0, first):
                add(number, [core ^ side ^ a ^ b for a in (0, last) for b in LINE])
    for core in (0, 1):
        add(2, [core ^ a ^ b for b in LINE for a in PLANE])
    return shapes, places


def reduce_parts(leaving):
    totals = []
    crossed = [[None, None], [None, None]]
    for side in (1, 0):
        for number in (0, 1):
            kept, sent = leaving[4 * number + side], leaving[4 * number + 2 + side]
            crossed[number][side] = kept.astype(f32) + swap(sent, 1).astype(f32)
    third = leaving[8].astype(f32) + swap(leaving[9], 1).astype(f32)
    crossed, third = lax.optimization_barrier((crossed, third))
    arrived = [swap(third[4 * at : 4 * at + 4].astype(bf16), mask) for at, mask in enumerate(LINE) if mask]
    third = third[:4] + sum(piece.astype(f32) for piece in arrived)
    for number, (first, last) in enumerate(TURNS):
        near, far = crossed[number]
        totals.append(near + swap(far.astype(bf16), first).astype(f32))
    totals, third = lax.optimization_barrier((totals, third))
    for number, (first, last) in enumerate(TURNS):
        total = totals[number]
        totals[number] = total[:4] + swap(total[4:].astype(bf16), last).astype(f32)
    whole = jnp.concatenate(totals, axis=1)
    return [
        [array[0]] + [swap(array[at].astype(bf16), mask) for at, mask in enumerate(masks) if mask]
        for array, masks in ((whole, LINE), (third, PLANE))
    ]


def last_sum(image_counts, count, loss, groups):
    def body(live, loss, groups, total, row):
        square, at = jnp.zeros((8, LANES), f32), 0
        for pieces in groups:
            value = pieces[0][...].astype(f32)
            for piece in pieces[1:]:
                value = value + piece[...].astype(f32)
            total[at : at + value.shape[0], :] = value
            at += value.shape[0]
            square = square + fold(value * value)
        square = jnp.sum(jnp.sum(square, axis=0, keepdims=True), axis=1, keepdims=True)
        lane = lax.broadcasted_iota(jnp.int32, (1, LANES), 1)
        scalars = jnp.where(lane == 0, loss[...], jnp.where(lane == 1, square, live[0].astype(f32)))
        row[...] = jnp.broadcast_to(scalars[None], row.shape)

    rows = sum(pieces[0].shape[0] for pieces in groups)
    return run(body, [image_counts], [loss, groups], [sds((rows, LANES)), sds((count, 1, LANES))], limit=16)


def update(adam_step, arrived, gradient, masters, firsts, seconds, places):
    def body(step, arrived, gradient, masters, firsts, seconds, loss, norm, outs):
        sums = jnp.sum(arrived[...], axis=0)
        live = 1.0 / sums[:, 2:3]
        loss[...] = sums[:, 0:1] * live
        size = jnp.sqrt(sums[:, 1:2]) * live
        norm[...] = size
        scale = clip_limit / jnp.maximum(size, clip_limit) * live
        powers = lax.fori_loop(
            0, step[0], lambda _, held: (held[0] * beta_one, held[1] * beta_two), (jnp.float32(1.0), jnp.float32(1.0))
        )
        fix_one, fix_two = 1.0 - powers[0], 1.0 - powers[1]
        at = 0
        for block, lo, hi in places:
            grad = gradient[at : at + hi - lo, :] * scale
            at += hi - lo
            master, first, second = (refs[block][lo:hi, :] for refs in (masters, firsts, seconds))
            first_new = beta_one * first + (1.0 - beta_one) * grad
            second_new = beta_two * second + (1.0 - beta_two) * grad * grad
            master_new = master - learn_rate * (
                first_new / fix_one / (jnp.sqrt(second_new / fix_two) + adam_eps) + decay_rate * master
            )
            for ref, value in zip(outs[block], (master_new, first_new, second_new, master_new.astype(bf16))):
                ref[lo:hi, :] = value

    shapes = [[sds(m.shape), sds(m.shape), sds(m.shape), sds(m.shape, bf16)] for m in masters]
    return run(
        body, [adam_step], [arrived, gradient, masters, firsts, seconds], [sds((1, 1)), sds((1, 1)), shapes], limit=24
    )


def gather_whole(shards):
    arrays = [
        lax.all_gather(shard.reshape(-1), AXES, axis=0, tiled=True).reshape(1, rows, LANES)
        for shard, rows in zip(shards, BLOCK_ROWS)
    ]
    return arrays, [[(block, (0,), 0, rows, 0, 0)] for block, rows in enumerate(BLOCK_ROWS)]


def leaving_whole():
    shapes = [sds((1, rows, LANES), bf16) for rows in BLOCK_ROWS]
    return shapes, [[(block, (0,), 0, rows, 0, 0)] for block, rows in enumerate(BLOCK_ROWS)]


def reduce_whole(leaving):
    sums = [
        lax.psum_scatter(array.astype(f32).reshape(-1), AXES, scatter_dimension=0, tiled=True) for array in leaving
    ]
    return [[jnp.concatenate([one.reshape(-1, LANES) for one in sums], axis=0)]]


def per_device(
    clean_images, noise_field, step_counts, time_index, teacher_size, image_counts, adam_step,
    stem_master, stem_first, stem_second, res_master, res_first, res_second,
    attn_master, attn_first, attn_second, head_master, head_first, head_second,
):
    blocks = [
        [block.reshape(-1, LANES) for block in state]
        for state in (
            (stem_master, res_master, attn_master, head_master),
            (stem_first, res_first, attn_first, head_first),
            (stem_second, res_second, attn_second, head_second),
        )
    ]
    masters = blocks[0]
    count = lax.axis_size(AXES)
    me = lax.axis_index(AXES).astype(jnp.int32).reshape(1)
    laid_out = count == SPAN and tuple(master.shape[0] for master in masters) == SHARD_ROWS
    prepared = prepare(clean_images, noise_field, step_counts, time_index, teacher_size, image_counts[0])
    if laid_out:
        arrays, places, prepared = gather_parts(pack_rows(masters), prepared)
        shapes, out_places = leaving_parts()
        order = [member for members in PARTS for member in members]
    else:
        arrays, places = gather_whole([master.astype(bf16) for master in masters])
        shapes, out_places = leaving_whole()
        order = [(block, 0, master.shape[0]) for block, master in enumerate(masters)]
    loss, leaving = local_step(me, arrays, places, shapes, out_places, *prepared)
    pieces = reduce_parts(leaving) if laid_out else reduce_whole(leaving)
    gradient, row = last_sum(image_counts, count, loss, pieces)
    arrived = lax.all_to_all(row, AXES, 0, 0, tiled=True)
    loss, norm, outs = update(adam_step, arrived, gradient, *blocks, order)
    return (loss[0, 0], norm[0, 0]) + tuple(value.reshape(-1) for block in outs for value in block)


def solution(mesh):
    split = P(("dp", "fsdp"))
    images = P(("dp", "fsdp"), None, None)
    return jax.shard_map(
        per_device,
        mesh=mesh,
        in_specs=(images, images, split, split, split, split, P()) + (split,) * 12,
        out_specs=(P(), P()) + (split,) * 16,
        check_vma=False,
    )
```

```python
from functools import partial
import math

import jax
import jax.numpy as jnp
from jax import lax
from jax.experimental import pallas as pl
from jax.experimental.pallas import tpu as pltpu
from jax.sharding import PartitionSpec as P

C1 = 128
C2 = 256
GROUPS = 32
TDIM = 128
TEMB = 512
CIN = 3
SIDE = 32
LANES = 128
IMGS = 4
LOW = 256
ROWS = IMGS * LOW
PAD = 16
PADDED = LOW + 2 * PAD

clip_limit = 0.05
learn_rate = 0.05
beta_one = 0.9
beta_two = 0.999
adam_eps = 1e-08
decay_rate = 0.01
norm_eps = 1e-05

f32 = jnp.float32
bf16 = jnp.bfloat16
highest = lax.Precision.HIGHEST

STEM_ROWS, RES_ROWS, ATTN_ROWS, HEAD_ROWS = 2560, 11008, 2304, 2560

STEM_AT = dict(kern_in=0, bias_in=27, kern_down=28, bias_down=2332, end=2334)
RES_AT = dict(
    dense_one=0, bias_one=512, dense_two=516, bias_two=1540, gain_first=1542, shift_first=1544,
    kern_first=1546, bias_first=6154, gain_second=6156, shift_second=6158, kern_second=6160,
    bias_second=10768, end=10770,
)
ATTN_AT = dict(gain_attn=0, shift_attn=2, kern_qkv=4, kern_proj=1540, bias_proj=2052, end=2054)
HEAD_AT = dict(kern_up=0, bias_up=2304, gain_out=2305, shift_out=2306, kern_out=2307, bias_out=2334, end=2335)


def mm(a, b):
    return jnp.dot(a, b, preferred_element_type=f32)


def mm_nt(a, b):
    return lax.dot_general(a, b, (((1,), (1,)), ((), ())), preferred_element_type=f32)


def mm_tn(a, b):
    return lax.dot_general(a, b, (((0,), (0,)), ((), ())), preferred_element_type=f32)


def parts_of(values):
    high = values.astype(bf16)
    rest = values - high.astype(f32)
    middle = rest.astype(bf16)
    return high, middle, (rest - middle.astype(f32)).astype(bf16)


def mm_exact(values, matrix):
    count = values.shape[0]
    rows = jnp.concatenate([piece.astype(f32) for piece in parts_of(values)], axis=0).astype(bf16)
    product = mm(rows, matrix)
    return product[:count] + product[count : 2 * count] + product[2 * count :]


def same_group(channels):
    size = channels // GROUPS
    down_at = lax.broadcasted_iota(jnp.int32, (channels, channels), 0) // size
    across = lax.broadcasted_iota(jnp.int32, (channels, channels), 1) // size
    return (down_at == across).astype(f32).astype(bf16)


def row_shift(values, step):
    count = values.shape[0]
    moved = pltpu.roll(values, (-step) % count, 0)
    column = lax.broadcasted_iota(jnp.int32, values.shape, 0) & 15
    return jnp.where(column == (0 if step < 0 else 15), 0.0, moved)


def chunks(total, size, body):
    def step(number, carry):
        body(pl.multiple_of(number * size, size))
        return carry

    lax.fori_loop(0, total // size, step, 0, unroll=True)


def widen(pieces, places, me, stage):
    for ref, (masks, lo, hi, per_shard, begin) in zip(pieces, places):
        for number, mask in enumerate(masks):
            owner = me ^ mask
            at = pl.multiple_of(owner * per_shard + begin, 8)
            stage[pl.ds(at, hi - lo), :] = ref[number, lo:hi, :].astype(f32)


def narrow_out(stage, me, outs, places):
    for ref, (masks, lo, hi, per_shard, begin) in zip(outs, places):
        for number, mask in enumerate(masks):
            owner = me ^ mask
            at = pl.multiple_of(owner * per_shard + begin, 8)
            ref[number, lo:hi, :] = stage[pl.ds(at, hi - lo), :].astype(ref.dtype)


def matrix_from(stage, base, out, depth, width):
    lanes = width // LANES

    def copy(at):
        for lane in range(lanes):
            out[pl.ds(at, 128), lane * LANES : (lane + 1) * LANES] = stage[
                pl.ds(base + lanes * at + lane, 128, lanes), :
            ].astype(bf16)

    chunks(depth, 128, copy)


def matrix_to(out, base, value):
    depth, width = value.shape
    lanes = width // LANES
    for lane in range(lanes):
        out[pl.ds(base + lane, depth, lanes), :] = value[:, lane * LANES : (lane + 1) * LANES]


def vector_at(stage, base, width):
    return jnp.concatenate([stage[base + lane : base + lane + 1, :] for lane in range(width // LANES)], axis=1)


def vector_to(out, base, value):
    for lane in range(value.shape[1] // LANES):
        out[base + lane : base + lane + 1, :] = value[:, lane * LANES : (lane + 1) * LANES]


def fold(values):
    return jnp.sum(values.reshape(values.shape[0] // 8, 8, values.shape[1]), axis=0)


def image_sums(load, phases, width, count=1):
    sums = []
    for image in range(IMGS):
        def step(number, carry):
            row = pl.multiple_of(image * LOW + number * 64, 64)
            for phase in range(phases):
                carry = tuple(c + fold(v) for c, v in zip(carry, load(phase, image, row)))
            return carry

        carry = lax.fori_loop(0, 4, step, tuple(jnp.zeros((8, width), f32) for _ in range(count)), unroll=True)
        sums.append([jnp.sum(c, axis=0, keepdims=True) for c in carry])
    return [jnp.concatenate(list(group), axis=0) for group in zip(*sums)]


def norm_stats(load, phases, width, ones):
    count = LOW * phases * (width // GROUPS)
    (total,) = image_sums(lambda phase, image, row: (load(phase, row),), phases, width)
    center = mm_exact(total, ones) * (1.0 / count)

    def squares(phase, image, row):
        away = load(phase, row) - center[image : image + 1, :]
        return (away * away,)

    (total,) = image_sums(squares, phases, width)
    spread = mm_exact(total, ones) * (1.0 / count)
    return center, lax.rsqrt(spread + norm_eps)


def norm_back_stats(load, phases, width, gain, ones):
    count = LOW * phases * (width // GROUPS)
    shift_sum, gain_sum = image_sums(load, phases, width, 2)
    means = mm_exact(jnp.concatenate([shift_sum * gain, gain_sum * gain], axis=0), ones) * (1.0 / count)
    return (
        jnp.sum(gain_sum, axis=0, keepdims=True),
        jnp.sum(shift_sum, axis=0, keepdims=True),
        means[:IMGS],
        means[IMGS:],
    )


def logistic(values):
    return 0.5 * jnp.tanh(0.5 * values) + 0.5


def each_chunk(body, phases=1, size=64):
    for image in range(IMGS):
        def step(number, carry):
            inside = pl.multiple_of(number * size, size)
            for phase in range(phases):
                body(phase, image, inside, image * LOW + inside)
            return carry

        lax.fori_loop(0, LOW // size, step, 0, unroll=True)


def clear_edges(wide):
    for image in range(IMGS):
        wide[image, 0:PAD, :] = jnp.zeros((PAD, wide.shape[2]), wide.dtype)
        wide[image, PAD + LOW : PADDED, :] = jnp.zeros((PAD, wide.shape[2]), wide.dtype)


def put_shifted(wide, image, inside, value):
    width = value.shape[1]
    at = pl.ds(PAD + inside, value.shape[0])
    wide[image, at, 0:width] = row_shift(value, -1).astype(bf16)
    wide[image, at, width : 2 * width] = value.astype(bf16)
    wide[image, at, 2 * width : 3 * width] = row_shift(value, 1).astype(bf16)


def wide_rows(wide, row_off, lo, hi):
    begin = PAD + 16 * row_off
    return wide[:, begin : begin + LOW, lo:hi].reshape(ROWS, hi - lo)


def conv_low(wide, kern):
    width = wide.shape[2]
    total = None
    for tap in range(3):
        part = mm(wide_rows(wide, tap - 1, 0, width), kern[tap * width : (tap + 1) * width, :])
        total = part if total is None else total + part
    return total


def conv_low_back(wide, kern):
    total = None
    for row_tap in range(3):
        taps = [kern[(row_tap * 3 + col_tap) * C2 : (row_tap * 3 + col_tap + 1) * C2, :] for col_tap in (2, 1, 0)]
        part = mm_nt(wide_rows(wide, 1 - row_tap, 0, 3 * C2), jnp.concatenate(taps, axis=1))
        total = part if total is None else total + part
    return total


def conv_low_grad(source, wide, out, base):
    for row_tap in range(3):
        product = mm_tn(source[...], wide_rows(wide, 1 - row_tap, 0, 3 * C2))
        for col_tap in range(3):
            tap = row_tap * 3 + col_tap
            matrix_to(out, base + tap * 2 * C2, product[:, (2 - col_tap) * C2 : (3 - col_tap) * C2])


def lane_masks(width):
    place = lax.broadcasted_iota(jnp.int32, (8, width), 1)
    row, column = (place >> 4) & 15, place & 15

    def valid(row_off, col_off):
        keep = None
        for at, off in ((row, row_off), (column, col_off)):
            if off:
                inside = at != (0 if off < 0 else 15)
                keep = inside if keep is None else keep & inside
        return keep

    return {(r, c): valid(r, c) for r in (-1, 0, 1) for c in (-1, 0, 1)}


def lane_shift(values, row_off, col_off, masks):
    step = 16 * row_off + col_off
    if step == 0:
        return values
    moved = pltpu.roll(values, (-step) % values.shape[1], 1)
    return jnp.where(masks[(row_off, col_off)], moved, 0.0)


def tap_source(phase, tap_off):
    row, col = phase // 2 + tap_off[0], phase % 2 + tap_off[1]
    return (row % 2) * 2 + col % 2, row // 2, col // 2


TAPS = tuple((row - 1, col - 1) for row in range(3) for col in range(3))


def taps_on_lanes(source, out, masks, sign):
    for phase in range(4):
        for tap, off in enumerate(TAPS):
            other, row_off, col_off = tap_source(phase, (sign * off[0], sign * off[1]))
            out[8 * tap : 8 * tap + 8, phase * ROWS : (phase + 1) * ROWS] = lane_shift(
                source[:, other * ROWS : (other + 1) * ROWS], row_off, col_off, masks
            )


def down_wide(load, wide_one, wide_zero):
    clear_edges(wide_one)

    def body(phase, image, inside, row):
        at = pl.ds(PAD + inside, 64)
        for wide, row_phase in ((wide_one, 1), (wide_zero, 0)):
            right = load(row_phase * 2 + 1, row)
            left = load(row_phase * 2, row)
            wide[image, at, 0:C1] = row_shift(right, -1).astype(bf16)
            wide[image, at, C1 : 2 * C1] = left.astype(bf16)
            wide[image, at, 2 * C1 : 3 * C1] = right.astype(bf16)

    each_chunk(body)


def stem_forward(places, me, gathered, noisy, top, down, kern_down, stage, taps, wide_one, wide_zero):
    at = STEM_AT
    widen(gathered, places, me[0], stage)
    matrix_from(stage, at["kern_down"], kern_down, 9 * C1, C2)
    masks = lane_masks(ROWS)
    taps_on_lanes(noisy, taps, masks, 1)
    kern_in = jnp.concatenate(
        [
            jnp.concatenate([stage[3 * tap : 3 * tap + 3, :], jnp.zeros((5, LANES), f32)], axis=0)
            for tap in range(9)
        ],
        axis=0,
    ).astype(bf16)
    bias_in = stage[at["bias_in"] : at["bias_in"] + 1, :]
    for phase in range(4):
        top[phase] = mm_tn(taps[:, phase * ROWS : (phase + 1) * ROWS].astype(bf16), kern_in) + bias_in
    down_wide(lambda phase, row: top[phase, pl.ds(row, 64), :], wide_one, wide_zero)
    width = 3 * C1
    source = jnp.concatenate(
        [wide_rows(wide_one, -1, 0, width), wide_rows(wide_zero, 0, 0, width), wide_rows(wide_one, 0, 0, width)],
        axis=1,
    )
    down[...] = mm(source, kern_down[...]) + vector_at(stage, at["bias_down"], C2)


def stem_backward(leaving, me, noisy, top, skip, grad_down, kern_down, sent, out, taps, wide_one, wide_zero, wide_grad, low_grad):
    at = STEM_AT
    taps_on_lanes(noisy, taps, lane_masks(ROWS), 1)
    down_wide(lambda phase, row: top[phase, pl.ds(row, 64), :], wide_one, wide_zero)
    clear_edges(wide_grad)

    def body(phase, image, inside, row):
        value = grad_down[pl.ds(row, 64), :].astype(bf16).astype(f32)
        here = pl.ds(PAD + inside, 64)
        wide_grad[image, here, 0:C2] = value.astype(bf16)
        wide_grad[image, here, C2 : 2 * C2] = row_shift(value, 1).astype(bf16)

    each_chunk(body)
    bias_down = jnp.zeros((8, C2), f32)
    bias_down = lax.fori_loop(
        0,
        ROWS // 64,
        lambda n, c: c + fold(grad_down[pl.ds(pl.multiple_of(n * 64, 64), 64), :].astype(bf16).astype(f32)),
        bias_down,
    )
    vector_to(out, at["bias_down"], jnp.sum(bias_down, axis=0, keepdims=True))
    center = wide_rows(wide_grad, 0, 0, C2)
    width = 3 * C1
    for row_tap, (wide, row_off) in enumerate(((wide_one, -1), (wide_zero, 0), (wide_one, 0))):
        product = mm_tn(wide_rows(wide, row_off, 0, width), center)
        matrix_to(out, at["kern_down"] + row_tap * 2 * width, product)

    def taps_rows(first, count):
        return kern_down[first * C1 : (first + count) * C1, :]

    moved = wide_rows(wide_grad, 0, C2, 2 * C2)
    below = wide_rows(wide_grad, 1, 0, C2)
    below_moved = wide_rows(wide_grad, 1, C2, 2 * C2)
    first_pair = mm_nt(center, taps_rows(4, 2))
    second_pair = mm_nt(center, taps_rows(7, 2)) + mm_nt(below, taps_rows(1, 2))
    grads = (
        first_pair[:, :C1],
        first_pair[:, C1:] + mm_nt(moved, taps_rows(3, 1)),
        second_pair[:, :C1],
        second_pair[:, C1:] + mm_nt(moved, taps_rows(6, 1)) + mm_nt(below_moved, taps_rows(0, 1)),
    )
    bias_in = jnp.zeros((8, C1), f32)
    for phase in range(4):
        low_grad[phase] = (skip[phase] + grads[phase]).astype(bf16)
        bias_in = bias_in + fold(low_grad[phase].astype(f32))
    vector_to(out, at["bias_in"], jnp.sum(bias_in, axis=0, keepdims=True))
    kern_in = None
    for phase in range(4):
        part = mm(taps[:, phase * ROWS : (phase + 1) * ROWS].astype(bf16), low_grad[phase])
        kern_in = part if kern_in is None else kern_in + part
    for tap in range(9):
        out[3 * tap : 3 * tap + 3, :] = kern_in[8 * tap : 8 * tap + 3, :]
    out[at["end"] :, :] = jnp.zeros((STEM_ROWS - at["end"], LANES), f32)
    narrow_out(out, me[0], sent, leaving)


def res_forward(
    places, me, gathered, down, embed,
    inner, res_out, act_one, act_two, kern_first, kern_second, dense_two, hidden_pre, stats, gains,
    stage, dense_one, wide,
):
    at = RES_AT
    widen(gathered, places, me[0], stage)
    matrix_from(stage, at["dense_one"], dense_one, TDIM, TEMB)
    matrix_from(stage, at["dense_two"], dense_two, TEMB, C2)
    matrix_from(stage, at["kern_first"], kern_first, 9 * C2, C2)
    matrix_from(stage, at["kern_second"], kern_second, 9 * C2, C2)
    pre = jnp.dot(embed[...], dense_one[...].astype(f32), precision=highest) + vector_at(stage, at["bias_one"], TEMB)
    hidden_pre[...] = pre
    hidden = pre * logistic(pre)
    time_proj = jnp.dot(hidden, dense_two[...].astype(f32), precision=highest) + vector_at(stage, at["bias_two"], C2)
    ones = same_group(C2)
    clear_edges(wide)
    gain = vector_at(stage, at["gain_first"], C2)
    shift = vector_at(stage, at["shift_first"], C2)
    gain_two = vector_at(stage, at["gain_second"], C2)
    shift_two = vector_at(stage, at["shift_second"], C2)
    gains[...] = jnp.concatenate([gain, shift, gain_two, shift_two, jnp.zeros((4, C2), f32)], axis=0)

    def normalize(source, place, gain, shift, keep):
        center, scale = norm_stats(lambda phase, row: source[pl.ds(row, 64), :], 1, C2, ones)
        stats[place : place + IMGS, :] = center
        stats[place + IMGS : place + 2 * IMGS, :] = scale

        def body(phase, image, inside, row):
            value = (source[pl.ds(row, 64), :] - center[image : image + 1, :]) * scale[image : image + 1, :]
            value = value * gain + shift
            value = value * logistic(value)
            keep[pl.ds(row, 64), :] = value.astype(bf16)
            put_shifted(wide, image, inside, value.astype(bf16).astype(f32))

        each_chunk(body)

    normalize(down, 0, gain, shift, act_one)
    bias = vector_at(stage, at["bias_first"], C2)
    product = conv_low(wide, kern_first)
    for image in range(IMGS):
        inner[image * LOW : (image + 1) * LOW, :] = (
            product[image * LOW : (image + 1) * LOW, :] + bias + time_proj[image : image + 1, :]
        )
    normalize(inner, 2 * IMGS, gain_two, shift_two, act_two)
    res_out[...] = down[...] + conv_low(wide, kern_second) + vector_at(stage, at["bias_second"], C2)


def norm_back(grad_ref, source, center, scale, gain, shift, ones, active, store):
    def normal(image, row):
        return (source[pl.ds(row, 64), :] - center[image : image + 1, :]) * scale[image : image + 1, :]

    def load(phase, image, row):
        xhat = normal(image, row)
        grad = grad_ref[pl.ds(row, 64), :]
        if active:
            value = xhat * gain + shift
            gate = logistic(value)
            grad = grad * (gate * (1.0 + value * (1.0 - gate)))
            grad_ref[pl.ds(row, 64), :] = grad
        return grad, grad * xhat

    gain_grad, shift_grad, mean_one, mean_two = norm_back_stats(load, 1, C2, gain, ones)

    def body(phase, image, inside, row):
        store(
            image,
            inside,
            row,
            scale[image : image + 1, :]
            * (
                grad_ref[pl.ds(row, 64), :] * gain
                - mean_one[image : image + 1, :]
                - normal(image, row) * mean_two[image : image + 1, :]
            ),
        )

    each_chunk(body)
    return gain_grad, shift_grad


def res_backward(
    leaving, me, grad_res, down, inner, act_one, act_two, kern_first, kern_second, dense_two, hidden_pre, stats, gains, embed,
    grad_down, sent, out,
    wide, grad_act,
):
    at = RES_AT
    ones = same_group(C2)
    clear_edges(wide)

    def lower(phase, image, inside, row):
        put_shifted(wide, image, inside, grad_res[pl.ds(row, 64), :].astype(bf16).astype(f32))

    each_chunk(lower)
    sums = image_sums(
        lambda phase, image, row: (grad_res[pl.ds(row, 64), :].astype(bf16).astype(f32),), 1, C2
    )[0]
    vector_to(out, at["bias_second"], jnp.sum(sums, axis=0, keepdims=True))
    grad_act[...] = conv_low_back(wide, kern_second)
    conv_low_grad(act_two, wide, out, at["kern_second"])

    def store_inner(image, inside, row, value):
        put_shifted(wide, image, inside, value.astype(bf16).astype(f32))

    gain_grad, shift_grad = norm_back(
        grad_act, inner, stats[8:12, :], stats[12:16, :],
        gains[2:3, :], gains[3:4, :], ones, True, store_inner,
    )
    vector_to(out, at["gain_second"], gain_grad)
    vector_to(out, at["shift_second"], shift_grad)
    inner_sum = jnp.concatenate(
        [
            jnp.sum(fold(wide[image, PAD : PAD + LOW, C2 : 2 * C2].astype(f32)), axis=0, keepdims=True)
            for image in range(IMGS)
        ]
        + [jnp.zeros((4, C2), f32)],
        axis=0,
    )
    time_sum = jnp.sum(inner_sum, axis=0, keepdims=True)
    vector_to(out, at["bias_first"], time_sum)
    vector_to(out, at["bias_two"], time_sum)
    pre = hidden_pre[...]
    gate = logistic(pre)
    contract = (((0,), (0,)), ((), ()))
    matrix_to(
        out, at["dense_two"],
        lax.dot_general(pre * gate, inner_sum, contract, precision=highest, preferred_element_type=f32),
    )
    grad_pre = lax.dot_general(
        inner_sum, dense_two[...].astype(f32), (((1,), (1,)), ((), ())), precision=highest, preferred_element_type=f32
    ) * (gate * (1.0 + pre * (1.0 - gate)))
    vector_to(out, at["bias_one"], jnp.sum(grad_pre, axis=0, keepdims=True))
    matrix_to(
        out, at["dense_one"],
        lax.dot_general(embed[...], grad_pre, contract, precision=highest, preferred_element_type=f32),
    )
    grad_act[...] = conv_low_back(wide, kern_first)
    conv_low_grad(act_one, wide, out, at["kern_first"])

    def store_down(image, inside, row, value):
        grad_down[pl.ds(row, 64), :] = value + grad_res[pl.ds(row, 64), :]

    gain_grad, shift_grad = norm_back(
        grad_act, down, stats[0:4, :], stats[4:8, :],
        gains[0:1, :], gains[1:2, :], ones, True, store_down,
    )
    vector_to(out, at["gain_first"], gain_grad)
    vector_to(out, at["shift_first"], shift_grad)
    out[at["end"] :, :] = jnp.zeros((RES_ROWS - at["end"], LANES), f32)
    narrow_out(out, me[0], sent, leaving)


def attn_forward(
    places, me, gathered, res_out,
    attn_low, normed, qkv, probs, mixed, kern_qkv, kern_proj, stats, gains,
    stage,
):
    at = ATTN_AT
    widen(gathered, places, me[0], stage)
    matrix_from(stage, at["kern_qkv"], kern_qkv, C2, 3 * C2)
    matrix_from(stage, at["kern_proj"], kern_proj, C2, C2)
    ones = same_group(C2)
    gain = vector_at(stage, at["gain_attn"], C2)
    shift = vector_at(stage, at["shift_attn"], C2)
    gains[...] = jnp.concatenate([gain, shift, jnp.zeros((6, C2), f32)], axis=0)
    center, scale = norm_stats(lambda phase, row: res_out[pl.ds(row, 64), :], 1, C2, ones)
    stats[0:IMGS, :] = center
    stats[IMGS : 2 * IMGS, :] = scale

    def body(phase, image, inside, row):
        value = (res_out[pl.ds(row, 64), :] - center[image : image + 1, :]) * scale[image : image + 1, :]
        normed[pl.ds(row, 64), :] = (value * gain + shift).astype(bf16)

    each_chunk(body)
    qkv[...] = mm(normed[...], kern_qkv[...]).astype(bf16)
    for image in range(IMGS):
        rows = slice(image * LOW, (image + 1) * LOW)
        logits = mm_nt(qkv[rows, 0:C2], qkv[rows, C2 : 2 * C2]) * C2 ** (-0.5)
        powers = jnp.exp(logits - jnp.max(logits, axis=1, keepdims=True))
        weights = powers / jnp.sum(powers, axis=1, keepdims=True)
        probs[image] = weights
        mixed[rows, :] = mm(weights.astype(bf16), qkv[rows, 2 * C2 : 3 * C2]).astype(bf16)
    attn_low[...] = (
        res_out[...] + mm(mixed[...], kern_proj[...]) + vector_at(stage, at["bias_proj"], C2)
    ).astype(bf16)


def attn_backward(
    leaving, me, grad_attn, res_out, normed, qkv, probs, mixed, kern_qkv, kern_proj, stats, gains,
    grad_res, sent, out,
    grad_qkv, grad_mixed, grad_normed, low,
):
    at = ATTN_AT
    ones = same_group(C2)
    low[...] = grad_attn[...].astype(bf16)
    sums = image_sums(lambda phase, image, row: (grad_attn[pl.ds(row, 64), :],), 1, C2)[0]
    vector_to(out, at["bias_proj"], jnp.sum(sums, axis=0, keepdims=True))
    matrix_to(out, at["kern_proj"], mm_tn(mixed[...], low[...]))
    grad_mixed[...] = mm_nt(low[...], kern_proj[...]).astype(bf16)
    scale_by = C2 ** (-0.5)
    for image in range(IMGS):
        rows = slice(image * LOW, (image + 1) * LOW)
        query, keys, value = (qkv[rows, part * C2 : (part + 1) * C2] for part in range(3))
        weights = probs[image]
        grad_probs = mm_nt(grad_mixed[rows, :], value)
        grad_qkv[rows, 2 * C2 : 3 * C2] = mm_tn(weights.astype(bf16), grad_mixed[rows, :]).astype(bf16)
        grad_logits = (
            weights * (grad_probs - jnp.sum(weights * grad_probs, axis=1, keepdims=True))
        ).astype(bf16)
        grad_qkv[rows, 0:C2] = (mm(grad_logits, keys) * scale_by).astype(bf16)
        grad_qkv[rows, C2 : 2 * C2] = (mm_tn(grad_logits, query) * scale_by).astype(bf16)
    matrix_to(out, at["kern_qkv"], mm_tn(normed[...], grad_qkv[...]))
    grad_normed[...] = mm_nt(grad_qkv[...], kern_qkv[...])

    def store(image, inside, row, value):
        grad_res[pl.ds(row, 64), :] = value + grad_attn[pl.ds(row, 64), :]

    gain_grad, shift_grad = norm_back(
        grad_normed, res_out, stats[0:4, :], stats[4:8, :],
        gains[0:1, :], gains[1:2, :], ones, False, store,
    )
    vector_to(out, at["gain_attn"], gain_grad)
    vector_to(out, at["shift_attn"], shift_grad)
    out[at["end"] :, :] = jnp.zeros((ATTN_ROWS - at["end"], LANES), f32)
    narrow_out(out, me[0], sent, leaving)


def pick(row, channel):
    lane = lax.broadcasted_iota(jnp.int32, (LANES, LANES), 0)
    ch = lax.broadcasted_iota(jnp.int32, (LANES, LANES), 1)
    return (row * LANES + lane == CIN * ch + channel).astype(f32).astype(bf16)


def head_step(
    places, leaving, me, gathered, attn_low, top, clean, factor,
    grad_attn, skip, loss, sent, out,
    stage, wide, kern_up, merged, act, taps, narrow, grad_wide_zero, grad_wide_one, boxes,
):
    at = HEAD_AT
    widen(gathered, places, me[0], stage)
    ones = same_group(C1)
    kern_up[...] = jnp.zeros(kern_up.shape, bf16)

    def combine(at_row):
        tap = [[stage[pl.ds((3 * a + b) * C2 + at_row, 64), :] for b in range(3)] for a in range(3)]
        by_row = {(0, 0): tap[0], (0, 1): [tap[1][b] + tap[2][b] for b in range(3)],
                  (1, 0): [tap[0][b] + tap[1][b] for b in range(3)], (1, 1): tap[2]}
        for (row_phase, slot), three in by_row.items():
            for col_off in range(3):
                base = (slot * 3 + col_off) * C2
                here = pl.ds(base + at_row, 64)
                if col_off == 0:
                    kern_up[row_phase, here, 0:C1] = three[0].astype(bf16)
                elif col_off == 1:
                    kern_up[row_phase, here, 0:C1] = (three[1] + three[2]).astype(bf16)
                    kern_up[row_phase, here, C1 : 2 * C1] = (three[0] + three[1]).astype(bf16)
                else:
                    kern_up[row_phase, here, C1 : 2 * C1] = three[2].astype(bf16)

    chunks(C2, 64, combine)
    clear_edges(wide)

    def spread_low(phase, image, inside, row):
        put_shifted(wide, image, inside, attn_low[pl.ds(row, 64), :].astype(f32))

    each_chunk(spread_low)
    bias_up = stage[at["bias_up"] : at["bias_up"] + 1, :]
    for row_phase in range(2):
        product = mm(
            jnp.concatenate(
                [wide_rows(wide, row_phase - 1, 0, 3 * C2), wide_rows(wide, row_phase, 0, 3 * C2)], axis=1
            ),
            kern_up[row_phase],
        )
        for col_phase in range(2):
            phase = row_phase * 2 + col_phase
            merged[phase] = product[:, col_phase * C1 : (col_phase + 1) * C1] + bias_up + top[phase]
    gain = stage[at["gain_out"] : at["gain_out"] + 1, :]
    shift = stage[at["shift_out"] : at["shift_out"] + 1, :]
    center, scale = norm_stats(lambda phase, row: merged[phase, pl.ds(row, 64), :], 4, C1, ones)

    def body(phase, image, inside, row):
        value = (merged[phase, pl.ds(row, 64), :] - center[image : image + 1, :]) * scale[image : image + 1, :]
        value = value * gain + shift
        gate = logistic(value)
        act[phase, pl.ds(row, 64), :] = (value * gate).astype(bf16)
        skip[phase, pl.ds(row, 64), :] = gate * (1.0 + value * (1.0 - gate))

    each_chunk(body, 4)
    for channel in range(CIN):
        total = None
        for row in range(3):
            part = mm(stage[pl.ds(at["kern_out"] + row, 9, 3), :].astype(bf16), pick(row, channel))
            total = part if total is None else total + part
        narrow[pl.ds(channel, 9, 8), :] = total
    for channel in range(CIN, 8):
        narrow[pl.ds(channel, 9, 8), :] = jnp.zeros((9, LANES), f32)
    kern_out = narrow[...].astype(bf16)
    masks = lane_masks(ROWS)
    for phase in range(4):
        taps[:, phase * ROWS : (phase + 1) * ROWS] = mm_nt(kern_out, act[phase])
    lane = lax.broadcasted_iota(jnp.int32, (8, LANES), 1)
    channel_at = lax.broadcasted_iota(jnp.int32, (8, LANES), 0)
    bias_out = jnp.sum(
        jnp.where((lane == channel_at) & (channel_at < CIN), stage[at["bias_out"] : at["bias_out"] + 1, :], 0.0),
        axis=1,
        keepdims=True,
    )
    pixel_count = CIN * SIDE * SIDE
    loss_sum = jnp.zeros((8, ROWS), f32)
    bias_grad = jnp.zeros((8, 1), f32)
    grad_lanes = []
    for phase in range(4):
        predict = bias_out
        for tap, off in enumerate(TAPS):
            other, row_off, col_off = tap_source(phase, off)
            predict = predict + lane_shift(
                taps[8 * tap : 8 * tap + 8, other * ROWS : (other + 1) * ROWS], row_off, col_off, masks
            )
        error = predict - clean[:, phase * ROWS : (phase + 1) * ROWS]
        loss_sum = loss_sum + error * error * factor[...]
        grad = ((2.0 / pixel_count) * factor[...] * error).astype(bf16).astype(f32)
        bias_grad = bias_grad + jnp.sum(grad, axis=1, keepdims=True)
        grad_lanes.append(grad)
    loss[...] = jnp.sum(jnp.sum(loss_sum, axis=1, keepdims=True), axis=0, keepdims=True) * (1.0 / pixel_count)
    out[at["bias_out"] : at["bias_out"] + 1, :] = jnp.sum(
        jnp.where((lane == channel_at) & (channel_at < CIN), bias_grad, 0.0), axis=0, keepdims=True
    )
    for phase in range(4):
        for tap, off in enumerate(TAPS):
            other, row_off, col_off = tap_source(phase, (-off[0], -off[1]))
            taps[8 * tap : 8 * tap + 8, phase * ROWS : (phase + 1) * ROWS] = lane_shift(
                grad_lanes[other], row_off, col_off, masks
            )
    kern_grad = None
    for phase in range(4):
        low = taps[:, phase * ROWS : (phase + 1) * ROWS].astype(bf16)
        part = mm(low, act[phase])
        kern_grad = part if kern_grad is None else kern_grad + part
        skip[phase] = mm_tn(low, kern_out) * skip[phase]
    narrow[...] = kern_grad
    for row in range(3):
        total = None
        for channel in range(CIN):
            pieces = parts_of(narrow[pl.ds(channel, 9, 8), :])
            part = sum(mm_nt(piece, pick(row, channel)) for piece in pieces)
            total = part if total is None else total + part
        out[pl.ds(at["kern_out"] + row, 9, 3), :] = total

    def pieces(phase, image, row):
        xhat = (merged[phase, pl.ds(row, 64), :] - center[image : image + 1, :]) * scale[image : image + 1, :]
        return skip[phase, pl.ds(row, 64), :], xhat

    def load(phase, image, row):
        grad, xhat = pieces(phase, image, row)
        return grad, grad * xhat

    gain_grad, shift_grad, mean_one, mean_two = norm_back_stats(load, 4, C1, gain, ones)
    vector_to(out, at["gain_out"], gain_grad)
    vector_to(out, at["shift_out"], shift_grad)
    clear_edges(grad_wide_zero)
    clear_edges(grad_wide_one)
    clear_edges(boxes)
    wides = (grad_wide_zero, grad_wide_one)

    def back(phase, image, inside, row):
        for row_phase in range(2):
            pair = []
            for col_phase in range(2):
                phase = row_phase * 2 + col_phase
                grad, xhat = pieces(phase, image, row)
                value = scale[image : image + 1, :] * (
                    grad * gain - mean_one[image : image + 1, :] - xhat * mean_two[image : image + 1, :]
                )
                skip[phase, pl.ds(row, 64), :] = value
                pair.append(value.astype(bf16).astype(f32))
            here = pl.ds(PAD + inside, 64)
            right, left = row_shift(pair[0], 1), row_shift(pair[1], -1)
            for number, value in enumerate((right, *pair, left)):
                wides[row_phase][image, here, number * C1 : (number + 1) * C1] = value.astype(bf16)
            base = row_phase * 3 * C1
            boxes[image, here, base : base + C1] = pair[1] + right
            boxes[image, here, base + C1 : base + 2 * C1] = pair[0] + pair[1]
            boxes[image, here, base + 2 * C1 : base + 3 * C1] = left + pair[0]

    each_chunk(back)
    bias_sum = jnp.zeros((8, C1), f32)
    for row_phase in range(2):
        for image in range(IMGS):
            both = fold(wides[row_phase][image, PAD : PAD + LOW, C1 : 3 * C1].astype(f32))
            bias_sum = bias_sum + both[:, :C1] + both[:, C1:]
    vector_to(out, at["bias_up"], jnp.sum(bias_sum, axis=0, keepdims=True))
    total = None
    for row_phase in range(2):
        for slot in range(2):
            base = slot * 3 * C2
            taps = [
                kern_up[row_phase, base : base + C2, 0:C1],
                kern_up[row_phase, base + C2 : base + 2 * C2, :],
                kern_up[row_phase, base + 2 * C2 : base + 3 * C2, C1:C2],
            ]
            part = mm_nt(wide_rows(wides[row_phase], 1 - row_phase - slot, 0, 4 * C1), jnp.concatenate(taps, axis=1))
            total = part if total is None else total + part
    grad_attn[...] = total
    width = 3 * C1

    def box_rows(row_off, row_phase):
        return boxes[
            :, PAD + 16 * row_off : PAD + 16 * row_off + LOW, row_phase * width : (row_phase + 1) * width
        ].reshape(ROWS, width)

    summed = (
        box_rows(0, 1) + box_rows(1, 0),
        box_rows(0, 0) + box_rows(0, 1),
        box_rows(-1, 1) + box_rows(0, 0),
    )
    for row_tap in range(3):
        product = mm_tn(attn_low[...], summed[row_tap].astype(bf16))
        for col_tap in range(3):
            tap = row_tap * 3 + col_tap
            out[tap * C2 : (tap + 1) * C2, :] = product[:, col_tap * C1 : (col_tap + 1) * C1]
    out[at["end"] :, :] = jnp.zeros((HEAD_ROWS - at["end"], LANES), f32)
    narrow_out(out, me[0], sent, leaving)


def sds(shape, dtype=f32):
    return jax.ShapeDtypeStruct(shape, dtype)


def run(body, scalars, ins, outs, scratch=(), limit=62):
    in_leaves, in_tree = jax.tree.flatten([*scalars, *ins])
    out_leaves, out_tree = jax.tree.flatten(outs)

    def kernel(*refs):
        split = len(in_leaves), len(in_leaves) + len(out_leaves)
        body(
            *jax.tree.unflatten(in_tree, refs[: split[0]]),
            *jax.tree.unflatten(out_tree, refs[split[0] : split[1]]),
            *refs[split[1] :],
        )

    whole = pl.BlockSpec(memory_space=pltpu.VMEM)
    scalar = pl.BlockSpec(memory_space=pltpu.SMEM)
    results = pl.pallas_call(
        kernel,
        out_shape=out_leaves,
        in_specs=[scalar] * len(scalars) + [whole] * (len(in_leaves) - len(scalars)),
        out_specs=[whole] * len(out_leaves),
        scratch_shapes=scratch,
        compiler_params=pltpu.CompilerParams(vmem_limit_bytes=limit * 2**20),
    )(*in_leaves)
    return jax.tree.unflatten(out_tree, results)


def wide_scratch(width, dtype=bf16):
    return pltpu.VMEM((IMGS, PADDED, width), dtype)


SAVED = dict(
    stage=((RES_ROWS, LANES), f32), block_out=((HEAD_ROWS, LANES), f32),
    taps=((72, 4 * ROWS), f32), low_taps=((72, 4 * ROWS), f32), narrow=((72, LANES), f32),
    top=((4, ROWS, C1), f32), down=((ROWS, C2), f32), inner=((ROWS, C2), f32), res_out=((ROWS, C2), f32),
    act_one=((ROWS, C2), bf16), act_two=((ROWS, C2), bf16), attn_low=((ROWS, C2), bf16), normed=((ROWS, C2), bf16),
    qkv=((ROWS, 3 * C2), bf16), probs=((IMGS, LOW, LOW), f32), mixed=((ROWS, C2), bf16),
    merged=((4, ROWS, C1), f32), act=((4, ROWS, C1), bf16), skip=((4, ROWS, C1), f32),
    grad_attn=((ROWS, C2), f32), grad_res=((ROWS, C2), f32), grad_act=((ROWS, C2), f32),
    grad_low=((ROWS, C2), bf16), grad_mixed=((ROWS, C2), bf16), grad_qkv=((ROWS, 3 * C2), bf16),
    dense_one=((TDIM, TEMB), bf16), dense_two=((TEMB, C2), bf16), kern_down=((9 * C1, C2), bf16),
    kern_first=((9 * C2, C2), bf16), kern_second=((9 * C2, C2), bf16), kern_qkv=((C2, 3 * C2), bf16),
    kern_proj=((C2, C2), bf16), kern_up=((2, 6 * C2, C2), bf16),
    hidden_pre=((8, TEMB), f32), res_stats=((16, C2), f32), res_gains=((8, C2), f32),
    attn_stats=((8, C2), f32), attn_gains=((8, C2), f32),
    wide=((IMGS, PADDED, 3 * C2), bf16), wide_zero=((IMGS, PADDED, 3 * C2), bf16),
    wide_one=((IMGS, PADDED, 3 * C2), bf16), boxes=((IMGS, PADDED, 6 * C1), f32),
)


class Named:
    def __init__(self, names, refs):
        self.__dict__.update(zip(names, refs))


def whole_step(places, leaving, me, gathered, noisy, clean, factor, embed, loss, sent, *refs):
    own = Named(SAVED, refs)
    stem_wide, stem_wide_zero = own.wide.at[:, :, 0 : 3 * C1], own.wide_zero.at[:, :, 0 : 3 * C1]
    stem_forward(
        places[0], me, gathered[0], noisy, own.top, own.down, own.kern_down, own.stage, own.taps, stem_wide, stem_wide_zero
    )
    res_forward(
        places[1], me, gathered[1], own.down, embed,
        own.inner, own.res_out, own.act_one, own.act_two, own.kern_first, own.kern_second, own.dense_two,
        own.hidden_pre, own.res_stats, own.res_gains,
        own.stage, own.dense_one, own.wide,
    )
    attn_forward(
        places[2], me, gathered[2], own.res_out,
        own.attn_low, own.normed, own.qkv, own.probs, own.mixed, own.kern_qkv, own.kern_proj,
        own.attn_stats, own.attn_gains,
        own.stage,
    )
    head_step(
        places[3], leaving[3], me, gathered[3], own.attn_low, own.top, clean, factor,
        own.grad_attn, own.skip, loss, sent[3], own.block_out,
        own.stage, own.wide, own.kern_up, own.merged, own.act, own.low_taps, own.narrow,
        own.wide_zero, own.wide_one, own.boxes,
    )
    attn_backward(
        leaving[2], me, own.grad_attn, own.res_out, own.normed, own.qkv, own.probs, own.mixed,
        own.kern_qkv, own.kern_proj, own.attn_stats, own.attn_gains,
        own.grad_res, sent[2], own.block_out.at[0:ATTN_ROWS],
        own.grad_qkv, own.grad_mixed, own.grad_act, own.grad_low,
    )
    res_backward(
        leaving[1], me, own.grad_res, own.down, own.inner, own.act_one, own.act_two, own.kern_first, own.kern_second,
        own.dense_two, own.hidden_pre, own.res_stats, own.res_gains, embed,
        own.grad_attn, sent[1], own.stage,
        own.wide, own.grad_act,
    )
    stem_backward(
        leaving[0], me, noisy, own.top, own.skip, own.grad_attn, own.kern_down, sent[0], own.block_out,
        own.taps, stem_wide, stem_wide_zero, own.wide_one.at[:, :, 0 : 2 * C2], own.act,
    )


def local_step(me, arrays, places, shapes, out_places, noisy, clean, factor, embed):
    def body(me, arrays, noisy, clean, factor, embed, loss, sent, *refs):
        gathered = [[arrays[place[0]] for place in block] for block in places]
        leaving = [[sent[place[0]] for place in block] for block in out_places]
        rest = [[place[1:] for place in block] for block in places]
        out_rest = [[place[1:] for place in block] for block in out_places]
        whole_step(rest, out_rest, me, gathered, noisy, clean, factor, embed, loss, leaving, *refs)

    return run(
        body,
        [me],
        [arrays, noisy, clean, factor, embed],
        [sds((1, 1)), shapes],
        [pltpu.VMEM(shape, dtype) for shape, dtype in SAVED.values()],
    )


def plan(step_counts, time_index, teacher_size):
    position = time_index % step_counts
    time_values = (2 * position + teacher_size).astype(f32) / (2 * step_counts).astype(f32)
    alpha_t = jnp.cos(0.5 * math.pi * time_values)
    sigma_t = jnp.sin(0.5 * math.pi * time_values)
    weight = jnp.maximum(alpha_t * alpha_t / (sigma_t * sigma_t), 1.0)
    return (time_values, alpha_t, sigma_t, weight)


def sinusoid(time_values):
    half_dim = TDIM // 2
    frequency = jnp.exp(-math.log(10000.0) * jnp.arange(half_dim, dtype=f32) / half_dim)
    angles = 1000.0 * time_values[:, None] * frequency[None, :]
    return jnp.concatenate([jnp.sin(angles), jnp.cos(angles)], axis=1)


def arrange(clean_images, noise_field, levels):
    def body(levels, clean, noise, noisy_out, clean_out, factor_out):
        image = lax.broadcasted_iota(jnp.int32, (IMGS, 1), 0)

        def column(kind):
            value = jnp.zeros((IMGS, 1), f32)
            for number in range(IMGS):
                value = jnp.where(image == number, levels[kind, number], value)
            return value

        alpha, sigma = column(1), column(2)
        mixed = [(alpha * clean[c] + sigma * noise[c]).astype(bf16).astype(f32) for c in range(CIN)]
        pieces = [piece.astype(f32) for piece in parts_of(jnp.concatenate([clean[c] for c in range(CIN)], axis=0))]
        rows = jnp.concatenate(mixed + pieces, axis=0).astype(bf16)
        held = CIN * IMGS
        noisy_out[...] = jnp.zeros(noisy_out.shape, f32)
        clean_out[...] = jnp.zeros(clean_out.shape, f32)
        for phase in range(4):
            place = lax.broadcasted_iota(jnp.int32, (SIDE * SIDE, LOW), 1)
            source = ((place >> 4) * 2 + phase // 2) * SIDE + (place & 15) * 2 + phase % 2
            chosen = lax.broadcasted_iota(jnp.int32, (SIDE * SIDE, LOW), 0) == source
            moved = mm(rows, chosen.astype(f32).astype(bf16))
            exact = moved[held : 2 * held] + moved[2 * held : 3 * held] + moved[3 * held : 4 * held]
            for number in range(IMGS):
                lanes = slice(phase * ROWS + number * LOW, phase * ROWS + (number + 1) * LOW)
                for c in range(CIN):
                    at = c * IMGS + number
                    noisy_out[c : c + 1, lanes] = moved[at : at + 1]
                    clean_out[c : c + 1, lanes] = exact[at : at + 1]
        for number in range(IMGS):
            factor_out[:, number * LOW : (number + 1) * LOW] = jnp.full((1, LOW), levels[0, number], f32)

    return run(
        body,
        [levels],
        [clean_images.transpose(1, 0, 2), noise_field.transpose(1, 0, 2)],
        [sds((8, 4 * ROWS)), sds((8, 4 * ROWS)), sds((1, ROWS))],
        limit=12,
    )


def prepare(clean_images, noise_field, step_counts, time_index, teacher_size, image_count):
    time_values, alpha_t, sigma_t, weight = plan(step_counts, time_index, teacher_size)
    live_mask = (jnp.arange(clean_images.shape[0], dtype=jnp.int32) < image_count).astype(f32)
    levels = jnp.stack([live_mask * weight, alpha_t, sigma_t], axis=0)
    embed = jnp.pad(sinusoid(time_values), ((0, 8 - IMGS), (0, 0)))
    return [*arrange(clean_images, noise_field, levels), embed]


AXES = ("dp", "fsdp")
BLOCK_ROWS = (STEM_ROWS, RES_ROWS, ATTN_ROWS, HEAD_ROWS)
SHARD_ROWS = (80, 344, 72, 80)
SPAN = 32
PARTS = (
    ((0, 0, 80), (1, 32, 184)),
    ((1, 184, 344), (2, 0, 72)),
    ((3, 0, 80), (1, 0, 32)),
)
PART_ROWS = tuple(sum(hi - lo for _, lo, hi in members) for members in PARTS)
TURNS = ((2, 4), (4, 2))
PLANE = (0, 2, 4, 6)
LINE = (0, 8, 16, 24)


def swap(values, mask):
    return lax.ppermute(values, AXES, [(here, here ^ mask) for here in range(SPAN)])


def pack_rows(masters):
    def body(refs, outs):
        for out, parts in zip(outs, (PARTS[:2], PARTS[2:])):
            at = 0
            for members in parts:
                for block, lo, hi in members:
                    out[at : at + hi - lo, :] = refs[block][lo:hi, :].astype(bf16)
                    at += hi - lo

    shapes = [sds((sum(PART_ROWS[:2]), LANES), bf16), sds((PART_ROWS[2], LANES), bf16)]
    return run(body, [], [masters], [shapes], limit=62)[0]


def part_places(number, array, masks):
    at, found = 0, []
    for block, lo, hi in PARTS[number]:
        found.append((block, (array, masks, at, at + hi - lo, SHARD_ROWS[block], lo)))
        at += hi - lo
    return found


def gather_parts(own, prepared):
    early, late = own
    *images, embed = prepared
    line = [early] + [swap(early, mask) for mask in LINE[1:]]
    near = jnp.stack([late, swap(late, PLANE[1])], axis=0)
    near = jnp.concatenate([near, swap(near, PLANE[2])], axis=0)
    arrays, places = [], [[] for _ in SHARD_ROWS]

    def add(number, array, masks):
        for block, place in part_places(number, len(arrays), masks):
            places[block].append(place)
        arrays.append(array)

    held = []
    for number, (last, first) in enumerate(TURNS):
        begin = number * PART_ROWS[0]
        piece = jnp.stack([rows[begin : begin + PART_ROWS[number]] for rows in line], axis=0)
        held.append(jnp.concatenate([piece, swap(piece, first)], axis=0))
    held, near, images = lax.optimization_barrier((held, near, images))
    far = [swap(held[number], last) for number, (last, first) in enumerate(TURNS)]
    third = jnp.concatenate([near] + [swap(near, mask) for mask in LINE[1:]], axis=0)
    far, third, embed = lax.optimization_barrier((far, third, embed))
    for number, (last, first) in enumerate(TURNS):
        masks = [a ^ b for a in (0, first) for b in LINE]
        add(number, held[number], masks)
        add(number, far[number], [mask ^ last for mask in masks])
        add(number, swap(held[number], 1), [mask ^ 1 for mask in masks])
        add(number, swap(far[number], 1), [mask ^ last ^ 1 for mask in masks])
    masks = [a ^ b for b in LINE for a in PLANE]
    add(2, third, masks)
    add(2, swap(third, 1), [mask ^ 1 for mask in masks])
    return arrays, places, (*images, embed)


def leaving_parts():
    shapes, places = [], [[] for _ in SHARD_ROWS]

    def add(number, masks):
        for block, place in part_places(number, len(shapes), masks):
            places[block].append(place)
        shapes.append(sds((len(masks), PART_ROWS[number], LANES), bf16))

    for number, (first, last) in enumerate(TURNS):
        for core in (0, 1):
            for side in (0, first):
                add(number, [core ^ side ^ a ^ b for a in (0, last) for b in LINE])
    for core in (0, 1):
        add(2, [core ^ a ^ b for b in LINE for a in PLANE])
    return shapes, places


def reduce_parts(leaving):
    totals = []
    crossed = [[swap(leaving[4 * number + 2 + side], 1) for side in (0, 1)] for number in (0, 1)]
    third = leaving[8].astype(f32) + swap(leaving[9], 1).astype(f32)
    far = [leaving[4 * number + 1].astype(f32) + crossed[number][1].astype(f32) for number in (0, 1)]
    near, far, third = lax.optimization_barrier(([crossed[0][0], crossed[1][0]], far, third))
    near = [leaving[4 * number].astype(f32) + near[number].astype(f32) for number in (0, 1)]
    arrived = [swap(third[4 * at : 4 * at + 4].astype(bf16), mask) for at, mask in enumerate(LINE) if mask]
    third = third[:4] + sum(piece.astype(f32) for piece in arrived)
    for number, (first, last) in enumerate(TURNS):
        totals.append(near[number] + swap(far[number].astype(bf16), first).astype(f32))
    totals, third = lax.optimization_barrier((totals, third))
    for number, (first, last) in enumerate(TURNS):
        total = totals[number]
        totals[number] = total[:4] + swap(total[4:].astype(bf16), last).astype(f32)
    whole = jnp.concatenate(totals, axis=1)
    return [
        [array[0]] + [swap(array[at].astype(bf16), mask) for at, mask in enumerate(masks) if mask]
        for array, masks in ((whole, LINE), (third, PLANE))
    ]


def last_sum(image_counts, count, loss, groups):
    def body(live, loss, groups, total, row):
        square, at = jnp.zeros((8, LANES), f32), 0
        for pieces in groups:
            value = pieces[0][...].astype(f32)
            for piece in pieces[1:]:
                value = value + piece[...].astype(f32)
            total[at : at + value.shape[0], :] = value
            at += value.shape[0]
            square = square + fold(value * value)
        square = jnp.sum(jnp.sum(square, axis=0, keepdims=True), axis=1, keepdims=True)
        lane = lax.broadcasted_iota(jnp.int32, (1, LANES), 1)
        scalars = jnp.where(lane == 0, loss[...], jnp.where(lane == 1, square, live[0].astype(f32)))
        row[...] = jnp.broadcast_to(scalars[None], row.shape)

    rows = sum(pieces[0].shape[0] for pieces in groups)
    return run(body, [image_counts], [loss, groups], [sds((rows, LANES)), sds((count, 1, LANES))], limit=16)


def update(adam_step, arrived, gradient, masters, firsts, seconds, places):
    def body(step, arrived, gradient, masters, firsts, seconds, loss, norm, outs):
        sums = jnp.sum(arrived[...], axis=0)
        live = 1.0 / sums[:, 2:3]
        loss[...] = sums[:, 0:1] * live
        size = jnp.sqrt(sums[:, 1:2]) * live
        norm[...] = size
        scale = clip_limit / jnp.maximum(size, clip_limit) * live
        powers = lax.fori_loop(
            0, step[0], lambda _, held: (held[0] * beta_one, held[1] * beta_two), (jnp.float32(1.0), jnp.float32(1.0))
        )
        fix_one, fix_two = 1.0 - powers[0], 1.0 - powers[1]
        at = 0
        for block, lo, hi in places:
            grad = gradient[at : at + hi - lo, :] * scale
            at += hi - lo
            master, first, second = (refs[block][lo:hi, :] for refs in (masters, firsts, seconds))
            first_new = beta_one * first + (1.0 - beta_one) * grad
            second_new = beta_two * second + (1.0 - beta_two) * grad * grad
            master_new = master - learn_rate * (
                first_new / fix_one / (jnp.sqrt(second_new / fix_two) + adam_eps) + decay_rate * master
            )
            for ref, value in zip(outs[block], (master_new, first_new, second_new, master_new.astype(bf16))):
                ref[lo:hi, :] = value

    shapes = [[sds(m.shape), sds(m.shape), sds(m.shape), sds(m.shape, bf16)] for m in masters]
    return run(
        body, [adam_step], [arrived, gradient, masters, firsts, seconds], [sds((1, 1)), sds((1, 1)), shapes], limit=24
    )


def gather_whole(shards):
    arrays = [
        lax.all_gather(shard.reshape(-1), AXES, axis=0, tiled=True).reshape(1, rows, LANES)
        for shard, rows in zip(shards, BLOCK_ROWS)
    ]
    return arrays, [[(block, (0,), 0, rows, 0, 0)] for block, rows in enumerate(BLOCK_ROWS)]


def leaving_whole():
    shapes = [sds((1, rows, LANES), bf16) for rows in BLOCK_ROWS]
    return shapes, [[(block, (0,), 0, rows, 0, 0)] for block, rows in enumerate(BLOCK_ROWS)]


def reduce_whole(leaving):
    sums = [
        lax.psum_scatter(array.astype(f32).reshape(-1), AXES, scatter_dimension=0, tiled=True) for array in leaving
    ]
    return [[jnp.concatenate([one.reshape(-1, LANES) for one in sums], axis=0)]]


def per_device(
    clean_images, noise_field, step_counts, time_index, teacher_size, image_counts, adam_step,
    stem_master, stem_first, stem_second, res_master, res_first, res_second,
    attn_master, attn_first, attn_second, head_master, head_first, head_second,
):
    blocks = [
        [block.reshape(-1, LANES) for block in state]
        for state in (
            (stem_master, res_master, attn_master, head_master),
            (stem_first, res_first, attn_first, head_first),
            (stem_second, res_second, attn_second, head_second),
        )
    ]
    masters = blocks[0]
    count = lax.axis_size(AXES)
    me = lax.axis_index(AXES).astype(jnp.int32).reshape(1)
    laid_out = count == SPAN and tuple(master.shape[0] for master in masters) == SHARD_ROWS
    prepared = prepare(clean_images, noise_field, step_counts, time_index, teacher_size, image_counts[0])
    if laid_out:
        arrays, places, prepared = gather_parts(pack_rows(masters), prepared)
        shapes, out_places = leaving_parts()
        order = [member for members in PARTS for member in members]
    else:
        arrays, places = gather_whole([master.astype(bf16) for master in masters])
        shapes, out_places = leaving_whole()
        order = [(block, 0, master.shape[0]) for block, master in enumerate(masters)]
    loss, leaving = local_step(me, arrays, places, shapes, out_places, *prepared)
    pieces = reduce_parts(leaving) if laid_out else reduce_whole(leaving)
    gradient, row = last_sum(image_counts, count, loss, pieces)
    arrived = lax.all_to_all(row, AXES, 0, 0, tiled=True)
    loss, norm, outs = update(adam_step, arrived, gradient, *blocks, order)
    return (loss[0, 0], norm[0, 0]) + tuple(value.reshape(-1) for block in outs for value in block)


def solution(mesh):
    split = P(("dp", "fsdp"))
    images = P(("dp", "fsdp"), None, None)
    return jax.shard_map(
        per_device,
        mesh=mesh,
        in_specs=(images, images, split, split, split, split, P()) + (split,) * 12,
        out_specs=(P(), P()) + (split,) * 16,
        check_vma=False,
    )
```

```python
from functools import partial
import math

import jax
import jax.numpy as jnp
from jax import lax
from jax.experimental import pallas as pl
from jax.experimental.pallas import tpu as pltpu
from jax.sharding import PartitionSpec as P

C1 = 128
C2 = 256
GROUPS = 32
TDIM = 128
TEMB = 512
CIN = 3
SIDE = 32
LANES = 128
IMGS = 4
LOW = 256
ROWS = IMGS * LOW
PAD = 16
PADDED = LOW + 2 * PAD

clip_limit = 0.05
learn_rate = 0.05
beta_one = 0.9
beta_two = 0.999
adam_eps = 1e-08
decay_rate = 0.01
norm_eps = 1e-05

f32 = jnp.float32
bf16 = jnp.bfloat16
highest = lax.Precision.HIGHEST

STEM_ROWS, RES_ROWS, ATTN_ROWS, HEAD_ROWS = 2560, 11008, 2304, 2560

STEM_AT = dict(kern_in=0, bias_in=27, kern_down=28, bias_down=2332, end=2334)
RES_AT = dict(
    dense_one=0, bias_one=512, dense_two=516, bias_two=1540, gain_first=1542, shift_first=1544,
    kern_first=1546, bias_first=6154, gain_second=6156, shift_second=6158, kern_second=6160,
    bias_second=10768, end=10770,
)
ATTN_AT = dict(gain_attn=0, shift_attn=2, kern_qkv=4, kern_proj=1540, bias_proj=2052, end=2054)
HEAD_AT = dict(kern_up=0, bias_up=2304, gain_out=2305, shift_out=2306, kern_out=2307, bias_out=2334, end=2335)


def mm(a, b):
    return jnp.dot(a, b, preferred_element_type=f32)


def mm_nt(a, b):
    return lax.dot_general(a, b, (((1,), (1,)), ((), ())), preferred_element_type=f32)


def mm_tn(a, b):
    return lax.dot_general(a, b, (((0,), (0,)), ((), ())), preferred_element_type=f32)


def parts_of(values):
    high = values.astype(bf16)
    rest = values - high.astype(f32)
    middle = rest.astype(bf16)
    return high, middle, (rest - middle.astype(f32)).astype(bf16)


def mm_exact(values, matrix):
    count = values.shape[0]
    rows = jnp.concatenate([piece.astype(f32) for piece in parts_of(values)], axis=0).astype(bf16)
    product = mm(rows, matrix)
    return product[:count] + product[count : 2 * count] + product[2 * count :]


def same_group(channels):
    size = channels // GROUPS
    down_at = lax.broadcasted_iota(jnp.int32, (channels, channels), 0) // size
    across = lax.broadcasted_iota(jnp.int32, (channels, channels), 1) // size
    return (down_at == across).astype(f32).astype(bf16)


def row_shift(values, step):
    count = values.shape[0]
    moved = pltpu.roll(values, (-step) % count, 0)
    column = lax.broadcasted_iota(jnp.int32, values.shape, 0) & 15
    return jnp.where(column == (0 if step < 0 else 15), 0.0, moved)


def chunks(total, size, body):
    def step(number, carry):
        body(pl.multiple_of(number * size, size))
        return carry

    lax.fori_loop(0, total // size, step, 0, unroll=True)


def widen(pieces, places, me, stage):
    for ref, (masks, lo, hi, per_shard, begin) in zip(pieces, places):
        for number, mask in enumerate(masks):
            owner = me ^ mask
            at = pl.multiple_of(owner * per_shard + begin, 8)
            stage[pl.ds(at, hi - lo), :] = ref[number, lo:hi, :].astype(f32)


def narrow_out(stage, me, outs, places):
    for ref, (masks, lo, hi, per_shard, begin) in zip(outs, places):
        for number, mask in enumerate(masks):
            owner = me ^ mask
            at = pl.multiple_of(owner * per_shard + begin, 8)
            ref[number, lo:hi, :] = stage[pl.ds(at, hi - lo), :].astype(ref.dtype)


def matrix_from(stage, base, out, depth, width):
    lanes = width // LANES

    def copy(at):
        for lane in range(lanes):
            out[pl.ds(at, 128), lane * LANES : (lane + 1) * LANES] = stage[
                pl.ds(base + lanes * at + lane, 128, lanes), :
            ].astype(bf16)

    chunks(depth, 128, copy)


def matrix_to(out, base, value):
    depth, width = value.shape
    lanes = width // LANES
    for lane in range(lanes):
        out[pl.ds(base + lane, depth, lanes), :] = value[:, lane * LANES : (lane + 1) * LANES]


def vector_at(stage, base, width):
    return jnp.concatenate([stage[base + lane : base + lane + 1, :] for lane in range(width // LANES)], axis=1)


def vector_to(out, base, value):
    for lane in range(value.shape[1] // LANES):
        out[base + lane : base + lane + 1, :] = value[:, lane * LANES : (lane + 1) * LANES]


def fold(values):
    return jnp.sum(values.reshape(values.shape[0] // 8, 8, values.shape[1]), axis=0)


def image_sums(load, phases, width, count=1):
    sums = []
    for image in range(IMGS):
        def step(number, carry):
            row = pl.multiple_of(image * LOW + number * 64, 64)
            for phase in range(phases):
                carry = tuple(c + fold(v) for c, v in zip(carry, load(phase, image, row)))
            return carry

        carry = lax.fori_loop(0, 4, step, tuple(jnp.zeros((8, width), f32) for _ in range(count)), unroll=True)
        sums.append([jnp.sum(c, axis=0, keepdims=True) for c in carry])
    return [jnp.concatenate(list(group), axis=0) for group in zip(*sums)]


def norm_stats(load, phases, width, ones):
    count = LOW * phases * (width // GROUPS)
    (total,) = image_sums(lambda phase, image, row: (load(phase, row),), phases, width)
    center = mm_exact(total, ones) * (1.0 / count)

    def squares(phase, image, row):
        away = load(phase, row) - center[image : image + 1, :]
        return (away * away,)

    (total,) = image_sums(squares, phases, width)
    spread = mm_exact(total, ones) * (1.0 / count)
    return center, lax.rsqrt(spread + norm_eps)


def norm_back_stats(load, phases, width, gain, ones):
    count = LOW * phases * (width // GROUPS)
    shift_sum, gain_sum = image_sums(load, phases, width, 2)
    means = mm_exact(jnp.concatenate([shift_sum * gain, gain_sum * gain], axis=0), ones) * (1.0 / count)
    return (
        jnp.sum(gain_sum, axis=0, keepdims=True),
        jnp.sum(shift_sum, axis=0, keepdims=True),
        means[:IMGS],
        means[IMGS:],
    )


def logistic(values):
    return 0.5 * jnp.tanh(0.5 * values) + 0.5


def each_chunk(body, phases=1, size=64):
    for image in range(IMGS):
        def step(number, carry):
            inside = pl.multiple_of(number * size, size)
            for phase in range(phases):
                body(phase, image, inside, image * LOW + inside)
            return carry

        lax.fori_loop(0, LOW // size, step, 0, unroll=True)


def clear_edges(wide):
    for image in range(IMGS):
        wide[image, 0:PAD, :] = jnp.zeros((PAD, wide.shape[2]), wide.dtype)
        wide[image, PAD + LOW : PADDED, :] = jnp.zeros((PAD, wide.shape[2]), wide.dtype)


def put_shifted(wide, image, inside, value):
    width = value.shape[1]
    at = pl.ds(PAD + inside, value.shape[0])
    wide[image, at, 0:width] = row_shift(value, -1).astype(bf16)
    wide[image, at, width : 2 * width] = value.astype(bf16)
    wide[image, at, 2 * width : 3 * width] = row_shift(value, 1).astype(bf16)


def wide_rows(wide, row_off, lo, hi):
    begin = PAD + 16 * row_off
    return wide[:, begin : begin + LOW, lo:hi].reshape(ROWS, hi - lo)


def conv_low(wide, kern):
    width = wide.shape[2]
    total = None
    for tap in range(3):
        part = mm(wide_rows(wide, tap - 1, 0, width), kern[tap * width : (tap + 1) * width, :])
        total = part if total is None else total + part
    return total


def conv_low_back(wide, kern):
    total = None
    for row_tap in range(3):
        taps = [kern[(row_tap * 3 + col_tap) * C2 : (row_tap * 3 + col_tap + 1) * C2, :] for col_tap in (2, 1, 0)]
        part = mm_nt(wide_rows(wide, 1 - row_tap, 0, 3 * C2), jnp.concatenate(taps, axis=1))
        total = part if total is None else total + part
    return total


def conv_low_grad(source, wide, out, base):
    for row_tap in range(3):
        product = mm_tn(source[...], wide_rows(wide, 1 - row_tap, 0, 3 * C2))
        for col_tap in range(3):
            tap = row_tap * 3 + col_tap
            matrix_to(out, base + tap * 2 * C2, product[:, (2 - col_tap) * C2 : (3 - col_tap) * C2])


def lane_masks(width):
    place = lax.broadcasted_iota(jnp.int32, (8, width), 1)
    row, column = (place >> 4) & 15, place & 15

    def valid(row_off, col_off):
        keep = None
        for at, off in ((row, row_off), (column, col_off)):
            if off:
                inside = at != (0 if off < 0 else 15)
                keep = inside if keep is None else keep & inside
        return keep

    return {(r, c): valid(r, c) for r in (-1, 0, 1) for c in (-1, 0, 1)}


def lane_shift(values, row_off, col_off, masks):
    step = 16 * row_off + col_off
    if step == 0:
        return values
    moved = pltpu.roll(values, (-step) % values.shape[1], 1)
    return jnp.where(masks[(row_off, col_off)], moved, 0.0)


def tap_source(phase, tap_off):
    row, col = phase // 2 + tap_off[0], phase % 2 + tap_off[1]
    return (row % 2) * 2 + col % 2, row // 2, col // 2


TAPS = tuple((row - 1, col - 1) for row in range(3) for col in range(3))


def taps_on_lanes(source, out, masks, sign):
    for phase in range(4):
        for tap, off in enumerate(TAPS):
            other, row_off, col_off = tap_source(phase, (sign * off[0], sign * off[1]))
            out[8 * tap : 8 * tap + 8, phase * ROWS : (phase + 1) * ROWS] = lane_shift(
                source[:, other * ROWS : (other + 1) * ROWS], row_off, col_off, masks
            )


def down_wide(load, wide_one, wide_zero):
    clear_edges(wide_one)

    def body(phase, image, inside, row):
        at = pl.ds(PAD + inside, 64)
        for wide, row_phase in ((wide_one, 1), (wide_zero, 0)):
            right = load(row_phase * 2 + 1, row)
            left = load(row_phase * 2, row)
            wide[image, at, 0:C1] = row_shift(right, -1).astype(bf16)
            wide[image, at, C1 : 2 * C1] = left.astype(bf16)
            wide[image, at, 2 * C1 : 3 * C1] = right.astype(bf16)

    each_chunk(body)


def stem_forward(places, me, gathered, noisy, top, down, kern_down, stage, taps, wide_one, wide_zero):
    at = STEM_AT
    widen(gathered, places, me[0], stage)
    matrix_from(stage, at["kern_down"], kern_down, 9 * C1, C2)
    masks = lane_masks(ROWS)
    taps_on_lanes(noisy, taps, masks, 1)
    kern_in = jnp.concatenate(
        [
            jnp.concatenate([stage[3 * tap : 3 * tap + 3, :], jnp.zeros((5, LANES), f32)], axis=0)
            for tap in range(9)
        ],
        axis=0,
    ).astype(bf16)
    bias_in = stage[at["bias_in"] : at["bias_in"] + 1, :]
    for phase in range(4):
        top[phase] = mm_tn(taps[:, phase * ROWS : (phase + 1) * ROWS].astype(bf16), kern_in) + bias_in
    down_wide(lambda phase, row: top[phase, pl.ds(row, 64), :], wide_one, wide_zero)
    width = 3 * C1
    source = jnp.concatenate(
        [wide_rows(wide_one, -1, 0, width), wide_rows(wide_zero, 0, 0, width), wide_rows(wide_one, 0, 0, width)],
        axis=1,
    )
    down[...] = mm(source, kern_down[...]) + vector_at(stage, at["bias_down"], C2)


def stem_backward(leaving, me, noisy, top, skip, grad_down, kern_down, sent, out, taps, wide_one, wide_zero, wide_grad, low_grad):
    at = STEM_AT
    taps_on_lanes(noisy, taps, lane_masks(ROWS), 1)
    down_wide(lambda phase, row: top[phase, pl.ds(row, 64), :], wide_one, wide_zero)
    clear_edges(wide_grad)

    def body(phase, image, inside, row):
        value = grad_down[pl.ds(row, 64), :].astype(bf16).astype(f32)
        here = pl.ds(PAD + inside, 64)
        wide_grad[image, here, 0:C2] = value.astype(bf16)
        wide_grad[image, here, C2 : 2 * C2] = row_shift(value, 1).astype(bf16)

    each_chunk(body)
    bias_down = jnp.zeros((8, C2), f32)
    bias_down = lax.fori_loop(
        0,
        ROWS // 64,
        lambda n, c: c + fold(grad_down[pl.ds(pl.multiple_of(n * 64, 64), 64), :].astype(bf16).astype(f32)),
        bias_down,
    )
    vector_to(out, at["bias_down"], jnp.sum(bias_down, axis=0, keepdims=True))
    center = wide_rows(wide_grad, 0, 0, C2)
    width = 3 * C1
    for row_tap, (wide, row_off) in enumerate(((wide_one, -1), (wide_zero, 0), (wide_one, 0))):
        product = mm_tn(wide_rows(wide, row_off, 0, width), center)
        matrix_to(out, at["kern_down"] + row_tap * 2 * width, product)

    def taps_rows(first, count):
        return kern_down[first * C1 : (first + count) * C1, :]

    moved = wide_rows(wide_grad, 0, C2, 2 * C2)
    below = wide_rows(wide_grad, 1, 0, C2)
    below_moved = wide_rows(wide_grad, 1, C2, 2 * C2)
    first_pair = mm_nt(center, taps_rows(4, 2))
    second_pair = mm_nt(center, taps_rows(7, 2)) + mm_nt(below, taps_rows(1, 2))
    grads = (
        first_pair[:, :C1],
        first_pair[:, C1:] + mm_nt(moved, taps_rows(3, 1)),
        second_pair[:, :C1],
        second_pair[:, C1:] + mm_nt(moved, taps_rows(6, 1)) + mm_nt(below_moved, taps_rows(0, 1)),
    )
    bias_in = jnp.zeros((8, C1), f32)
    for phase in range(4):
        low_grad[phase] = (skip[phase] + grads[phase]).astype(bf16)
        bias_in = bias_in + fold(low_grad[phase].astype(f32))
    vector_to(out, at["bias_in"], jnp.sum(bias_in, axis=0, keepdims=True))
    kern_in = None
    for phase in range(4):
        part = mm(taps[:, phase * ROWS : (phase + 1) * ROWS].astype(bf16), low_grad[phase])
        kern_in = part if kern_in is None else kern_in + part
    for tap in range(9):
        out[3 * tap : 3 * tap + 3, :] = kern_in[8 * tap : 8 * tap + 3, :]
    out[at["end"] :, :] = jnp.zeros((STEM_ROWS - at["end"], LANES), f32)
    narrow_out(out, me[0], sent, leaving)


def res_forward(
    places, me, gathered, down, embed,
    inner, res_out, act_one, act_two, kern_first, kern_second, dense_two, hidden_pre, stats, gains,
    stage, dense_one, wide,
):
    at = RES_AT
    widen(gathered, places, me[0], stage)
    matrix_from(stage, at["dense_one"], dense_one, TDIM, TEMB)
    matrix_from(stage, at["dense_two"], dense_two, TEMB, C2)
    matrix_from(stage, at["kern_first"], kern_first, 9 * C2, C2)
    matrix_from(stage, at["kern_second"], kern_second, 9 * C2, C2)
    pre = jnp.dot(embed[...], dense_one[...].astype(f32), precision=highest) + vector_at(stage, at["bias_one"], TEMB)
    hidden_pre[...] = pre
    hidden = pre * logistic(pre)
    time_proj = jnp.dot(hidden, dense_two[...].astype(f32), precision=highest) + vector_at(stage, at["bias_two"], C2)
    ones = same_group(C2)
    clear_edges(wide)
    gain = vector_at(stage, at["gain_first"], C2)
    shift = vector_at(stage, at["shift_first"], C2)
    gain_two = vector_at(stage, at["gain_second"], C2)
    shift_two = vector_at(stage, at["shift_second"], C2)
    gains[...] = jnp.concatenate([gain, shift, gain_two, shift_two, jnp.zeros((4, C2), f32)], axis=0)

    def normalize(source, place, gain, shift, keep):
        center, scale = norm_stats(lambda phase, row: source[pl.ds(row, 64), :], 1, C2, ones)
        stats[place : place + IMGS, :] = center
        stats[place + IMGS : place + 2 * IMGS, :] = scale

        def body(phase, image, inside, row):
            value = (source[pl.ds(row, 64), :] - center[image : image + 1, :]) * scale[image : image + 1, :]
            value = value * gain + shift
            value = value * logistic(value)
            keep[pl.ds(row, 64), :] = value.astype(bf16)
            put_shifted(wide, image, inside, value.astype(bf16).astype(f32))

        each_chunk(body)

    normalize(down, 0, gain, shift, act_one)
    bias = vector_at(stage, at["bias_first"], C2)
    product = conv_low(wide, kern_first)
    for image in range(IMGS):
        inner[image * LOW : (image + 1) * LOW, :] = (
            product[image * LOW : (image + 1) * LOW, :] + bias + time_proj[image : image + 1, :]
        )
    normalize(inner, 2 * IMGS, gain_two, shift_two, act_two)
    res_out[...] = down[...] + conv_low(wide, kern_second) + vector_at(stage, at["bias_second"], C2)


def norm_back(grad_ref, source, center, scale, gain, shift, ones, active, store):
    def normal(image, row):
        return (source[pl.ds(row, 64), :] - center[image : image + 1, :]) * scale[image : image + 1, :]

    def load(phase, image, row):
        xhat = normal(image, row)
        grad = grad_ref[pl.ds(row, 64), :]
        if active:
            value = xhat * gain + shift
            gate = logistic(value)
            grad = grad * (gate * (1.0 + value * (1.0 - gate)))
            grad_ref[pl.ds(row, 64), :] = grad
        return grad, grad * xhat

    gain_grad, shift_grad, mean_one, mean_two = norm_back_stats(load, 1, C2, gain, ones)

    def body(phase, image, inside, row):
        store(
            image,
            inside,
            row,
            scale[image : image + 1, :]
            * (
                grad_ref[pl.ds(row, 64), :] * gain
                - mean_one[image : image + 1, :]
                - normal(image, row) * mean_two[image : image + 1, :]
            ),
        )

    each_chunk(body)
    return gain_grad, shift_grad


def res_backward(
    leaving, me, grad_res, down, inner, act_one, act_two, kern_first, kern_second, dense_two, hidden_pre, stats, gains, embed,
    grad_down, sent, out,
    wide, grad_act,
):
    at = RES_AT
    ones = same_group(C2)
    clear_edges(wide)

    def lower(phase, image, inside, row):
        put_shifted(wide, image, inside, grad_res[pl.ds(row, 64), :].astype(bf16).astype(f32))

    each_chunk(lower)
    sums = image_sums(
        lambda phase, image, row: (grad_res[pl.ds(row, 64), :].astype(bf16).astype(f32),), 1, C2
    )[0]
    vector_to(out, at["bias_second"], jnp.sum(sums, axis=0, keepdims=True))
    grad_act[...] = conv_low_back(wide, kern_second)
    conv_low_grad(act_two, wide, out, at["kern_second"])

    def store_inner(image, inside, row, value):
        put_shifted(wide, image, inside, value.astype(bf16).astype(f32))

    gain_grad, shift_grad = norm_back(
        grad_act, inner, stats[8:12, :], stats[12:16, :],
        gains[2:3, :], gains[3:4, :], ones, True, store_inner,
    )
    vector_to(out, at["gain_second"], gain_grad)
    vector_to(out, at["shift_second"], shift_grad)
    inner_sum = jnp.concatenate(
        [
            jnp.sum(fold(wide[image, PAD : PAD + LOW, C2 : 2 * C2].astype(f32)), axis=0, keepdims=True)
            for image in range(IMGS)
        ]
        + [jnp.zeros((4, C2), f32)],
        axis=0,
    )
    time_sum = jnp.sum(inner_sum, axis=0, keepdims=True)
    vector_to(out, at["bias_first"], time_sum)
    vector_to(out, at["bias_two"], time_sum)
    pre = hidden_pre[...]
    gate = logistic(pre)
    contract = (((0,), (0,)), ((), ()))
    matrix_to(
        out, at["dense_two"],
        lax.dot_general(pre * gate, inner_sum, contract, precision=highest, preferred_element_type=f32),
    )
    grad_pre = lax.dot_general(
        inner_sum, dense_two[...].astype(f32), (((1,), (1,)), ((), ())), precision=highest, preferred_element_type=f32
    ) * (gate * (1.0 + pre * (1.0 - gate)))
    vector_to(out, at["bias_one"], jnp.sum(grad_pre, axis=0, keepdims=True))
    matrix_to(
        out, at["dense_one"],
        lax.dot_general(embed[...], grad_pre, contract, precision=highest, preferred_element_type=f32),
    )
    grad_act[...] = conv_low_back(wide, kern_first)
    conv_low_grad(act_one, wide, out, at["kern_first"])

    def store_down(image, inside, row, value):
        grad_down[pl.ds(row, 64), :] = value + grad_res[pl.ds(row, 64), :]

    gain_grad, shift_grad = norm_back(
        grad_act, down, stats[0:4, :], stats[4:8, :],
        gains[0:1, :], gains[1:2, :], ones, True, store_down,
    )
    vector_to(out, at["gain_first"], gain_grad)
    vector_to(out, at["shift_first"], shift_grad)
    out[at["end"] :, :] = jnp.zeros((RES_ROWS - at["end"], LANES), f32)
    narrow_out(out, me[0], sent, leaving)


def attn_forward(
    places, me, gathered, res_out,
    attn_low, normed, qkv, probs, mixed, kern_qkv, kern_proj, stats, gains,
    stage,
):
    at = ATTN_AT
    widen(gathered, places, me[0], stage)
    matrix_from(stage, at["kern_qkv"], kern_qkv, C2, 3 * C2)
    matrix_from(stage, at["kern_proj"], kern_proj, C2, C2)
    ones = same_group(C2)
    gain = vector_at(stage, at["gain_attn"], C2)
    shift = vector_at(stage, at["shift_attn"], C2)
    gains[...] = jnp.concatenate([gain, shift, jnp.zeros((6, C2), f32)], axis=0)
    center, scale = norm_stats(lambda phase, row: res_out[pl.ds(row, 64), :], 1, C2, ones)
    stats[0:IMGS, :] = center
    stats[IMGS : 2 * IMGS, :] = scale

    def body(phase, image, inside, row):
        value = (res_out[pl.ds(row, 64), :] - center[image : image + 1, :]) * scale[image : image + 1, :]
        normed[pl.ds(row, 64), :] = (value * gain + shift).astype(bf16)

    each_chunk(body)
    qkv[...] = mm(normed[...], kern_qkv[...]).astype(bf16)
    for image in range(IMGS):
        rows = slice(image * LOW, (image + 1) * LOW)
        logits = mm_nt(qkv[rows, 0:C2], qkv[rows, C2 : 2 * C2]) * C2 ** (-0.5)
        powers = jnp.exp(logits - jnp.max(logits, axis=1, keepdims=True))
        weights = powers / jnp.sum(powers, axis=1, keepdims=True)
        probs[image] = weights
        mixed[rows, :] = mm(weights.astype(bf16), qkv[rows, 2 * C2 : 3 * C2]).astype(bf16)
    attn_low[...] = (
        res_out[...] + mm(mixed[...], kern_proj[...]) + vector_at(stage, at["bias_proj"], C2)
    ).astype(bf16)


def attn_backward(
    leaving, me, grad_attn, res_out, normed, qkv, probs, mixed, kern_qkv, kern_proj, stats, gains,
    grad_res, sent, out,
    grad_qkv, grad_mixed, grad_normed, low,
):
    at = ATTN_AT
    ones = same_group(C2)
    low[...] = grad_attn[...].astype(bf16)
    sums = image_sums(lambda phase, image, row: (grad_attn[pl.ds(row, 64), :],), 1, C2)[0]
    vector_to(out, at["bias_proj"], jnp.sum(sums, axis=0, keepdims=True))
    matrix_to(out, at["kern_proj"], mm_tn(mixed[...], low[...]))
    grad_mixed[...] = mm_nt(low[...], kern_proj[...]).astype(bf16)
    scale_by = C2 ** (-0.5)
    for image in range(IMGS):
        rows = slice(image * LOW, (image + 1) * LOW)
        query, keys, value = (qkv[rows, part * C2 : (part + 1) * C2] for part in range(3))
        weights = probs[image]
        grad_probs = mm_nt(grad_mixed[rows, :], value)
        grad_qkv[rows, 2 * C2 : 3 * C2] = mm_tn(weights.astype(bf16), grad_mixed[rows, :]).astype(bf16)
        grad_logits = (
            weights * (grad_probs - jnp.sum(weights * grad_probs, axis=1, keepdims=True))
        ).astype(bf16)
        grad_qkv[rows, 0:C2] = (mm(grad_logits, keys) * scale_by).astype(bf16)
        grad_qkv[rows, C2 : 2 * C2] = (mm_tn(grad_logits, query) * scale_by).astype(bf16)
    matrix_to(out, at["kern_qkv"], mm_tn(normed[...], grad_qkv[...]))
    grad_normed[...] = mm_nt(grad_qkv[...], kern_qkv[...])

    def store(image, inside, row, value):
        grad_res[pl.ds(row, 64), :] = value + grad_attn[pl.ds(row, 64), :]

    gain_grad, shift_grad = norm_back(
        grad_normed, res_out, stats[0:4, :], stats[4:8, :],
        gains[0:1, :], gains[1:2, :], ones, False, store,
    )
    vector_to(out, at["gain_attn"], gain_grad)
    vector_to(out, at["shift_attn"], shift_grad)
    out[at["end"] :, :] = jnp.zeros((ATTN_ROWS - at["end"], LANES), f32)
    narrow_out(out, me[0], sent, leaving)


def pick(row, channel):
    lane = lax.broadcasted_iota(jnp.int32, (LANES, LANES), 0)
    ch = lax.broadcasted_iota(jnp.int32, (LANES, LANES), 1)
    return (row * LANES + lane == CIN * ch + channel).astype(f32).astype(bf16)


def head_step(
    places, leaving, me, gathered, attn_low, top, clean, factor,
    grad_attn, skip, loss, sent, out,
    stage, wide, kern_up, merged, act, taps, narrow, grad_wide_zero, grad_wide_one, boxes,
):
    at = HEAD_AT
    widen(gathered, places, me[0], stage)
    ones = same_group(C1)
    kern_up[...] = jnp.zeros(kern_up.shape, bf16)

    def combine(at_row):
        tap = [[stage[pl.ds((3 * a + b) * C2 + at_row, 64), :] for b in range(3)] for a in range(3)]
        by_row = {(0, 0): tap[0], (0, 1): [tap[1][b] + tap[2][b] for b in range(3)],
                  (1, 0): [tap[0][b] + tap[1][b] for b in range(3)], (1, 1): tap[2]}
        for (row_phase, slot), three in by_row.items():
            for col_off in range(3):
                base = (slot * 3 + col_off) * C2
                here = pl.ds(base + at_row, 64)
                if col_off == 0:
                    kern_up[row_phase, here, 0:C1] = three[0].astype(bf16)
                elif col_off == 1:
                    kern_up[row_phase, here, 0:C1] = (three[1] + three[2]).astype(bf16)
                    kern_up[row_phase, here, C1 : 2 * C1] = (three[0] + three[1]).astype(bf16)
                else:
                    kern_up[row_phase, here, C1 : 2 * C1] = three[2].astype(bf16)

    chunks(C2, 64, combine)
    clear_edges(wide)

    def spread_low(phase, image, inside, row):
        put_shifted(wide, image, inside, attn_low[pl.ds(row, 64), :].astype(f32))

    each_chunk(spread_low)
    bias_up = stage[at["bias_up"] : at["bias_up"] + 1, :]
    for row_phase in range(2):
        product = mm(
            jnp.concatenate(
                [wide_rows(wide, row_phase - 1, 0, 3 * C2), wide_rows(wide, row_phase, 0, 3 * C2)], axis=1
            ),
            kern_up[row_phase],
        )
        for col_phase in range(2):
            phase = row_phase * 2 + col_phase
            merged[phase] = product[:, col_phase * C1 : (col_phase + 1) * C1] + bias_up + top[phase]
    gain = stage[at["gain_out"] : at["gain_out"] + 1, :]
    shift = stage[at["shift_out"] : at["shift_out"] + 1, :]
    center, scale = norm_stats(lambda phase, row: merged[phase, pl.ds(row, 64), :], 4, C1, ones)

    def body(phase, image, inside, row):
        value = (merged[phase, pl.ds(row, 64), :] - center[image : image + 1, :]) * scale[image : image + 1, :]
        value = value * gain + shift
        gate = logistic(value)
        act[phase, pl.ds(row, 64), :] = (value * gate).astype(bf16)
        skip[phase, pl.ds(row, 64), :] = gate * (1.0 + value * (1.0 - gate))

    each_chunk(body, 4)
    for channel in range(CIN):
        total = None
        for row in range(3):
            part = mm(stage[pl.ds(at["kern_out"] + row, 9, 3), :].astype(bf16), pick(row, channel))
            total = part if total is None else total + part
        narrow[pl.ds(channel, 9, 8), :] = total
    for channel in range(CIN, 8):
        narrow[pl.ds(channel, 9, 8), :] = jnp.zeros((9, LANES), f32)
    kern_out = narrow[...].astype(bf16)
    masks = lane_masks(ROWS)
    for phase in range(4):
        taps[:, phase * ROWS : (phase + 1) * ROWS] = mm_nt(kern_out, act[phase])
    lane = lax.broadcasted_iota(jnp.int32, (8, LANES), 1)
    channel_at = lax.broadcasted_iota(jnp.int32, (8, LANES), 0)
    bias_out = jnp.sum(
        jnp.where((lane == channel_at) & (channel_at < CIN), stage[at["bias_out"] : at["bias_out"] + 1, :], 0.0),
        axis=1,
        keepdims=True,
    )
    pixel_count = CIN * SIDE * SIDE
    loss_sum = jnp.zeros((8, ROWS), f32)
    bias_grad = jnp.zeros((8, 1), f32)
    grad_lanes = []
    for phase in range(4):
        predict = bias_out
        for tap, off in enumerate(TAPS):
            other, row_off, col_off = tap_source(phase, off)
            predict = predict + lane_shift(
                taps[8 * tap : 8 * tap + 8, other * ROWS : (other + 1) * ROWS], row_off, col_off, masks
            )
        error = predict - clean[:, phase * ROWS : (phase + 1) * ROWS]
        loss_sum = loss_sum + error * error * factor[...]
        grad = ((2.0 / pixel_count) * factor[...] * error).astype(bf16).astype(f32)
        bias_grad = bias_grad + jnp.sum(grad, axis=1, keepdims=True)
        grad_lanes.append(grad)
    loss[...] = jnp.sum(jnp.sum(loss_sum, axis=1, keepdims=True), axis=0, keepdims=True) * (1.0 / pixel_count)
    out[at["bias_out"] : at["bias_out"] + 1, :] = jnp.sum(
        jnp.where((lane == channel_at) & (channel_at < CIN), bias_grad, 0.0), axis=0, keepdims=True
    )
    for phase in range(4):
        for tap, off in enumerate(TAPS):
            other, row_off, col_off = tap_source(phase, (-off[0], -off[1]))
            taps[8 * tap : 8 * tap + 8, phase * ROWS : (phase + 1) * ROWS] = lane_shift(
                grad_lanes[other], row_off, col_off, masks
            )
    kern_grad = None
    for phase in range(4):
        low = taps[:, phase * ROWS : (phase + 1) * ROWS].astype(bf16)
        part = mm(low, act[phase])
        kern_grad = part if kern_grad is None else kern_grad + part
        skip[phase] = mm_tn(low, kern_out) * skip[phase]
    narrow[...] = kern_grad
    for row in range(3):
        total = None
        for channel in range(CIN):
            pieces = parts_of(narrow[pl.ds(channel, 9, 8), :])
            part = sum(mm_nt(piece, pick(row, channel)) for piece in pieces)
            total = part if total is None else total + part
        out[pl.ds(at["kern_out"] + row, 9, 3), :] = total

    def pieces(phase, image, row):
        xhat = (merged[phase, pl.ds(row, 64), :] - center[image : image + 1, :]) * scale[image : image + 1, :]
        return skip[phase, pl.ds(row, 64), :], xhat

    def load(phase, image, row):
        grad, xhat = pieces(phase, image, row)
        return grad, grad * xhat

    gain_grad, shift_grad, mean_one, mean_two = norm_back_stats(load, 4, C1, gain, ones)
    vector_to(out, at["gain_out"], gain_grad)
    vector_to(out, at["shift_out"], shift_grad)
    clear_edges(grad_wide_zero)
    clear_edges(grad_wide_one)
    clear_edges(boxes)
    wides = (grad_wide_zero, grad_wide_one)

    def back(phase, image, inside, row):
        for row_phase in range(2):
            pair = []
            for col_phase in range(2):
                phase = row_phase * 2 + col_phase
                grad, xhat = pieces(phase, image, row)
                value = scale[image : image + 1, :] * (
                    grad * gain - mean_one[image : image + 1, :] - xhat * mean_two[image : image + 1, :]
                )
                skip[phase, pl.ds(row, 64), :] = value
                pair.append(value.astype(bf16).astype(f32))
            here = pl.ds(PAD + inside, 64)
            right, left = row_shift(pair[0], 1), row_shift(pair[1], -1)
            for number, value in enumerate((right, *pair, left)):
                wides[row_phase][image, here, number * C1 : (number + 1) * C1] = value.astype(bf16)
            base = row_phase * 3 * C1
            boxes[image, here, base : base + C1] = pair[1] + right
            boxes[image, here, base + C1 : base + 2 * C1] = pair[0] + pair[1]
            boxes[image, here, base + 2 * C1 : base + 3 * C1] = left + pair[0]

    each_chunk(back)
    bias_sum = jnp.zeros((8, C1), f32)
    for row_phase in range(2):
        for image in range(IMGS):
            both = fold(wides[row_phase][image, PAD : PAD + LOW, C1 : 3 * C1].astype(f32))
            bias_sum = bias_sum + both[:, :C1] + both[:, C1:]
    vector_to(out, at["bias_up"], jnp.sum(bias_sum, axis=0, keepdims=True))
    total = None
    for row_phase in range(2):
        for slot in range(2):
            base = slot * 3 * C2
            taps = [
                kern_up[row_phase, base : base + C2, 0:C1],
                kern_up[row_phase, base + C2 : base + 2 * C2, :],
                kern_up[row_phase, base + 2 * C2 : base + 3 * C2, C1:C2],
            ]
            part = mm_nt(wide_rows(wides[row_phase], 1 - row_phase - slot, 0, 4 * C1), jnp.concatenate(taps, axis=1))
            total = part if total is None else total + part
    grad_attn[...] = total
    width = 3 * C1

    def box_rows(row_off, row_phase):
        return boxes[
            :, PAD + 16 * row_off : PAD + 16 * row_off + LOW, row_phase * width : (row_phase + 1) * width
        ].reshape(ROWS, width)

    summed = (
        box_rows(0, 1) + box_rows(1, 0),
        box_rows(0, 0) + box_rows(0, 1),
        box_rows(-1, 1) + box_rows(0, 0),
    )
    for row_tap in range(3):
        product = mm_tn(attn_low[...], summed[row_tap].astype(bf16))
        for col_tap in range(3):
            tap = row_tap * 3 + col_tap
            out[tap * C2 : (tap + 1) * C2, :] = product[:, col_tap * C1 : (col_tap + 1) * C1]
    out[at["end"] :, :] = jnp.zeros((HEAD_ROWS - at["end"], LANES), f32)
    narrow_out(out, me[0], sent, leaving)


def sds(shape, dtype=f32):
    return jax.ShapeDtypeStruct(shape, dtype)


def run(body, scalars, ins, outs, scratch=(), limit=62):
    in_leaves, in_tree = jax.tree.flatten([*scalars, *ins])
    out_leaves, out_tree = jax.tree.flatten(outs)

    def kernel(*refs):
        split = len(in_leaves), len(in_leaves) + len(out_leaves)
        body(
            *jax.tree.unflatten(in_tree, refs[: split[0]]),
            *jax.tree.unflatten(out_tree, refs[split[0] : split[1]]),
            *refs[split[1] :],
        )

    whole = pl.BlockSpec(memory_space=pltpu.VMEM)
    scalar = pl.BlockSpec(memory_space=pltpu.SMEM)
    results = pl.pallas_call(
        kernel,
        out_shape=out_leaves,
        in_specs=[scalar] * len(scalars) + [whole] * (len(in_leaves) - len(scalars)),
        out_specs=[whole] * len(out_leaves),
        scratch_shapes=scratch,
        compiler_params=pltpu.CompilerParams(vmem_limit_bytes=limit * 2**20),
    )(*in_leaves)
    return jax.tree.unflatten(out_tree, results)


def wide_scratch(width, dtype=bf16):
    return pltpu.VMEM((IMGS, PADDED, width), dtype)


SAVED = dict(
    stage=((RES_ROWS, LANES), f32), block_out=((HEAD_ROWS, LANES), f32),
    taps=((72, 4 * ROWS), f32), low_taps=((72, 4 * ROWS), f32), narrow=((72, LANES), f32),
    top=((4, ROWS, C1), f32), down=((ROWS, C2), f32), inner=((ROWS, C2), f32), res_out=((ROWS, C2), f32),
    act_one=((ROWS, C2), bf16), act_two=((ROWS, C2), bf16), attn_low=((ROWS, C2), bf16), normed=((ROWS, C2), bf16),
    qkv=((ROWS, 3 * C2), bf16), probs=((IMGS, LOW, LOW), f32), mixed=((ROWS, C2), bf16),
    merged=((4, ROWS, C1), f32), act=((4, ROWS, C1), bf16), skip=((4, ROWS, C1), f32),
    grad_attn=((ROWS, C2), f32), grad_res=((ROWS, C2), f32), grad_act=((ROWS, C2), f32),
    grad_low=((ROWS, C2), bf16), grad_mixed=((ROWS, C2), bf16), grad_qkv=((ROWS, 3 * C2), bf16),
    dense_one=((TDIM, TEMB), bf16), dense_two=((TEMB, C2), bf16), kern_down=((9 * C1, C2), bf16),
    kern_first=((9 * C2, C2), bf16), kern_second=((9 * C2, C2), bf16), kern_qkv=((C2, 3 * C2), bf16),
    kern_proj=((C2, C2), bf16), kern_up=((2, 6 * C2, C2), bf16),
    hidden_pre=((8, TEMB), f32), res_stats=((16, C2), f32), res_gains=((8, C2), f32),
    attn_stats=((8, C2), f32), attn_gains=((8, C2), f32),
    wide=((IMGS, PADDED, 3 * C2), bf16), wide_zero=((IMGS, PADDED, 3 * C2), bf16),
    wide_one=((IMGS, PADDED, 3 * C2), bf16), boxes=((IMGS, PADDED, 6 * C1), f32),
)


class Named:
    def __init__(self, names, refs):
        self.__dict__.update(zip(names, refs))


def whole_step(places, leaving, me, gathered, noisy, clean, factor, embed, loss, sent, *refs):
    own = Named(SAVED, refs)
    stem_wide, stem_wide_zero = own.wide.at[:, :, 0 : 3 * C1], own.wide_zero.at[:, :, 0 : 3 * C1]
    stem_forward(
        places[0], me, gathered[0], noisy, own.top, own.down, own.kern_down, own.stage, own.taps, stem_wide, stem_wide_zero
    )
    res_forward(
        places[1], me, gathered[1], own.down, embed,
        own.inner, own.res_out, own.act_one, own.act_two, own.kern_first, own.kern_second, own.dense_two,
        own.hidden_pre, own.res_stats, own.res_gains,
        own.stage, own.dense_one, own.wide,
    )
    attn_forward(
        places[2], me, gathered[2], own.res_out,
        own.attn_low, own.normed, own.qkv, own.probs, own.mixed, own.kern_qkv, own.kern_proj,
        own.attn_stats, own.attn_gains,
        own.stage,
    )
    head_step(
        places[3], leaving[3], me, gathered[3], own.attn_low, own.top, clean, factor,
        own.grad_attn, own.skip, loss, sent[3], own.block_out,
        own.stage, own.wide, own.kern_up, own.merged, own.act, own.low_taps, own.narrow,
        own.wide_zero, own.wide_one, own.boxes,
    )
    attn_backward(
        leaving[2], me, own.grad_attn, own.res_out, own.normed, own.qkv, own.probs, own.mixed,
        own.kern_qkv, own.kern_proj, own.attn_stats, own.attn_gains,
        own.grad_res, sent[2], own.block_out.at[0:ATTN_ROWS],
        own.grad_qkv, own.grad_mixed, own.grad_act, own.grad_low,
    )
    res_backward(
        leaving[1], me, own.grad_res, own.down, own.inner, own.act_one, own.act_two, own.kern_first, own.kern_second,
        own.dense_two, own.hidden_pre, own.res_stats, own.res_gains, embed,
        own.grad_attn, sent[1], own.stage,
        own.wide, own.grad_act,
    )
    stem_backward(
        leaving[0], me, noisy, own.top, own.skip, own.grad_attn, own.kern_down, sent[0], own.block_out,
        own.taps, stem_wide, stem_wide_zero, own.wide_one.at[:, :, 0 : 2 * C2], own.act,
    )


def local_step(me, arrays, places, shapes, out_places, noisy, clean, factor, embed):
    def body(me, arrays, noisy, clean, factor, embed, loss, sent, *refs):
        gathered = [[arrays[place[0]] for place in block] for block in places]
        leaving = [[sent[place[0]] for place in block] for block in out_places]
        rest = [[place[1:] for place in block] for block in places]
        out_rest = [[place[1:] for place in block] for block in out_places]
        whole_step(rest, out_rest, me, gathered, noisy, clean, factor, embed, loss, leaving, *refs)

    return run(
        body,
        [me],
        [arrays, noisy, clean, factor, embed],
        [sds((1, 1)), shapes],
        [pltpu.VMEM(shape, dtype) for shape, dtype in SAVED.values()],
        limit=50,
    )


def plan(step_counts, time_index, teacher_size):
    position = time_index % step_counts
    time_values = (2 * position + teacher_size).astype(f32) / (2 * step_counts).astype(f32)
    alpha_t = jnp.cos(0.5 * math.pi * time_values)
    sigma_t = jnp.sin(0.5 * math.pi * time_values)
    weight = jnp.maximum(alpha_t * alpha_t / (sigma_t * sigma_t), 1.0)
    return (time_values, alpha_t, sigma_t, weight)


def sinusoid(time_values):
    half_dim = TDIM // 2
    frequency = jnp.exp(-math.log(10000.0) * jnp.arange(half_dim, dtype=f32) / half_dim)
    angles = 1000.0 * time_values[:, None] * frequency[None, :]
    return jnp.concatenate([jnp.sin(angles), jnp.cos(angles)], axis=1)


def arrange(clean_images, noise_field, levels):
    def body(levels, clean, noise, noisy_out, clean_out, factor_out):
        image = lax.broadcasted_iota(jnp.int32, (IMGS, 1), 0)

        def column(kind):
            value = jnp.zeros((IMGS, 1), f32)
            for number in range(IMGS):
                value = jnp.where(image == number, levels[kind, number], value)
            return value

        alpha, sigma = column(1), column(2)
        mixed = [(alpha * clean[c] + sigma * noise[c]).astype(bf16).astype(f32) for c in range(CIN)]
        pieces = [piece.astype(f32) for piece in parts_of(jnp.concatenate([clean[c] for c in range(CIN)], axis=0))]
        rows = jnp.concatenate(mixed + pieces, axis=0).astype(bf16)
        held = CIN * IMGS
        noisy_out[...] = jnp.zeros(noisy_out.shape, f32)
        clean_out[...] = jnp.zeros(clean_out.shape, f32)
        for phase in range(4):
            place = lax.broadcasted_iota(jnp.int32, (SIDE * SIDE, LOW), 1)
            source = ((place >> 4) * 2 + phase // 2) * SIDE + (place & 15) * 2 + phase % 2
            chosen = lax.broadcasted_iota(jnp.int32, (SIDE * SIDE, LOW), 0) == source
            moved = mm(rows, chosen.astype(f32).astype(bf16))
            exact = moved[held : 2 * held] + moved[2 * held : 3 * held] + moved[3 * held : 4 * held]
            for number in range(IMGS):
                lanes = slice(phase * ROWS + number * LOW, phase * ROWS + (number + 1) * LOW)
                for c in range(CIN):
                    at = c * IMGS + number
                    noisy_out[c : c + 1, lanes] = moved[at : at + 1]
                    clean_out[c : c + 1, lanes] = exact[at : at + 1]
        for number in range(IMGS):
            factor_out[:, number * LOW : (number + 1) * LOW] = jnp.full((1, LOW), levels[0, number], f32)

    return run(
        body,
        [levels],
        [clean_images.transpose(1, 0, 2), noise_field.transpose(1, 0, 2)],
        [sds((8, 4 * ROWS)), sds((8, 4 * ROWS)), sds((1, ROWS))],
        limit=12,
    )


def prepare(clean_images, noise_field, step_counts, time_index, teacher_size, image_count):
    time_values, alpha_t, sigma_t, weight = plan(step_counts, time_index, teacher_size)
    live_mask = (jnp.arange(clean_images.shape[0], dtype=jnp.int32) < image_count).astype(f32)
    levels = jnp.stack([live_mask * weight, alpha_t, sigma_t], axis=0)
    embed = jnp.pad(sinusoid(time_values), ((0, 8 - IMGS), (0, 0)))
    return [*arrange(clean_images, noise_field, levels), embed]


AXES = ("dp", "fsdp")
BLOCK_ROWS = (STEM_ROWS, RES_ROWS, ATTN_ROWS, HEAD_ROWS)
SHARD_ROWS = (80, 344, 72, 80)
SPAN = 32
PARTS = (
    ((0, 0, 80), (1, 32, 184)),
    ((1, 184, 344), (2, 0, 72)),
    ((3, 0, 80), (1, 0, 32)),
)
PART_ROWS = tuple(sum(hi - lo for _, lo, hi in members) for members in PARTS)
TURNS = ((2, 4), (4, 2))
PLANE = (0, 2, 4, 6)
LINE = (0, 8, 16, 24)


def swap(values, mask):
    return lax.ppermute(values, AXES, [(here, here ^ mask) for here in range(SPAN)])


def pack_rows(masters):
    def body(refs, outs):
        for out, parts in zip(outs, (PARTS[:2], PARTS[2:])):
            at = 0
            for members in parts:
                for block, lo, hi in members:
                    out[at : at + hi - lo, :] = refs[block][lo:hi, :].astype(bf16)
                    at += hi - lo

    shapes = [sds((sum(PART_ROWS[:2]), LANES), bf16), sds((PART_ROWS[2], LANES), bf16)]
    return run(body, [], [masters], [shapes], limit=62)[0]


def part_places(number, array, masks):
    at, found = 0, []
    for block, lo, hi in PARTS[number]:
        found.append((block, (array, masks, at, at + hi - lo, SHARD_ROWS[block], lo)))
        at += hi - lo
    return found


def gather_parts(own, prepared):
    early, late = own
    *images, embed = prepared
    line = [early] + [swap(early, mask) for mask in LINE[1:]]
    near = jnp.stack([late, swap(late, PLANE[1])], axis=0)
    near = jnp.concatenate([near, swap(near, PLANE[2])], axis=0)
    arrays, places = [], [[] for _ in SHARD_ROWS]

    def add(number, array, masks):
        for block, place in part_places(number, len(arrays), masks):
            places[block].append(place)
        arrays.append(array)

    held = []
    for number, (last, first) in enumerate(TURNS):
        begin = number * PART_ROWS[0]
        piece = jnp.stack([rows[begin : begin + PART_ROWS[number]] for rows in line], axis=0)
        held.append(jnp.concatenate([piece, swap(piece, first)], axis=0))
    held, near, images = lax.optimization_barrier((held, near, images))
    far = [swap(held[number], last) for number, (last, first) in enumerate(TURNS)]
    third = jnp.concatenate([near] + [swap(near, mask) for mask in LINE[1:]], axis=0)
    far, third, embed = lax.optimization_barrier((far, third, embed))
    for number, (last, first) in enumerate(TURNS):
        masks = [a ^ b for a in (0, first) for b in LINE]
        add(number, held[number], masks)
        add(number, far[number], [mask ^ last for mask in masks])
        add(number, swap(held[number], 1), [mask ^ 1 for mask in masks])
        add(number, swap(far[number], 1), [mask ^ last ^ 1 for mask in masks])
    masks = [a ^ b for b in LINE for a in PLANE]
    add(2, third, masks)
    add(2, swap(third, 1), [mask ^ 1 for mask in masks])
    return arrays, places, (*images, embed)


def leaving_parts():
    shapes, places = [], [[] for _ in SHARD_ROWS]

    def add(number, masks):
        for block, place in part_places(number, len(shapes), masks):
            places[block].append(place)
        shapes.append(sds((len(masks), PART_ROWS[number], LANES), bf16))

    for number, (first, last) in enumerate(TURNS):
        for core in (0, 1):
            for side in (0, first):
                add(number, [core ^ side ^ a ^ b for a in (0, last) for b in LINE])
    for core in (0, 1):
        add(2, [core ^ a ^ b for b in LINE for a in PLANE])
    return shapes, places


def reduce_parts(leaving):
    totals = []
    crossed = [[swap(leaving[4 * number + 2 + side], 1) for side in (0, 1)] for number in (0, 1)]
    third = leaving[8].astype(f32) + swap(leaving[9], 1).astype(f32)
    far = [leaving[4 * number + 1].astype(f32) + crossed[number][1].astype(f32) for number in (0, 1)]
    near, far, third = lax.optimization_barrier(([crossed[0][0], crossed[1][0]], far, third))
    near = [leaving[4 * number].astype(f32) + near[number].astype(f32) for number in (0, 1)]
    arrived = [swap(third[4 * at : 4 * at + 4].astype(bf16), mask) for at, mask in enumerate(LINE) if mask]
    third = third[:4] + sum(piece.astype(f32) for piece in arrived)
    for number, (first, last) in enumerate(TURNS):
        totals.append(near[number] + swap(far[number].astype(bf16), first).astype(f32))
    totals, third = lax.optimization_barrier((totals, third))
    for number, (first, last) in enumerate(TURNS):
        total = totals[number]
        totals[number] = total[:4] + swap(total[4:].astype(bf16), last).astype(f32)
    whole = jnp.concatenate(totals, axis=1)
    return [
        [array[0]] + [swap(array[at].astype(bf16), mask) for at, mask in enumerate(masks) if mask]
        for array, masks in ((whole, LINE), (third, PLANE))
    ]


def last_sum(image_counts, count, loss, groups):
    def body(live, loss, groups, total, row):
        square, at = jnp.zeros((8, LANES), f32), 0
        for pieces in groups:
            value = pieces[0][...].astype(f32)
            for piece in pieces[1:]:
                value = value + piece[...].astype(f32)
            total[at : at + value.shape[0], :] = value
            at += value.shape[0]
            square = square + fold(value * value)
        square = jnp.sum(jnp.sum(square, axis=0, keepdims=True), axis=1, keepdims=True)
        lane = lax.broadcasted_iota(jnp.int32, (1, LANES), 1)
        scalars = jnp.where(lane == 0, loss[...], jnp.where(lane == 1, square, live[0].astype(f32)))
        row[...] = jnp.broadcast_to(scalars[None], row.shape)

    rows = sum(pieces[0].shape[0] for pieces in groups)
    return run(body, [image_counts], [loss, groups], [sds((rows, LANES)), sds((count, 1, LANES))], limit=16)


def update(adam_step, arrived, gradient, masters, firsts, seconds, places):
    def body(step, arrived, gradient, masters, firsts, seconds, loss, norm, outs):
        sums = jnp.sum(arrived[...], axis=0)
        live = 1.0 / sums[:, 2:3]
        loss[...] = sums[:, 0:1] * live
        size = jnp.sqrt(sums[:, 1:2]) * live
        norm[...] = size
        scale = clip_limit / jnp.maximum(size, clip_limit) * live
        powers = lax.fori_loop(
            0, step[0], lambda _, held: (held[0] * beta_one, held[1] * beta_two), (jnp.float32(1.0), jnp.float32(1.0))
        )
        fix_one, fix_two = 1.0 - powers[0], 1.0 - powers[1]
        at = 0
        for block, lo, hi in places:
            grad = gradient[at : at + hi - lo, :] * scale
            at += hi - lo
            master, first, second = (refs[block][lo:hi, :] for refs in (masters, firsts, seconds))
            first_new = beta_one * first + (1.0 - beta_one) * grad
            second_new = beta_two * second + (1.0 - beta_two) * grad * grad
            master_new = master - learn_rate * (
                first_new / fix_one / (jnp.sqrt(second_new / fix_two) + adam_eps) + decay_rate * master
            )
            for ref, value in zip(outs[block], (master_new, first_new, second_new, master_new.astype(bf16))):
                ref[lo:hi, :] = value

    shapes = [[sds(m.shape), sds(m.shape), sds(m.shape), sds(m.shape, bf16)] for m in masters]
    return run(
        body, [adam_step], [arrived, gradient, masters, firsts, seconds], [sds((1, 1)), sds((1, 1)), shapes], limit=24
    )


def gather_whole(shards):
    arrays = [
        lax.all_gather(shard.reshape(-1), AXES, axis=0, tiled=True).reshape(1, rows, LANES)
        for shard, rows in zip(shards, BLOCK_ROWS)
    ]
    return arrays, [[(block, (0,), 0, rows, 0, 0)] for block, rows in enumerate(BLOCK_ROWS)]


def leaving_whole():
    shapes = [sds((1, rows, LANES), bf16) for rows in BLOCK_ROWS]
    return shapes, [[(block, (0,), 0, rows, 0, 0)] for block, rows in enumerate(BLOCK_ROWS)]


def reduce_whole(leaving):
    sums = [
        lax.psum_scatter(array.astype(f32).reshape(-1), AXES, scatter_dimension=0, tiled=True) for array in leaving
    ]
    return [[jnp.concatenate([one.reshape(-1, LANES) for one in sums], axis=0)]]


def per_device(
    clean_images, noise_field, step_counts, time_index, teacher_size, image_counts, adam_step,
    stem_master, stem_first, stem_second, res_master, res_first, res_second,
    attn_master, attn_first, attn_second, head_master, head_first, head_second,
):
    blocks = [
        [block.reshape(-1, LANES) for block in state]
        for state in (
            (stem_master, res_master, attn_master, head_master),
            (stem_first, res_first, attn_first, head_first),
            (stem_second, res_second, attn_second, head_second),
        )
    ]
    masters = blocks[0]
    count = lax.axis_size(AXES)
    me = lax.axis_index(AXES).astype(jnp.int32).reshape(1)
    laid_out = count == SPAN and tuple(master.shape[0] for master in masters) == SHARD_ROWS
    prepared = prepare(clean_images, noise_field, step_counts, time_index, teacher_size, image_counts[0])
    if laid_out:
        arrays, places, prepared = gather_parts(pack_rows(masters), prepared)
        shapes, out_places = leaving_parts()
        order = [member for members in PARTS for member in members]
    else:
        arrays, places = gather_whole([master.astype(bf16) for master in masters])
        shapes, out_places = leaving_whole()
        order = [(block, 0, master.shape[0]) for block, master in enumerate(masters)]
    loss, leaving = local_step(me, arrays, places, shapes, out_places, *prepared)
    pieces = reduce_parts(leaving) if laid_out else reduce_whole(leaving)
    gradient, row = last_sum(image_counts, count, loss, pieces)
    arrived = lax.all_to_all(row, AXES, 0, 0, tiled=True)
    loss, norm, outs = update(adam_step, arrived, gradient, *blocks, order)
    return (loss[0, 0], norm[0, 0]) + tuple(value.reshape(-1) for block in outs for value in block)


def solution(mesh):
    split = P(("dp", "fsdp"))
    images = P(("dp", "fsdp"), None, None)
    return jax.shard_map(
        per_device,
        mesh=mesh,
        in_specs=(images, images, split, split, split, split, P()) + (split,) * 12,
        out_specs=(P(), P()) + (split,) * 16,
        check_vma=False,
    )
```
